32 devices in a mesh: fsdp: 32 (over z, y, x, core).
Axes of the slice: x: 2, y: 2, z: 4, core: 2. Of those that a mesh axis runs over, the one named last changes fastest.
Arguments:
- tokens: bfloat16 [12544, 768], P('fsdp'), may hold values from -6 to 6
- window_pos: int32 [64], P('fsdp'), may hold values from 0 to 24
- norm1_gain: float32 [768], P('fsdp'), may hold values from 0.5 to 1.5
- norm1_bias: float32 [768], P('fsdp'), may hold values from -4 to 4
- qkv_weight: float32 [768, 2304], P('fsdp'), may hold values from -0.21875 to 0.21875
- qkv_bias: float32 [2304], P('fsdp'), may hold values from -4 to 4
- rel_pos_h: float32 [27, 64], replicated, may hold values from -2 to 2
- rel_pos_w: float32 [27, 64], replicated, may hold values from -2 to 2
- proj_weight: float32 [768, 768], P('fsdp'), may hold values from -0.875 to 0.875
- proj_bias: float32 [768], P('fsdp'), may hold values from -4 to 4
- norm2_gain: float32 [768], P('fsdp'), may hold values from 0.5 to 1.5
- norm2_bias: float32 [768], P('fsdp'), may hold values from -4 to 4
- lin1_weight: float32 [768, 3072], P('fsdp'), may hold values from -0.21875 to 0.21875
- lin1_bias: float32 [3072], P('fsdp'), may hold values from -4 to 4
- lin2_weight: float32 [3072, 768], P('fsdp'), may hold values from -0.15625 to 0.15625
- lin2_bias: float32 [768], P('fsdp'), may hold values from -4 to 4
- out_grad: bfloat16 [12544, 768], P('fsdp'), may hold values from -6 to 6
Outputs:
- output: bfloat16 [12544, 768], P('fsdp')
- tokens_grad: bfloat16 [12544, 768], P('fsdp')
- norm1_gain_grad: float32 [768], P('fsdp')
- norm1_bias_grad: float32 [768], P('fsdp')
- qkv_weight_grad: float32 [768, 2304], P('fsdp')
- qkv_bias_grad: float32 [2304], P('fsdp')
- rel_pos_h_grad: float32 [27, 64], replicated
- rel_pos_w_grad: float32 [27, 64], replicated
- proj_weight_grad: float32 [768, 768], P('fsdp')
- proj_bias_grad: float32 [768], P('fsdp')
- norm2_gain_grad: float32 [768], P('fsdp')
- norm2_bias_grad: float32 [768], P('fsdp')
- lin1_weight_grad: float32 [768, 3072], P('fsdp')
- lin1_bias_grad: float32 [3072], P('fsdp')
- lin2_weight_grad: float32 [3072, 768], P('fsdp')
- lin2_bias_grad: float32 [768], P('fsdp')
The draws below stay inside these ranges and needn't reach their ends.
Inputs may be any that keep to these rules, and one draw needn't show every extreme that they name: `window_pos`: the place of each window in its image's 5 x 5 grid of windows, row-major.
All inputs are finite; a program needn't handle non-finite values.
Results may differ from the reference program's by a relative error of at most 0.014.
The reference program's roundings to bfloat16 on the way count: a program that leaves them out, or rounds other values in their place, can miss the bound.
Values may be sent and summed in bfloat16 or wider, within the bound.
No kernel may reach another device: no remote copies, remote signals or barrier semaphores. Data moves between devices by JAX's collectives and lax.ppermute only.
A program may use at most 192 MiB of HBM per device.

```python
import jax
import jax.numpy as jnp
from jax import lax

D = 768
HEADS = 12
HEAD_DIM = 64
FF = 3072
WIN = 14
NWS = 5
EDGE = 8
WINDOWS = 64
TOKENS = 12544


def plant(entries, key, low, top_value):
    index_at = [jax.random.randint(jax.random.fold_in(key, axis), (), 0, length) for axis, length in enumerate(entries.shape)]
    main_axis = entries.shape.index(max(entries.shape))
    beside = index_at[:main_axis] + [(index_at[main_axis] + 1) % entries.shape[main_axis]] + index_at[main_axis + 1:]
    return entries.at[tuple(index_at)].set(low).at[tuple(beside)].set(top_value)


def with_spikes(entries, rng, source, target, shards_of, factor):
    def block_of(position):
        return (jnp.arange(entries.shape[position]) // (entries.shape[position] // shards_of)).reshape((-1,) + (1,) * (entries.ndim - 1 - position))

    first = jax.random.permutation(rng, shards_of)[block_of(target)]
    other_side = (block_of(target) + shards_of // 2) % shards_of
    return jnp.where((block_of(source) == first) | (block_of(source) == other_side), factor * entries, entries)


def steps_of(own_key, extent, shards, least, top_value):
    def one(position, parts):
        heights = jax.random.uniform(jax.random.fold_in(jax.random.fold_in(own_key, 6), position), (parts,), jnp.float32, least / len(shards), top_value / len(shards))
        return jnp.repeat(jnp.exp(heights), extent[position] // parts).reshape((-1,) + (1,) * (len(extent) - position - 1))

    loudness = one(*shards[0])
    for cut in shards[1:]:
        loudness = loudness * one(*cut)
    return loudness


def normal_values(rng, extent, spread, limit, cuts=(), kind=jnp.bfloat16):
    factor_of = steps_of(rng, extent, cuts, -0.22, 0.18) if cuts else 1.0
    drawn = jax.random.normal(rng, extent, jnp.float32) * spread * factor_of
    return jnp.minimum(jnp.maximum(drawn, -limit), limit).astype(kind)


def bell_draw_with(rng, shape, spread, most, split, heavy, kind=jnp.bfloat16):
    drawn = spread * jax.random.normal(rng, shape, jnp.float32)
    if split:
        drawn = drawn * steps_of(rng, shape, split, -0.22, 0.18)
    return jnp.clip(with_spikes(drawn, jax.random.fold_in(rng, 3), *heavy), -most, most).astype(kind)


def setup_inputs(seed: int = 0) -> dict:
    key_list = jax.random.split(jax.random.key(seed), 18)
    tokens = normal_values(key_list[0], (TOKENS, D), 1.0, 6.0, ((0, 32),))
    window_pos = plant(jax.random.randint(key_list[1], (WINDOWS,), 0, NWS * NWS), jax.random.fold_in(key_list[1], 1), 0, (NWS * NWS) - 1).astype(jnp.int32)
    norm1_gain = jnp.clip(1.0 + 0.1 * jax.random.normal(key_list[2], (D,), jnp.float32), 0.5, 1.5)
    norm1_bias = normal_values(key_list[3], (D,), 0.3, 4.0, ((0, 32),), jnp.float32)
    qkv_weight = normal_values(key_list[4], (D, 3 * D), D ** -0.5, 0.21875, ((0, 32),), jnp.float32)
    qkv_bias = normal_values(key_list[5], (3 * D,), 0.3, 4.0, ((0, 32),), jnp.float32)
    rel_pos_h = normal_values(key_list[6], (2 * WIN - 1, HEAD_DIM), 0.15, 2.0, (), jnp.float32)
    rel_pos_w = normal_values(key_list[7], (2 * WIN - 1, HEAD_DIM), 0.15, 2.0, (), jnp.float32)
    proj_weight = normal_values(key_list[8], (D, D), (D // 16) ** -0.5, 0.875, ((0, 32),), jnp.float32)
    proj_bias = normal_values(key_list[9], (D,), 0.3, 4.0, ((0, 32),), jnp.float32)
    norm2_gain = jnp.clip(1.0 + 0.1 * jax.random.normal(key_list[10], (D,), jnp.float32), 0.5, 1.5)
    norm2_bias = normal_values(key_list[11], (D,), 0.3, 4.0, ((0, 32),), jnp.float32)
    lin1_weight = normal_values(key_list[12], (D, FF), D ** -0.5, 0.21875, ((0, 32),), jnp.float32)
    lin1_bias = normal_values(key_list[13], (FF,), 0.3, 4.0, ((0, 32),), jnp.float32)
    lin2_weight = normal_values(key_list[14], (FF, D), (FF // 2) ** -0.5, 0.15625, ((0, 32),), jnp.float32)
    lin2_bias = normal_values(key_list[15], (D,), 0.3, 4.0, ((0, 32),), jnp.float32)
    out_grad = bell_draw_with(key_list[16], (TOKENS, D), 1.0, 6.0, ((0, 32),), (0, 1, 32, 2.75))
    return dict(tokens=tokens, window_pos=window_pos, norm1_gain=norm1_gain, norm1_bias=norm1_bias, qkv_weight=qkv_weight, qkv_bias=qkv_bias, rel_pos_h=rel_pos_h, rel_pos_w=rel_pos_w, proj_weight=proj_weight, proj_bias=proj_bias, norm2_gain=norm2_gain, norm2_bias=norm2_bias, lin1_weight=lin1_weight, lin1_bias=lin1_bias, lin2_weight=lin2_weight, lin2_bias=lin2_bias, out_grad=out_grad)


@jax.custom_vjp
def low(v):
    return lax.optimization_barrier(v.astype(jnp.bfloat16)).astype(jnp.float32)

@jax.custom_vjp
def low_back(v):
    return v

def low_keep(v):
    return (low(v), None)

def low_pass(kept, grad):
    return (grad,)

def back_keep(v):
    return (v, None)

def back_low(kept, grad):
    return (low(grad),)
low.defvjp(low_keep, low_pass)
low_back.defvjp(back_keep, back_low)
highest = lax.Precision.HIGHEST
eps_norm = 1e-06

def layer_norm(values, gain_vec, shift_vec):
    row_mean = lax.optimization_barrier(jnp.mean(values, axis=-1, keepdims=True))
    centred = values - row_mean
    row_var = lax.optimization_barrier(jnp.mean(centred * centred, axis=-1, keepdims=True))
    return centred * lax.rsqrt(row_var + eps_norm) * gain_vec + shift_vec

def slot_mask(window_pos):
    row_win = window_pos // NWS
    col_win = window_pos % NWS
    rows_ok = jnp.where(row_win == NWS - 1, EDGE, WIN)
    cols_ok = jnp.where(col_win == NWS - 1, EDGE, WIN)
    positions = jnp.arange(WIN, dtype=jnp.int32)
    inside = (positions[None, :, None] < rows_ok[:, None, None]) & (positions[None, None, :] < cols_ok[:, None, None])
    return inside.reshape(-1, WIN * WIN).astype(jnp.float32)

def spread_table(table):
    positions = jnp.arange(WIN, dtype=jnp.int32)
    offsets = positions[:, None] - positions[None, :] + WIN - 1
    return table[offsets]

def window_block(token_rows, live, params):
    gain_one, bias_one, w_qkv, b_qkv, table_rows, table_cols, w_proj, b_proj, gain_two, bias_two, w_up, b_up, w_down, b_down = params
    windows = token_rows.shape[0]
    length = WIN * WIN
    score_scale = HEAD_DIM ** (-0.5)
    live_col = live[..., None]
    normed_one = low(layer_norm(token_rows, gain_one, bias_one) * live_col)
    qkv = jnp.einsum('wld,de->wle', normed_one, w_qkv, precision=highest) + b_qkv
    qkv = low(low_back(qkv))
    head_split = qkv.reshape(windows, length, 3, HEADS, HEAD_DIM)
    queries = head_split[:, :, 0]
    keys_all = head_split[:, :, 1]
    values_all = head_split[:, :, 2]
    direct = jnp.einsum('wqhc,wkhc->whqk', queries, keys_all, precision=highest) * score_scale
    grid_q = queries.reshape(windows, WIN, WIN, HEADS, HEAD_DIM)
    rel_rows = jnp.einsum('wyxhc,ykc->whyxk', grid_q, spread_table(table_rows), precision=highest)
    rel_cols = jnp.einsum('wyxhc,xkc->whyxk', grid_q, spread_table(table_cols), precision=highest)
    combined = direct.reshape(windows, HEADS, WIN, WIN, WIN, WIN) + rel_rows[..., :, None] + rel_cols[..., None, :]
    scores = low_back(combined.reshape(windows, HEADS, length, length))
    attn_probs = low(jax.nn.softmax(scores, axis=-1))
    mixed_rows = jnp.einsum('whqk,wkhc->wqhc', attn_probs, values_all, precision=highest)
    mixed_rows = low(low_back(mixed_rows.reshape(windows, length, D)))
    attn_out = low_back(jnp.einsum('wld,de->wle', mixed_rows, w_proj, precision=highest) + b_proj)
    residual = token_rows + attn_out
    normed_two = low(layer_norm(residual, gain_two, bias_two))
    hidden = low_back(jnp.einsum('wld,df->wlf', normed_two, w_up, precision=highest) + b_up)
    active = low(jax.nn.gelu(hidden, approximate=False))
    branch = low_back(jnp.einsum('wlf,fd->wld', active, w_down, precision=highest) + b_down)
    return (residual + branch) * live_col

def forward(token_rows, window_pos, params):
    group_size = 8
    rounded = tuple((low(piece) for piece in params))
    live = slot_mask(window_pos).reshape(-1, group_size, WIN * WIN)
    grouped = token_rows.reshape(-1, group_size, WIN * WIN, D)
    block_fn = jax.checkpoint(lambda pair: window_block(pair[0], pair[1], rounded))
    results = lax.map(block_fn, (grouped, live))
    return results.reshape(-1, D)

def reference(tokens, window_pos, norm1_gain, norm1_bias, qkv_weight, qkv_bias, rel_pos_h, rel_pos_w, proj_weight, proj_bias, norm2_gain, norm2_bias, lin1_weight, lin1_bias, lin2_weight, lin2_bias, out_grad):
    params = (norm1_gain, norm1_bias, qkv_weight, qkv_bias, rel_pos_h, rel_pos_w, proj_weight, proj_bias, norm2_gain, norm2_bias, lin1_weight, lin1_bias, lin2_weight, lin2_bias)
    params = tuple((piece.astype(jnp.float32) for piece in params))

    def whole(token_rows, *pieces):
        return forward(token_rows, window_pos, pieces)
    result, pullback = jax.vjp(whole, tokens.astype(jnp.float32), *params)
    grads = pullback(out_grad.astype(jnp.float32))
    return (result.astype(jnp.bfloat16), grads[0].astype(jnp.bfloat16), grads[1], grads[2], grads[3], grads[4], grads[5], grads[6], grads[7], grads[8], grads[9], grads[10], grads[11], grads[12], grads[13], grads[14])
```

```python
import jax
import jax.numpy as jnp
import numpy as np
from jax import lax
from jax.experimental import pallas as pl
from jax.experimental.pallas import tpu as pltpu
from jax.sharding import PartitionSpec as P

D = 768
HEADS = 12
HEAD_DIM = 64
FF = 3072
WIN = 14
NWS = 5
EDGE = 8
LENGTH = WIN * WIN
PAIRS = HEADS // 2
BLOCK = 200
SCALE = HEAD_DIM ** (-0.5)
EPS = 1e-06
ONE_LANE = 60
BF = jnp.bfloat16
F32 = jnp.float32


def window_constants():
    onehot = np.zeros((2, BLOCK, 128), np.float32)
    shift = np.zeros((2, BLOCK, 128), np.int32)
    for win in range(2):
        for row in range(BLOCK):
            slot = row - 4 * win
            if not 0 <= slot < LENGTH:
                onehot[win, row, ONE_LANE] = onehot[win, row, 64 + ONE_LANE] = -1e30
                continue
            y, x = divmod(slot, WIN)
            for base in (0, 64):
                for lane in (y, WIN + y, 32 + x, 32 + WIN + x):
                    onehot[win, row, base + lane] = 1.0
                shift[win, row, base : base + 32] = WIN - 1 - y
                shift[win, row, base + 32 : base + 64] = WIN - 1 - x
    return onehot, shift


def table_lanes(rel_pos_h, rel_pos_w):
    flip = jnp.concatenate(
        (
            jnp.pad(rel_pos_h[::-1].T, ((0, 0), (0, 5))),
            jnp.pad(rel_pos_w[::-1].T, ((0, 0), (0, 5))),
        ),
        axis=1,
    ).astype(BF)
    nothing = jnp.zeros_like(flip)
    return jnp.concatenate(
        (jnp.concatenate((nothing, flip), axis=1), jnp.concatenate((flip, nothing), axis=1)), axis=0
    )


def table_grads(lanes_grad):
    folded = lanes_grad[64:, :64] + lanes_grad[:64, 64:]
    count = 2 * WIN - 1
    return folded[:count][::-1], folded[32 : 32 + count][::-1]


def dot_nn(a, b):
    return jnp.dot(a, b, preferred_element_type=F32)


def dot_nt(a, b):
    return lax.dot_general(a, b, (((1,), (1,)), ((), ())), preferred_element_type=F32)


def dot_tn(a, b):
    return lax.dot_general(a, b, (((0,), (0,)), ((), ())), preferred_element_type=F32)


def lane_facts():
    lane = lax.broadcasted_iota(jnp.int32, (BLOCK, 128), 1)
    row = lax.broadcasted_iota(jnp.int32, (BLOCK, 128), 0)
    return lane, row, lane < 64, (lane & 31) < WIN


def row_valid(row, win):
    return row < LENGTH if win == 0 else row >= BLOCK - LENGTH


def merge_windows(first, second):
    return jnp.concatenate((first[:192], first[192:] + second[:8], second[8:]), axis=0)


def attn_fwd_kernel(q_ref, k_ref, v_ref, table_ref, onehot_ref, shift_ref, mixed_ref, probs_ref):
    lane, row, low_half, rel_lanes = lane_facts()
    one_lane = (lane & 63) == ONE_LANE
    mixed = []
    for win in range(2):
        rows = pl.ds(192 * win, BLOCK)
        q = q_ref[rows, :]
        k = k_ref[rows, :].astype(F32)
        v = v_ref[rows, :]
        rel = dot_nn(q, table_ref[...])
        shift = shift_ref[win]
        for bit in range(4):
            rel = jnp.where((shift & (1 << bit)) != 0, pltpu.roll(rel, 128 - (1 << bit), 1), rel)
        rel = jnp.where(rel_lanes, rel, 0.0)
        rel_top = rel.astype(BF).astype(F32)
        extra = rel_top + pltpu.roll(rel - rel_top, WIN, 1)
        extra = jnp.where(one_lane, 1.0, extra)
        scaled = q.astype(F32) * SCALE
        onehot = onehot_ref[win].astype(F32)
        halves = []
        for head in range(2):
            own = low_half if head == 0 else jnp.logical_not(low_half)
            left = jnp.where(own, scaled, extra).astype(BF)
            right = jnp.where(own, k, onehot).astype(BF)
            scores = dot_nt(left, right)
            expon = jnp.exp(scores - jnp.max(scores, axis=-1, keepdims=True))
            probs = expon * (1.0 / jnp.sum(expon, axis=-1, keepdims=True))
            probs_ref[0, 2 * win + head] = probs
            halves.append(dot_nn(probs.astype(BF), v))
        both = jnp.where(low_half, halves[0], halves[1])
        mixed.append(jnp.where(row_valid(row, win), both, 0.0))
    mixed_ref[...] = merge_windows(*mixed).astype(BF)


def attn_bwd_kernel(
    q_ref,
    k_ref,
    v_ref,
    grad_ref,
    probs_ref,
    table_ref,
    onehot_ref,
    shift_ref,
    grad_qkv_ref,
    table_grad_ref,
):
    pair = pl.program_id(0)
    lane, row, low_half, rel_lanes = lane_facts()

    @pl.when(pair == 0)
    def _():
        table_grad_ref[...] = jnp.zeros_like(table_grad_ref)

    parts = ([], [], [])
    table_total = jnp.zeros((128, 128), F32)
    for win in range(2):
        rows = pl.ds(192 * win, BLOCK)
        q = q_ref[rows, :]
        k = k_ref[rows, :].astype(F32)
        v = v_ref[rows, :]
        grad = jnp.where(row_valid(row, win), grad_ref[rows, :].astype(F32), 0.0)
        grad_low = grad.astype(BF)
        onehot = onehot_ref[win].astype(F32)
        by_query, by_key, by_value = [], [], []
        for head in range(2):
            own = low_half if head == 0 else jnp.logical_not(low_half)
            right = jnp.where(own, k, onehot).astype(BF)
            probs = probs_ref[0, 2 * win + head]
            grad_probs = dot_nt(jnp.where(own, grad, 0.0).astype(BF), v)
            row_dot = jnp.sum(probs * grad_probs, axis=-1, keepdims=True)
            grad_scores = (probs * (grad_probs - row_dot)).astype(BF)
            by_value.append(dot_tn(probs.astype(BF), grad_low))
            by_query.append(dot_nn(grad_scores, right))
            by_key.append(dot_tn(grad_scores, q))
        rel = jnp.where(rel_lanes, jnp.where(low_half, by_query[1], by_query[0]), 0.0)
        shift = shift_ref[win]
        for bit in range(4):
            rel = jnp.where((shift & (1 << bit)) != 0, pltpu.roll(rel, 1 << bit, 1), rel)
        rel_top = rel.astype(BF)
        rel_rest = (rel - rel_top.astype(F32)).astype(BF)
        table = table_ref[...]
        from_rel = dot_nt(rel_top, table) + dot_nt(rel_rest, table)
        table_total += dot_tn(rel_top, q) + dot_tn(rel_rest, q)
        parts[0].append(jnp.where(low_half, by_query[0], by_query[1]) * SCALE + from_rel)
        parts[1].append(jnp.where(low_half, by_key[0], by_key[1]) * SCALE)
        parts[2].append(jnp.where(low_half, by_value[0], by_value[1]))
    for block in range(3):
        at = pl.multiple_of(block * D + pair * 128, 128)
        grad_qkv_ref[:, pl.ds(at, 128)] = merge_windows(*parts[block]).astype(BF)
    table_grad_ref[...] += table_total


def attention_specs(rows):
    column = lambda block: pl.BlockSpec((rows, 128), lambda pair: (0, block * PAIRS + pair))
    whole = lambda *shape: pl.BlockSpec(shape, lambda pair: (0,) * len(shape))
    return (
        [column(0), column(1), column(2)],
        [whole(128, 128), whole(2, BLOCK, 128), whole(2, BLOCK, 128)],
        pl.BlockSpec((1, 4, BLOCK, BLOCK), lambda pair: (pair, 0, 0, 0)),
        whole,
    )


def attention(qkv, table, onehot, shift):
    rows = qkv.shape[0]
    columns, constants, probs_spec, _ = attention_specs(rows)
    return pl.pallas_call(
        attn_fwd_kernel,
        grid=(PAIRS,),
        in_specs=columns + constants,
        out_specs=[pl.BlockSpec((rows, 128), lambda pair: (0, pair)), probs_spec],
        out_shape=[
            jax.ShapeDtypeStruct((rows, D), BF),
            jax.ShapeDtypeStruct((PAIRS, 4, BLOCK, BLOCK), F32),
        ],
        compiler_params=pltpu.CompilerParams(vmem_limit_bytes=32 * 1024 * 1024),
        name="attention",
    )(qkv, qkv, qkv, table, onehot, shift)


def attention_back(qkv, grad_mixed, probs, table, onehot, shift):
    rows = qkv.shape[0]
    columns, constants, probs_spec, whole = attention_specs(rows)
    return pl.pallas_call(
        attn_bwd_kernel,
        grid=(PAIRS,),
        in_specs=columns + [pl.BlockSpec((rows, 128), lambda pair: (0, pair)), probs_spec] + constants,
        out_specs=[whole(rows, 3 * D), whole(128, 128)],
        out_shape=[
            jax.ShapeDtypeStruct((rows, 3 * D), BF),
            jax.ShapeDtypeStruct((128, 128), F32),
        ],
        compiler_params=pltpu.CompilerParams(vmem_limit_bytes=32 * 1024 * 1024),
        name="attention_back",
    )(qkv, qkv, qkv, grad_mixed, probs, table, onehot, shift)


def slot_mask(window_pos):
    row_win = window_pos // NWS
    col_win = window_pos % NWS
    rows_ok = jnp.where(row_win == NWS - 1, EDGE, WIN)
    cols_ok = jnp.where(col_win == NWS - 1, EDGE, WIN)
    positions = jnp.arange(WIN, dtype=jnp.int32)
    inside = (positions[None, :, None] < rows_ok[:, None, None]) & (
        positions[None, None, :] < cols_ok[:, None, None]
    )
    return inside.reshape(-1, 1).astype(F32)


def normalise(values):
    centred = values - jnp.mean(values, axis=-1, keepdims=True)
    rstd = lax.rsqrt(jnp.mean(centred * centred, axis=-1, keepdims=True) + EPS)
    return centred * rstd, rstd


def normalise_back(grad, hat, rstd, gain):
    grad_hat = grad * gain
    return rstd * (
        grad_hat
        - jnp.mean(grad_hat, axis=-1, keepdims=True)
        - hat * jnp.mean(grad_hat * hat, axis=-1, keepdims=True)
    )


def normal_cdf(values):
    return 0.5 * (1.0 + lax.erf(values * np.float32(np.sqrt(0.5))))


def normal_pdf(values):
    return np.float32(1.0 / np.sqrt(2.0 * np.pi)) * jnp.exp(-0.5 * values * values)


def gather(shard):
    return lax.all_gather(shard, "fsdp", axis=0, tiled=True)


def scatter_sum(partial):
    return lax.psum_scatter(partial, "fsdp", scatter_dimension=0, tiled=True)


def per_device(
    tokens,
    window_pos,
    norm1_gain,
    norm1_bias,
    qkv_weight,
    qkv_bias,
    rel_pos_h,
    rel_pos_w,
    proj_weight,
    proj_bias,
    norm2_gain,
    norm2_bias,
    lin1_weight,
    lin1_bias,
    lin2_weight,
    lin2_bias,
    out_grad,
):
    vectors = (
        norm1_gain,
        norm1_bias,
        qkv_bias,
        proj_bias,
        norm2_gain,
        norm2_bias,
        lin1_bias,
        lin2_bias,
    )
    sizes = [v.shape[0] for v in vectors]
    count = sum(sizes)
    shard_rows = qkv_weight.shape[0]
    packed = jnp.pad(
        jnp.concatenate(vectors).astype(BF), (0, shard_rows * 128 - count)
    ).reshape(shard_rows, 128)
    chunk_one = gather(
        jnp.concatenate((qkv_weight.astype(BF), proj_weight.astype(BF), packed), axis=1)
    )
    w_qkv = chunk_one[:, : 3 * D]
    w_proj = chunk_one[:, 3 * D : 4 * D]
    small = chunk_one[:, 4 * D :].reshape(-1, shard_rows * 128)[:, :count].astype(F32)
    edges = np.cumsum([0] + sizes)
    gain_one, bias_one, b_qkv, b_proj, gain_two, bias_two, b_up, b_down = (
        small[:, lo:hi].reshape(-1) for lo, hi in zip(edges[:-1], edges[1:])
    )
    w_up = gather(lin1_weight.astype(BF))
    w_down = gather(lin2_weight.astype(BF))

    onehot, shift = window_constants()
    onehot = jnp.asarray(onehot, BF)
    shift = jnp.asarray(shift)
    table = table_lanes(rel_pos_h, rel_pos_w)
    live = slot_mask(window_pos)

    inputs = tokens.astype(F32)
    hat_one, rstd_one = normalise(inputs)
    normed_one = ((hat_one * gain_one + bias_one) * live).astype(BF)
    qkv = (dot_nn(normed_one, w_qkv) + b_qkv).astype(BF)
    mixed, probs = attention(qkv, table, onehot, shift)
    residual = inputs + dot_nn(mixed, w_proj) + b_proj
    hat_two, rstd_two = normalise(residual)
    normed_two = (hat_two * gain_two + bias_two).astype(BF)
    hidden = dot_nn(normed_two, w_up) + b_up
    cdf = normal_cdf(hidden)
    active = (hidden * cdf).astype(BF)
    slope = cdf + hidden * normal_pdf(hidden)
    grad_out = out_grad.astype(F32) * live
    grad_branch = grad_out.astype(BF)
    grad_w_down = dot_tn(active, grad_branch).astype(BF)
    own_down = scatter_sum(grad_w_down)
    output = ((residual + dot_nn(active, w_down) + b_down) * live).astype(BF)

    grad_hidden = (dot_nt(grad_branch, w_down) * slope).astype(BF)
    grad_w_up = dot_tn(normed_two, grad_hidden).astype(BF)
    own_up = scatter_sum(grad_w_up)
    grad_normed_two = dot_nt(grad_hidden, w_up)
    grad_residual = grad_out + normalise_back(grad_normed_two, hat_two, rstd_two, gain_two)
    grad_attn = grad_residual.astype(BF)
    grad_w_proj = dot_tn(mixed, grad_attn).astype(BF)
    grad_mixed = dot_nt(grad_attn, w_proj).astype(BF)
    grad_qkv, lanes_grad = attention_back(qkv, grad_mixed, probs, table, onehot, shift)
    grad_w_qkv = dot_tn(normed_one, grad_qkv).astype(BF)
    own_attn = scatter_sum(jnp.concatenate((grad_w_qkv, grad_w_proj), axis=1))
    grad_normed_one = dot_nt(grad_qkv, w_qkv) * live
    tokens_grad = (
        grad_residual + normalise_back(grad_normed_one, hat_one, rstd_one, gain_one)
    ).astype(BF)

    totals = (
        jnp.sum(grad_normed_one * hat_one, axis=0),
        jnp.sum(grad_normed_one, axis=0),
        jnp.sum(grad_qkv.astype(F32), axis=0),
        jnp.sum(grad_attn.astype(F32), axis=0),
        jnp.sum(grad_normed_two * hat_two, axis=0),
        jnp.sum(grad_normed_two, axis=0),
        jnp.sum(grad_hidden.astype(F32), axis=0),
        jnp.sum(grad_branch.astype(F32), axis=0),
    )
    small_total = lax.psum(jnp.concatenate(totals + (lanes_grad.reshape(-1),)), "fsdp")
    me = lax.axis_index("fsdp")
    owned, at = [], 0
    for size, total in zip(sizes, totals):
        owned.append(lax.dynamic_slice(small_total, (at + me * size,), (size,)))
        at += total.shape[0]
    table_h, table_w = table_grads(small_total[at:].reshape(128, 128))

    return (
        output,
        tokens_grad,
        owned[0],
        owned[1],
        own_attn[:, : 3 * D].astype(F32),
        owned[2],
        table_h,
        table_w,
        own_attn[:, 3 * D :].astype(F32),
        owned[3],
        owned[4],
        owned[5],
        own_up.astype(F32),
        owned[6],
        own_down.astype(F32),
        owned[7],
    )


def solution(mesh):
    rows = P("fsdp", None)
    line = P("fsdp")
    return jax.shard_map(
        per_device,
        mesh=mesh,
        in_specs=(
            rows,
            line,
            line,
            line,
            rows,
            line,
            P(),
            P(),
            rows,
            line,
            line,
            line,
            rows,
            line,
            rows,
            line,
            rows,
        ),
        out_specs=(
            rows,
            rows,
            line,
            line,
            rows,
            line,
            P(),
            P(),
            rows,
            line,
            line,
            line,
            rows,
            line,
            rows,
            line,
        ),
        check_vma=False,
    )
```

```python
import functools

import jax
import jax.numpy as jnp
import numpy as np
from jax import lax
from jax.experimental import pallas as pl
from jax.experimental.pallas import tpu as pltpu
from jax.sharding import PartitionSpec as P

D = 768
HEADS = 12
HEAD_DIM = 64
FF = 3072
WIN = 14
NWS = 5
EDGE = 8
LENGTH = WIN * WIN
PAIRS = HEADS // 2
BLOCK = 200
SCALE = HEAD_DIM ** (-0.5)
EPS = 1e-06
LANES = 256
BF = jnp.bfloat16
F32 = jnp.float32


def window_constants():
    onehot = np.zeros((2, BLOCK, 128), np.float32)
    shift = np.zeros((2, 16, LANES), np.int32)
    for win in range(2):
        for row in range(BLOCK):
            slot = row - 4 * win
            if not 0 <= slot < LENGTH:
                onehot[win, row, 63] = onehot[win, row, 127] = -1e30
                continue
            y, x = divmod(slot, WIN)
            for base in (0, 64):
                for lane in (y, 16 + y, 32 + x, 48 + x):
                    onehot[win, row, base + lane] = 1.0
            shift[win, :8, row] = WIN - 1 - y
            shift[win, 8:, row] = WIN - 1 - x
    return onehot, shift


def table_lanes(rel_pos_h, rel_pos_w):
    flip = jnp.concatenate(
        (
            jnp.pad(rel_pos_h[::-1], ((0, 5), (0, 0))),
            jnp.pad(rel_pos_w[::-1], ((0, 5), (0, 0))),
        ),
        axis=0,
    ).astype(BF) * BF(1.0 / SCALE)
    nothing = jnp.zeros_like(flip)
    return jnp.concatenate(
        (jnp.concatenate((nothing, flip), axis=1), jnp.concatenate((flip, nothing), axis=1)), axis=0
    )


def table_grads(lanes_grad):
    folded = (lanes_grad[64:, :64] + lanes_grad[:64, 64:]) * np.float32(1.0 / SCALE)
    count = 2 * WIN - 1
    return folded[:count][::-1], folded[32 : 32 + count][::-1]


def dot_nn(a, b):
    return jnp.dot(a, b, preferred_element_type=F32)


def dot_nt(a, b):
    return lax.dot_general(a, b, (((1,), (1,)), ((), ())), preferred_element_type=F32)


def dot_tn(a, b):
    return lax.dot_general(a, b, (((0,), (0,)), ((), ())), preferred_element_type=F32)


def low_half():
    return lax.broadcasted_iota(jnp.int32, (BLOCK, 128), 1) < 64


def row_valid(win):
    row = lax.broadcasted_iota(jnp.int32, (BLOCK, 128), 0)
    return row < LENGTH if win == 0 else row >= BLOCK - LENGTH


def merge_windows(first, second):
    return jnp.concatenate((first[:192], first[192:] + second[:8], second[8:]), axis=0)


def pad_rows(values):
    return jnp.concatenate((values, jnp.zeros((LANES - BLOCK, 128), F32)), axis=0)


def bit_masks(shift, rows):
    shift = jnp.broadcast_to(shift[:1], (rows, LANES))
    return [(shift & (1 << bit)) != 0 for bit in range(4)]


def skew(values, masks):
    values = jnp.where(masks[3], values[8:], values[:24])
    values = jnp.where(masks[2], pltpu.roll(values, 20, 0), values)
    values = jnp.where(masks[1], pltpu.roll(values, 22, 0), values)[:16]
    return jnp.where(masks[0][:16], pltpu.roll(values, 15, 0), values)


def unskew(values, masks):
    nothing = jnp.zeros((8, LANES), F32)
    values = jnp.concatenate((values, nothing), axis=0)
    for bit in range(3):
        values = jnp.where(masks[bit], pltpu.roll(values, 1 << bit, 0), values)
    return jnp.concatenate(
        (
            jnp.where(masks[3][:8], 0.0, values[:8]),
            jnp.where(masks[3][:16], values[:16], values[8:]),
            jnp.where(masks[3][:8], values[16:], 0.0),
        ),
        axis=0,
    )


def attn_fwd_kernel(q_ref, k_ref, v_ref, table_ref, onehot_ref, shift_ref, mixed_ref, probs_ref):
    low = low_half()
    last = lax.broadcasted_iota(jnp.int32, (16, LANES), 0) == 15
    mixed = []
    for win in range(2):
        rows = pl.ds(192 * win, BLOCK)
        queries = pad_rows(q_ref[rows, :].astype(F32) * SCALE).T
        k = k_ref[rows, :].astype(F32)
        v = v_ref[rows, :]
        rel = dot_nn(table_ref[...], queries.astype(BF))
        onehot = onehot_ref[win].astype(F32)
        by_row = bit_masks(shift_ref[win, :8], 24)
        by_col = bit_masks(shift_ref[win, 8:], 24)
        halves = []
        for head in range(2):
            base = 64 if head == 0 else 0
            from_row = skew(rel[base : base + 32], by_row)
            from_col = skew(rel[base + 32 : base + 64], by_col)
            row_top = from_row.astype(BF).astype(F32)
            col_top = from_col.astype(BF).astype(F32)
            extra = (row_top, from_row - row_top, col_top, jnp.where(last, 1.0, from_col - col_top))
            if head == 0:
                left = jnp.concatenate((queries[:64],) + extra, axis=0).astype(BF)
                right = jnp.where(low, k, onehot).astype(BF)
            else:
                left = jnp.concatenate(extra + (queries[64:],), axis=0).astype(BF)
                right = jnp.where(low, onehot, k).astype(BF)
            scores = dot_nn(right, left)
            expon = jnp.exp(scores - jnp.max(scores, axis=0, keepdims=True))
            probs = expon * (1.0 / jnp.sum(expon, axis=0, keepdims=True))
            probs_ref[0, 2 * win + head] = probs
            halves.append(dot_tn(v, probs.astype(BF)))
        both = jnp.concatenate((halves[0][:HEAD_DIM], halves[1][HEAD_DIM:]), axis=0).T[:BLOCK]
        mixed.append(jnp.where(row_valid(win), both, 0.0))
    mixed_ref[...] = merge_windows(*mixed).astype(BF)


def attn_bwd_kernel(
    q_ref,
    k_ref,
    v_ref,
    grad_ref,
    probs_ref,
    table_ref,
    onehot_ref,
    shift_ref,
    grad_qkv_ref,
    table_grad_ref,
):
    pair = pl.program_id(0)
    low = low_half()

    @pl.when(pair == 0)
    def _():
        table_grad_ref[...] = jnp.zeros_like(table_grad_ref)

    parts = ([], [], [])
    table_total = jnp.zeros((128, 128), F32)
    for win in range(2):
        rows = pl.ds(192 * win, BLOCK)
        q = pad_rows(q_ref[rows, :].astype(F32) * SCALE).astype(BF)
        k = k_ref[rows, :].astype(F32)
        v = v_ref[rows, :]
        grad = pad_rows(jnp.where(row_valid(win), grad_ref[rows, :].astype(F32), 0.0))
        grad_low = grad.astype(BF)
        wide_low = lax.broadcasted_iota(jnp.int32, (LANES, 128), 1) < 64
        onehot = onehot_ref[win].astype(F32)
        by_row = bit_masks(shift_ref[win, :8], 24)
        by_col = bit_masks(shift_ref[win, 8:], 24)
        by_query, by_key, by_value, rel = [], [], [], []
        for head in range(2):
            if head == 0:
                right = jnp.where(low, k, onehot).astype(BF)
                grad_own = jnp.where(wide_low, grad, 0.0).astype(BF)
            else:
                right = jnp.where(low, onehot, k).astype(BF)
                grad_own = jnp.where(wide_low, 0.0, grad).astype(BF)
            probs = probs_ref[0, 2 * win + head]
            grad_probs = dot_nt(v, grad_own)
            row_dot = jnp.sum(probs * grad_probs, axis=0, keepdims=True)
            grad_scores = (probs * (grad_probs - row_dot)).astype(BF)
            by_value.append(dot_nn(probs.astype(BF), grad_low))
            by_key.append(dot_nn(grad_scores, q))
            back = dot_tn(right, grad_scores)
            own, base = (back[:64], 64) if head == 0 else (back[64:], 0)
            by_query.append(own)
            rel.append(unskew(back[base : base + 16], by_row))
            rel.append(unskew(back[base + 32 : base + 48], by_col))
        rel = jnp.concatenate((rel[2], rel[3], rel[0], rel[1]), axis=0)
        rel_top = rel.astype(BF)
        rel_rest = (rel - rel_top.astype(F32)).astype(BF)
        table = table_ref[...]
        from_rel = dot_tn(table, rel_top) + dot_tn(table, rel_rest)
        table_total += dot_nn(rel_top, q) + dot_nn(rel_rest, q)
        parts[0].append((jnp.concatenate(by_query, axis=0) + from_rel).T[:BLOCK] * SCALE)
        parts[1].append(jnp.where(low, by_key[0], by_key[1]))
        parts[2].append(jnp.where(low, by_value[0], by_value[1]))
    for block in range(3):
        at = pl.multiple_of(block * D + pair * 128, 128)
        grad_qkv_ref[:, pl.ds(at, 128)] = merge_windows(*parts[block]).astype(BF)
    table_grad_ref[...] += table_total


def attention_specs(rows):
    column = lambda block: pl.BlockSpec((rows, 128), lambda pair: (0, block * PAIRS + pair))
    whole = lambda *shape: pl.BlockSpec(shape, lambda pair: (0,) * len(shape))
    return (
        [column(0), column(1), column(2)],
        [whole(128, 128), whole(2, BLOCK, 128), whole(2, 16, LANES)],
        pl.BlockSpec((1, 4, BLOCK, LANES), lambda pair: (pair, 0, 0, 0)),
        whole,
    )


def attention(qkv, table, onehot, shift):
    rows = qkv.shape[0]
    columns, constants, probs_spec, _ = attention_specs(rows)
    return pl.pallas_call(
        attn_fwd_kernel,
        grid=(PAIRS,),
        in_specs=columns + constants,
        out_specs=[pl.BlockSpec((rows, 128), lambda pair: (0, pair)), probs_spec],
        out_shape=[
            jax.ShapeDtypeStruct((rows, D), BF),
            jax.ShapeDtypeStruct((PAIRS, 4, BLOCK, LANES), F32),
        ],
        compiler_params=pltpu.CompilerParams(vmem_limit_bytes=32 * 1024 * 1024),
        name="attention",
    )(qkv, qkv, qkv, table, onehot, shift)


def attention_back(qkv, grad_mixed, probs, table, onehot, shift):
    rows = qkv.shape[0]
    columns, constants, probs_spec, whole = attention_specs(rows)
    return pl.pallas_call(
        attn_bwd_kernel,
        grid=(PAIRS,),
        in_specs=columns + [pl.BlockSpec((rows, 128), lambda pair: (0, pair)), probs_spec] + constants,
        out_specs=[whole(rows, 3 * D), whole(128, 128)],
        out_shape=[
            jax.ShapeDtypeStruct((rows, 3 * D), BF),
            jax.ShapeDtypeStruct((128, 128), F32),
        ],
        compiler_params=pltpu.CompilerParams(vmem_limit_bytes=32 * 1024 * 1024),
        name="attention_back",
    )(qkv, qkv, qkv, grad_mixed, probs, table, onehot, shift)


def slot_mask(window_pos):
    row_win = window_pos // NWS
    col_win = window_pos % NWS
    rows_ok = jnp.where(row_win == NWS - 1, EDGE, WIN)
    cols_ok = jnp.where(col_win == NWS - 1, EDGE, WIN)
    positions = jnp.arange(WIN, dtype=jnp.int32)
    inside = (positions[None, :, None] < rows_ok[:, None, None]) & (
        positions[None, None, :] < cols_ok[:, None, None]
    )
    return inside.reshape(-1, 1).astype(F32)


def normalise(values):
    centred = values - jnp.mean(values, axis=-1, keepdims=True)
    rstd = lax.rsqrt(jnp.mean(centred * centred, axis=-1, keepdims=True) + EPS)
    return centred * rstd, rstd


def normalise_back(grad, hat, rstd, gain):
    grad_hat = grad * gain
    return rstd * (
        grad_hat
        - jnp.mean(grad_hat, axis=-1, keepdims=True)
        - hat * jnp.mean(grad_hat * hat, axis=-1, keepdims=True)
    )


def normal_cdf(values):
    return 0.5 * (1.0 + lax.erf(values * np.float32(np.sqrt(0.5))))


def normal_pdf(values):
    return np.float32(1.0 / np.sqrt(2.0 * np.pi)) * jnp.exp(-0.5 * values * values)


def hop(array, mask, count):
    return lax.ppermute(array, "fsdp", [(i, i ^ mask) for i in range(count)])


def hop_plan(count):
    far = count // 4
    return (far, 2 * far, 3 * far), [1 << bit for bit in range(1, far.bit_length() - 1)]


def gather_pieces(shard, count):
    far, middle = hop_plan(count)
    received = [hop(shard, mask, count) for mask in far]
    stacks = (
        [jnp.stack((shard, received[0])), [0, far[0]], middle],
        [jnp.stack((received[1], received[2])), [far[1], far[2]], middle[::-1]],
    )
    pieces = []
    for stack, owners, masks in stacks:
        for mask in masks[:-1]:
            stack = jnp.concatenate((stack, hop(stack, mask, count)), axis=0)
            owners = owners + [owner ^ mask for owner in owners]
        pieces.append((stack, owners))
        pieces.append((hop(stack, masks[-1], count), [owner ^ masks[-1] for owner in owners]))
    other = [(hop(stack, 1, count), [owner ^ 1 for owner in owners]) for stack, owners in pieces]
    return pieces + other


def place_kernel(owners, columns, me_ref, *refs):
    stacks, outs, sem = refs[: len(owners)], refs[len(owners) : -1], refs[-1]
    copies = []
    for stack, stack_owners in zip(stacks, owners):
        for index, mask in enumerate(stack_owners):
            owner = jnp.bitwise_xor(me_ref[0], mask)
            for out, (lo, hi) in zip(outs, columns):
                copies.append(
                    pltpu.make_async_copy(
                        stack.at[index, :, lo:hi], out.at[owner], sem.at[len(copies)]
                    )
                )
                copies[-1].start()
    for copy in copies:
        copy.wait()


def place(pieces, widths, me, count):
    edges = np.cumsum([0] + list(widths))
    columns = tuple(zip(edges[:-1].tolist(), edges[1:].tolist()))
    stacks = [stack for stack, _ in pieces]
    rows = stacks[0].shape[1]
    outs = pl.pallas_call(
        functools.partial(place_kernel, tuple(tuple(o) for _, o in pieces), columns),
        in_specs=[pl.BlockSpec(memory_space=pltpu.SMEM)]
        + [pl.BlockSpec(memory_space=pl.ANY)] * len(stacks),
        out_specs=[pl.BlockSpec(memory_space=pltpu.VMEM)] * len(widths),
        out_shape=[jax.ShapeDtypeStruct((count, rows, width), BF) for width in widths],
        scratch_shapes=[pltpu.SemaphoreType.DMA((count * len(widths),))],
        compiler_params=pltpu.CompilerParams(vmem_limit_bytes=16 * 1024 * 1024),
        name="place",
    )(me.reshape(1), *stacks)
    return [out.reshape(count * rows, width) for out, width in zip(outs, widths)]


def sum_order(count):
    far, middle = hop_plan(count)
    order = []
    for masks, last in ((middle, (0, far[0])), (middle[::-1], (far[1], far[2]))):
        block = list(last)
        for mask in masks[::-1]:
            block = block + [owner ^ mask for owner in block]
        order += block
    return order + [owner ^ 1 for owner in order]


def order_matrix(me, count, rows):
    masks = np.repeat(np.array(sum_order(count), np.int32), rows)
    wanted = jnp.bitwise_xor(me, masks) * rows + np.tile(np.arange(rows, dtype=np.int32), count)
    features = lax.broadcasted_iota(jnp.int32, (count * rows, count * rows), 0)
    return (features == wanted[None, :]).astype(BF)


def pick_kernel(masks, me_ref, stack, kept, sent, sem):
    half = len(masks) // 2
    copies = []
    for index, mask in enumerate(masks):
        owner = jnp.bitwise_xor(me_ref[0], mask)
        out = kept if index < half else sent
        copies.append(
            pltpu.make_async_copy(stack.at[owner], out.at[index % half], sem.at[index])
        )
        copies[-1].start()
    for copy in copies:
        copy.wait()


def pick(array, me, count):
    stack = array.reshape(count, -1, array.shape[-1])
    half = jax.ShapeDtypeStruct((count // 2,) + stack.shape[1:], BF)
    return pl.pallas_call(
        functools.partial(pick_kernel, tuple(sum_order(count))),
        in_specs=[
            pl.BlockSpec(memory_space=pltpu.SMEM),
            pl.BlockSpec(memory_space=pl.ANY),
        ],
        out_specs=[pl.BlockSpec(memory_space=pltpu.VMEM)] * 2,
        out_shape=[half, half],
        scratch_shapes=[pltpu.SemaphoreType.DMA((count,))],
        compiler_params=pltpu.CompilerParams(vmem_limit_bytes=16 * 1024 * 1024),
        name="pick",
    )(me.reshape(1), stack)


def add_low(left, right):
    return (left.astype(F32) + right.astype(F32)).astype(BF)


def scatter_sum(kept, sent, count):
    far, middle = hop_plan(count)
    blocks = count // 2
    kept = kept.reshape(blocks, -1, kept.shape[-1])
    arrived = hop(sent.reshape(kept.shape), 1, count)
    half = blocks // 2
    ends = []
    for at, masks in ((0, middle), (half, middle[::-1])):
        here, there, size = kept[at : at + half], arrived[at : at + half], half
        for mask in masks:
            size //= 2
            away = hop(add_low(here[size:], there[size:]), mask, count)
            here, there = add_low(here[:size], there[:size]), away
        ends.append((here, there))
    (near, near_in), (back, back_in) = ends
    total = near[0].astype(F32) + near_in[0].astype(F32)
    sends = (
        add_low(near[1], near_in[1]),
        add_low(back[0], back_in[0]),
        add_low(back[1], back_in[1]),
    )
    for block, mask in zip(sends, far):
        total = total + hop(block, mask, count).astype(F32)
    return total


def sum_everywhere(vector, count):
    mask = 1
    while mask < count:
        vector = vector + hop(vector, mask, count)
        mask *= 2
    return vector


def per_device(
    tokens,
    window_pos,
    norm1_gain,
    norm1_bias,
    qkv_weight,
    qkv_bias,
    rel_pos_h,
    rel_pos_w,
    proj_weight,
    proj_bias,
    norm2_gain,
    norm2_bias,
    lin1_weight,
    lin1_bias,
    lin2_weight,
    lin2_bias,
    out_grad,
):
    vectors = (
        norm1_gain,
        norm1_bias,
        qkv_bias,
        proj_bias,
        norm2_gain,
        norm2_bias,
        lin1_bias,
        lin2_bias,
    )
    sizes = [v.shape[0] for v in vectors]
    used = sum(sizes)
    shard_rows = qkv_weight.shape[0]
    packed = jnp.pad(
        jnp.concatenate(vectors).astype(BF), (0, shard_rows * 128 - used)
    ).reshape(shard_rows, 128)
    count = lax.axis_size("fsdp")
    me = lax.axis_index("fsdp")
    first = jnp.concatenate((qkv_weight.astype(BF), proj_weight.astype(BF), packed), axis=1)
    w_qkv, w_proj, small = place(gather_pieces(first, count), (3 * D, D, 128), me, count)
    (w_up,) = place(gather_pieces(lin1_weight.astype(BF), count), (FF,), me, count)
    w_down = lax.all_gather(lin2_weight.astype(BF), "fsdp", axis=0, tiled=True)
    small = small.reshape(count, shard_rows * 128)[:, :used].astype(F32)
    edges = np.cumsum([0] + sizes)
    gain_one, bias_one, b_qkv, b_proj, gain_two, bias_two, b_up, b_down = (
        small[:, lo:hi].reshape(-1) for lo, hi in zip(edges[:-1], edges[1:])
    )
    order = order_matrix(me, count, shard_rows)

    onehot, shift = window_constants()
    onehot = jnp.asarray(onehot, BF)
    shift = jnp.asarray(shift)
    table = table_lanes(rel_pos_h, rel_pos_w)
    live = slot_mask(window_pos)

    inputs = tokens.astype(F32)
    hat_one, rstd_one = normalise(inputs)
    normed_one = ((hat_one * gain_one + bias_one) * live).astype(BF)
    qkv = (dot_nn(normed_one, w_qkv) + b_qkv).astype(BF)
    mixed, probs = attention(qkv, table, onehot, shift)
    residual = inputs + dot_nn(mixed, w_proj) + b_proj
    hat_two, rstd_two = normalise(residual)
    normed_two = (hat_two * gain_two + bias_two).astype(BF)
    hidden = dot_nn(normed_two, w_up) + b_up
    cdf = normal_cdf(hidden)
    active = (hidden * cdf).astype(BF)
    slope = cdf + hidden * normal_pdf(hidden)
    grad_out = out_grad.astype(F32) * live
    grad_branch = grad_out.astype(BF)
    grad_w_down = dot_tn(active, grad_branch).astype(BF)
    own_down = scatter_sum(*pick(grad_w_down, me, count), count)
    output = ((residual + dot_nn(active, w_down) + b_down) * live).astype(BF)

    grad_hidden = (dot_nt(grad_branch, w_down) * slope).astype(BF)
    ordered = dot_nn(normed_two, order).astype(BF)
    kept = dot_tn(ordered[:, : D // 2], grad_hidden).astype(BF)
    sent = dot_tn(ordered[:, D // 2 :], grad_hidden).astype(BF)
    kept, sent, grad_hidden = lax.optimization_barrier((kept, sent, grad_hidden))
    own_up = scatter_sum(kept, sent, count)
    grad_normed_two = dot_nt(grad_hidden, w_up)
    grad_residual = grad_out + normalise_back(grad_normed_two, hat_two, rstd_two, gain_two)
    grad_attn = grad_residual.astype(BF)
    ordered = dot_nn(mixed, order).astype(BF)
    kept = dot_tn(ordered[:, : D // 2], grad_attn).astype(BF)
    sent = dot_tn(ordered[:, D // 2 :], grad_attn).astype(BF)
    kept, sent, grad_attn = lax.optimization_barrier((kept, sent, grad_attn))
    own_proj = scatter_sum(kept, sent, count)
    grad_mixed = dot_nt(grad_attn, w_proj).astype(BF)
    grad_qkv, lanes_grad = attention_back(qkv, grad_mixed, probs, table, onehot, shift)
    ordered = dot_nn(normed_one, order).astype(BF)
    kept = dot_tn(ordered[:, : D // 2], grad_qkv).astype(BF)
    sent = dot_tn(ordered[:, D // 2 :], grad_qkv).astype(BF)
    kept, sent, grad_qkv = lax.optimization_barrier((kept, sent, grad_qkv))
    own_qkv = scatter_sum(kept, sent, count)
    grad_normed_one = dot_nt(grad_qkv, w_qkv) * live
    tokens_grad = (
        grad_residual + normalise_back(grad_normed_one, hat_one, rstd_one, gain_one)
    ).astype(BF)

    totals = (
        jnp.sum(grad_normed_one * hat_one, axis=0),
        jnp.sum(grad_normed_one, axis=0),
        jnp.sum(grad_qkv.astype(F32), axis=0),
        jnp.sum(grad_attn.astype(F32), axis=0),
        jnp.sum(grad_normed_two * hat_two, axis=0),
        jnp.sum(grad_normed_two, axis=0),
        jnp.sum(grad_hidden.astype(F32), axis=0),
        jnp.sum(grad_branch.astype(F32), axis=0),
    )
    by_owner = jnp.concatenate([total.reshape(count, -1) for total in totals], axis=1).reshape(-1)
    table_h, table_w = table_grads(lanes_grad)
    small_total = sum_everywhere(
        jnp.concatenate((by_owner, table_h.reshape(-1), table_w.reshape(-1))), count
    )
    own_small = lax.dynamic_slice(small_total, (me * used,), (used,))
    owned = [own_small[lo:hi] for lo, hi in zip(edges[:-1], edges[1:])]
    table_h, table_w = small_total[count * used :].reshape(2, 2 * WIN - 1, HEAD_DIM)

    return (
        output,
        tokens_grad,
        owned[0],
        owned[1],
        own_qkv,
        owned[2],
        table_h,
        table_w,
        own_proj,
        owned[3],
        owned[4],
        owned[5],
        own_up,
        owned[6],
        own_down.astype(F32),
        owned[7],
    )


def solution(mesh):
    rows = P("fsdp", None)
    line = P("fsdp")
    return jax.shard_map(
        per_device,
        mesh=mesh,
        in_specs=(
            rows,
            line,
            line,
            line,
            rows,
            line,
            P(),
            P(),
            rows,
            line,
            line,
            line,
            rows,
            line,
            rows,
            line,
            rows,
        ),
        out_specs=(
            rows,
            rows,
            line,
            line,
            rows,
            line,
            P(),
            P(),
            rows,
            line,
            line,
            line,
            rows,
            line,
            rows,
            line,
        ),
        check_vma=False,
    )
```

```python
import functools

import jax
import jax.numpy as jnp
import numpy as np
from jax import lax
from jax.experimental import pallas as pl
from jax.experimental.pallas import tpu as pltpu
from jax.sharding import PartitionSpec as P

D = 768
HEADS = 12
HEAD_DIM = 64
FF = 3072
WIN = 14
NWS = 5
EDGE = 8
LENGTH = WIN * WIN
GROUPS = 2
PAIRS = HEADS // 2 // GROUPS
GROUP = PAIRS * 128
BLOCK = 200
SCALE = HEAD_DIM ** (-0.5)
EPS = 1e-06
QUICK = pl.CostEstimate(flops=1, bytes_accessed=1, transcendentals=0)
LANES = 256
BF = jnp.bfloat16
F32 = jnp.float32


def window_constants():
    onehot = np.zeros((2, BLOCK, 128), np.float32)
    shift = np.zeros((2, 16, LANES), np.int32)
    for win in range(2):
        for row in range(BLOCK):
            slot = row - 4 * win
            if not 0 <= slot < LENGTH:
                onehot[win, row, 63] = onehot[win, row, 127] = -1e30
                continue
            y, x = divmod(slot, WIN)
            for base in (0, 64):
                for lane in (0, 16):
                    onehot[win, row, base + lane + WIN - 1 - y] = 1.0
                    onehot[win, row, base + 32 + lane + WIN - 1 - x] = 1.0
            shift[win, :8, row] = y
            shift[win, 8:, row] = x
    return onehot, shift


def table_lanes(rel_pos_h, rel_pos_w):
    flip = jnp.concatenate(
        (
            jnp.pad(rel_pos_h, ((0, 5), (0, 0))),
            jnp.pad(rel_pos_w, ((0, 5), (0, 0))),
        ),
        axis=0,
    ).astype(BF) * BF(1.0 / SCALE)
    nothing = jnp.zeros_like(flip)
    return jnp.concatenate(
        (jnp.concatenate((nothing, flip), axis=1), jnp.concatenate((flip, nothing), axis=1)), axis=0
    )


def dot_nn(a, b):
    return jnp.dot(a, b, preferred_element_type=F32)


def dot_nt(a, b):
    return lax.dot_general(a, b, (((1,), (1,)), ((), ())), preferred_element_type=F32)


def dot_tn(a, b):
    return lax.dot_general(a, b, (((0,), (0,)), ((), ())), preferred_element_type=F32)


def low_half():
    return lax.broadcasted_iota(jnp.int32, (BLOCK, 128), 1) < 64


def row_valid(win):
    row = lax.broadcasted_iota(jnp.int32, (BLOCK, 128), 0)
    return row < LENGTH if win == 0 else row >= BLOCK - LENGTH


def merge_windows(first, second):
    return jnp.concatenate((first[:192], first[192:] + second[:8], second[8:]), axis=0)


def pad_rows(values):
    return jnp.concatenate((values, jnp.zeros((LANES - BLOCK, 128), F32)), axis=0)


def bit_masks(shift, rows):
    shift = jnp.broadcast_to(shift[:1], (rows, LANES))
    return [(shift & (1 << bit)) != 0 for bit in range(4)]


def skew(values, masks):
    values = jnp.where(masks[3], values[8:], values[:24])
    values = jnp.where(masks[2], pltpu.roll(values, 20, 0), values)
    values = jnp.where(masks[1], pltpu.roll(values, 22, 0), values)[:16]
    return jnp.where(masks[0][:16], pltpu.roll(values, 15, 0), values)


def unskew(values, masks):
    nothing = jnp.zeros((8, LANES), F32)
    values = jnp.concatenate((values, nothing), axis=0)
    for bit in range(3):
        values = jnp.where(masks[bit], pltpu.roll(values, 1 << bit, 0), values)
    return jnp.concatenate(
        (
            jnp.where(masks[3][:8], 0.0, values[:8]),
            jnp.where(masks[3][:16], values[:16], values[8:]),
            jnp.where(masks[3][:8], values[16:], 0.0),
        ),
        axis=0,
    )


def attn_fwd_kernel(q_ref, k_ref, v_ref, table_ref, onehot_ref, shift_ref, mixed_ref, probs_ref):
    low = low_half()
    last = lax.broadcasted_iota(jnp.int32, (16, LANES), 0) == 15
    mixed = []
    for win in range(2):
        rows = pl.ds(192 * win, BLOCK)
        queries = pad_rows(q_ref[rows, :].astype(F32) * SCALE).T
        k = k_ref[rows, :].astype(F32)
        v = v_ref[rows, :]
        rel = dot_nn(table_ref[...], queries.astype(BF))
        onehot = onehot_ref[win].astype(F32)
        by_row = bit_masks(shift_ref[win, :8], 24)
        by_col = bit_masks(shift_ref[win, 8:], 24)
        halves = []
        for head in range(2):
            base = 64 if head == 0 else 0
            from_row = skew(rel[base : base + 32], by_row)
            from_col = skew(rel[base + 32 : base + 64], by_col)
            row_top = from_row.astype(BF).astype(F32)
            col_top = from_col.astype(BF).astype(F32)
            extra = (row_top, from_row - row_top, col_top, jnp.where(last, 1.0, from_col - col_top))
            if head == 0:
                left = jnp.concatenate((queries[:64],) + extra, axis=0).astype(BF)
                right = jnp.where(low, k, onehot).astype(BF)
            else:
                left = jnp.concatenate(extra + (queries[64:],), axis=0).astype(BF)
                right = jnp.where(low, onehot, k).astype(BF)
            scores = dot_nn(right, left)
            expon = jnp.exp(scores - jnp.max(scores, axis=0, keepdims=True))
            probs = expon * (1.0 / jnp.sum(expon, axis=0, keepdims=True))
            probs_ref[0, 2 * win + head] = probs
            halves.append(dot_tn(v, probs.astype(BF)))
        both = jnp.concatenate((halves[0][:HEAD_DIM], halves[1][HEAD_DIM:]), axis=0).T[:BLOCK]
        mixed.append(jnp.where(row_valid(win), both, 0.0))
    mixed_ref[...] = merge_windows(*mixed).astype(BF)


def attn_bwd_kernel(
    q_ref,
    k_ref,
    v_ref,
    grad_ref,
    probs_ref,
    table_ref,
    onehot_ref,
    shift_ref,
    grad_qkv_ref,
    table_grad_ref,
):
    pair = pl.program_id(0)
    low = low_half()

    @pl.when(pair == 0)
    def _():
        table_grad_ref[...] = jnp.zeros_like(table_grad_ref)

    parts = ([], [], [])
    table_total = jnp.zeros((128, 128), F32)
    for win in range(2):
        rows = pl.ds(192 * win, BLOCK)
        q = pad_rows(q_ref[rows, :].astype(F32) * SCALE).astype(BF)
        k = k_ref[rows, :].astype(F32)
        v = v_ref[rows, :]
        grad = pad_rows(jnp.where(row_valid(win), grad_ref[rows, :].astype(F32), 0.0))
        grad_low = grad.astype(BF)
        wide_low = lax.broadcasted_iota(jnp.int32, (LANES, 128), 1) < 64
        onehot = onehot_ref[win].astype(F32)
        by_row = bit_masks(shift_ref[win, :8], 24)
        by_col = bit_masks(shift_ref[win, 8:], 24)
        by_query, by_key, by_value, rel = [], [], [], []
        for head in range(2):
            if head == 0:
                right = jnp.where(low, k, onehot).astype(BF)
                grad_own = jnp.where(wide_low, grad, 0.0).astype(BF)
            else:
                right = jnp.where(low, onehot, k).astype(BF)
                grad_own = jnp.where(wide_low, 0.0, grad).astype(BF)
            probs = probs_ref[0, 2 * win + head]
            grad_probs = dot_nt(v, grad_own)
            row_dot = jnp.sum(probs * grad_probs, axis=0, keepdims=True)
            grad_scores = (probs * (grad_probs - row_dot)).astype(BF)
            by_value.append(dot_nn(probs.astype(BF), grad_low))
            by_key.append(dot_nn(grad_scores, q))
            back = dot_tn(right, grad_scores)
            own, base = (back[:64], 64) if head == 0 else (back[64:], 0)
            by_query.append(own)
            rel.append(unskew(back[base : base + 16], by_row))
            rel.append(unskew(back[base + 32 : base + 48], by_col))
        rel = jnp.concatenate((rel[2], rel[3], rel[0], rel[1]), axis=0)
        rel_top = rel.astype(BF)
        rel_rest = (rel - rel_top.astype(F32)).astype(BF)
        table = table_ref[...]
        from_rel = dot_tn(table, rel_top) + dot_tn(table, rel_rest)
        table_total += dot_nn(rel_top, q) + dot_nn(rel_rest, q)
        parts[0].append((jnp.concatenate(by_query, axis=0) + from_rel).T[:BLOCK] * SCALE)
        parts[1].append(jnp.where(low, by_key[0], by_key[1]))
        parts[2].append(jnp.where(low, by_value[0], by_value[1]))
    for block in range(3):
        at = pl.multiple_of(block * GROUP + pair * 128, 128)
        grad_qkv_ref[:, pl.ds(at, 128)] = merge_windows(*parts[block]).astype(BF)
    table_grad_ref[...] += table_total


def attention_specs(rows):
    column = lambda block: pl.BlockSpec((rows, 128), lambda pair: (0, block * PAIRS + pair))
    whole = lambda *shape: pl.BlockSpec(shape, lambda pair: (0,) * len(shape))
    return (
        [column(0), column(1), column(2)],
        [whole(128, 128), whole(2, BLOCK, 128), whole(2, 16, LANES)],
        pl.BlockSpec((1, 4, BLOCK, LANES), lambda pair: (pair, 0, 0, 0)),
        whole,
    )


def attention(qkv, table, onehot, shift):
    rows = qkv.shape[0]
    columns, constants, probs_spec, _ = attention_specs(rows)
    return pl.pallas_call(
        attn_fwd_kernel,
        grid=(PAIRS,),
        in_specs=columns + constants,
        out_specs=[pl.BlockSpec((rows, 128), lambda pair: (0, pair)), probs_spec],
        out_shape=[
            jax.ShapeDtypeStruct((rows, GROUP), BF),
            jax.ShapeDtypeStruct((PAIRS, 4, BLOCK, LANES), F32),
        ],
        cost_estimate=QUICK,
        compiler_params=pltpu.CompilerParams(vmem_limit_bytes=32 * 1024 * 1024),
        name="attention",
    )(qkv, qkv, qkv, table, onehot, shift)


def attention_back(qkv, grad_mixed, probs, table, onehot, shift):
    rows = qkv.shape[0]
    columns, constants, probs_spec, whole = attention_specs(rows)
    return pl.pallas_call(
        attn_bwd_kernel,
        grid=(PAIRS,),
        in_specs=columns + [pl.BlockSpec((rows, 128), lambda pair: (0, pair)), probs_spec] + constants,
        out_specs=[whole(rows, 3 * GROUP), whole(128, 128)],
        out_shape=[
            jax.ShapeDtypeStruct((rows, 3 * GROUP), BF),
            jax.ShapeDtypeStruct((128, 128), F32),
        ],
        cost_estimate=QUICK,
        compiler_params=pltpu.CompilerParams(vmem_limit_bytes=32 * 1024 * 1024),
        name="attention_back",
    )(qkv, qkv, qkv, grad_mixed, probs, table, onehot, shift)


def slot_mask(window_pos):
    row_win = window_pos // NWS
    col_win = window_pos % NWS
    rows_ok = jnp.where(row_win == NWS - 1, EDGE, WIN)
    cols_ok = jnp.where(col_win == NWS - 1, EDGE, WIN)
    positions = jnp.arange(WIN, dtype=jnp.int32)
    inside = (positions[None, :, None] < rows_ok[:, None, None]) & (
        positions[None, None, :] < cols_ok[:, None, None]
    )
    return inside.reshape(-1, 1).astype(F32)


def normalise(values):
    centred = values - jnp.mean(values, axis=-1, keepdims=True)
    rstd = lax.rsqrt(jnp.mean(centred * centred, axis=-1, keepdims=True) + EPS)
    return centred * rstd, rstd


def normalise_back(grad, hat, rstd, gain):
    grad_hat = grad * gain
    return rstd * (
        grad_hat
        - jnp.mean(grad_hat, axis=-1, keepdims=True)
        - hat * jnp.mean(grad_hat * hat, axis=-1, keepdims=True)
    )


def normal_cdf(values):
    return 0.5 * (1.0 + lax.erf(values * np.float32(np.sqrt(0.5))))


def normal_pdf(values):
    return np.float32(1.0 / np.sqrt(2.0 * np.pi)) * jnp.exp(-0.5 * values * values)


def copy_rows(pieces, columns, out, to, sems):
    rows = pieces[0].shape[0]
    lo, width = columns
    return [
        pltpu.make_async_copy(
            piece.at[:, pl.ds(lo, width)],
            out.at[index * rows : (index + 1) * rows, pl.ds(to, width)],
            sems.at[index],
        )
        for index, piece in enumerate(pieces)
    ]


def start_all(copies):
    for copy in copies:
        copy.start()


def wait_all(copies):
    for copy in copies:
        copy.wait()


def front_kernel(tokens_ref, live_ref, order_ref, rows_ref, b_qkv_ref, *rest):
    pieces, (normed_ref, one_ref, two_ref, weight, sem) = rest[:PIECES], rest[PIECES:]
    copies = [copy_rows(pieces, (block * D, D), weight, block * D, sem.at[block]) for block in range(3)]
    for block in copies:
        start_all(block)
    unit, _ = normalise(tokens_ref[...].astype(F32))
    normed = ((unit * rows_ref[0:1, :] + rows_ref[1:2, :]) * live_ref[...]).astype(BF)
    normed = dot_nn(normed, order_ref[...]).astype(BF)
    normed_ref[...] = normed
    for block in range(3):
        wait_all(copies[block])
        at = block * D
        values = (dot_nn(normed, weight[:, at : at + D]) + b_qkv_ref[:, at : at + D]).astype(BF)
        one_ref[:, block * GROUP : (block + 1) * GROUP] = values[:, :GROUP]
        two_ref[:, block * GROUP : (block + 1) * GROUP] = values[:, GROUP:]


PIECES = 8
HBM = pl.BlockSpec(memory_space=pl.ANY)
VMEM = pl.BlockSpec(memory_space=pltpu.VMEM)
SMEM = pl.BlockSpec(memory_space=pltpu.SMEM)


def front(tokens, live, order, vectors, b_qkv, pieces):
    rows = tokens.shape[0]
    return pl.pallas_call(
        front_kernel,
        in_specs=[VMEM] * 5 + [HBM] * PIECES,
        out_specs=[VMEM] * 3,
        out_shape=[struct((rows, D), BF)] + [struct((rows, 3 * GROUP), BF)] * GROUPS,
        scratch_shapes=[pltpu.VMEM((D, 3 * D), BF), pltpu.SemaphoreType.DMA((3, PIECES))],
        cost_estimate=QUICK,
        compiler_params=pltpu.CompilerParams(vmem_limit_bytes=32 * 1024 * 1024),
        name="front",
    )(tokens, live, order, vectors, b_qkv, *in_hbm(pieces))


def proj_kernel(tokens_ref, one_ref, two_ref, order_ref, rows_ref, *rest):
    pieces, (residual_ref, normed_ref, turned_ref, mixed_ref, w_proj, sem) = rest[:PIECES], rest[PIECES:]
    b_proj, gain, bias = (rows_ref[i : i + 1, :] for i in range(3))
    copies = copy_rows(pieces, (0, D), w_proj, 0, sem)
    start_all(copies)
    mixed = dot_nn(one_ref[...], order_ref[:GROUP, :]) + dot_nn(two_ref[...], order_ref[GROUP:, :])
    mixed = mixed.astype(BF)
    mixed_ref[...] = mixed
    wait_all(copies)
    values = tokens_ref[...].astype(F32) + dot_nn(mixed, w_proj[...]) + b_proj
    residual_ref[...] = values
    low = (normalise(values)[0] * gain + bias).astype(BF)
    low = dot_nn(low, order_ref[...])
    normed_ref[...] = low.astype(BF)
    turned_ref[...] = low.T.astype(BF)


def mlp_kernel(split_rows, owners, place_ref, me_ref, *rest):
    normed_ref, turned_ref, residual_ref, mixed_ref, live_ref, out_grad_ref, *rest = rest
    order_ref, rows_ref, b_up_ref, *rest = rest
    up_pieces, rest = rest[:PIECES], rest[PIECES:]
    down_pieces, rest = rest[: len(owners)], rest[len(owners) :]
    output_ref, grad_residual_ref, grad_one_ref, grad_two_ref, kept_ref, sent_ref, *rest = rest
    kept_proj_ref, sent_proj_ref, sums_ref, grad_b_ref, *rest = rest
    if split_rows:
        kept_down_ref, sent_down_ref, *rest = rest
    else:
        grad_down_ref, *rest = rest
    branch, total, grad_normed, w_up, w_down, w_proj, staged, sem, up_sem, down_sem = rest
    step = pl.program_id(0)
    last = STEPS - 1
    half = D // 2

    def up_copies(index):
        return copy_rows(up_pieces, (D + index * TILE, TILE), w_up, index * TILE, up_sem.at[index])

    def proj_copies():
        return copy_rows(up_pieces, (0, D), w_proj, 0, up_sem.at[STEPS])

    def down_copies():
        copies = []
        for piece, masks in zip(down_pieces, owners):
            rows = piece.shape[0] // len(masks)
            for index, mask in enumerate(masks):
                to = jnp.bitwise_xor(me_ref[0], mask) * rows
                copies.append(
                    pltpu.make_async_copy(
                        piece.at[index * rows : (index + 1) * rows],
                        w_down.at[pl.ds(pl.multiple_of(to, rows), rows)],
                        down_sem.at[len(copies)],
                    )
                )
        return copies

    @pl.when(step == 0)
    def _():
        start_all(up_copies(0))
        copies = down_copies()
        start_all(copies)
        for index in range(1, STEPS):
            start_all(up_copies(index))
        start_all(proj_copies())
        branch[...] = (out_grad_ref[...].astype(F32) * live_ref[...]).astype(BF)
        total[...] = jnp.zeros_like(total)
        grad_normed[...] = jnp.zeros_like(grad_normed)
        wait_all(copies)

    wait_all(up_copies(step))
    at = pl.multiple_of(step * TILE, TILE)
    weight = w_down[pl.ds(at, TILE), :]
    weight_up = w_up[:, pl.ds(at, TILE)]
    hidden = dot_nn(normed_ref[...], weight_up) + b_up_ref[...]
    grad_active = dot_nt(branch[...], weight)
    cdf = normal_cdf(hidden)
    active = (hidden * cdf).astype(BF)
    grad_hidden = (grad_active * (cdf + hidden * normal_pdf(hidden))).astype(BF)
    grad_down = dot_tn(active, branch[...]).astype(BF)
    total[...] += dot_nn(active, weight)
    sent_ref[...] = dot_nn(turned_ref[half:, :], grad_hidden).astype(BF)
    kept_ref[...] = dot_nn(turned_ref[:half, :], grad_hidden).astype(BF)
    grad_normed[...] += dot_nt(grad_hidden, weight_up)
    grad_b_ref[...] = jnp.sum(grad_hidden.astype(F32), axis=0, keepdims=True)
    if split_rows:
        slot = lax.rem(step, 2)
        blocks = staged.shape[1]

        def copy(slot, block, out, to):
            return pltpu.make_async_copy(staged.at[slot, block], out.at[to], sem.at[slot, block])

        @pl.when(step >= 2)
        def _():
            for block in range(blocks):
                copy(slot, block, kept_down_ref, 0).wait()

        staged[slot] = grad_down.reshape(blocks, split_rows, D)
        places = kept_down_ref.shape[0]
        for block in range(blocks):
            to = place_ref[step * blocks + block]

            @pl.when(to < places)
            def _():
                copy(slot, block, kept_down_ref, to).start()

            @pl.when(to >= places)
            def _():
                copy(slot, block, sent_down_ref, to - places).start()

    else:
        grad_down_ref[...] = grad_down

    @pl.when(step == last)
    def _():
        wait_all(proj_copies())
        gain, b_down = rows_ref[1:2, :], rows_ref[3:4, :]
        live = live_ref[...]
        residual = residual_ref[...]
        output_ref[...] = ((residual + total[...] + b_down) * live).astype(BF)
        grad = natural_order(grad_normed[...], order_ref[...])
        unit, rstd = normalise(residual)
        grad_residual = out_grad_ref[...].astype(F32) * live + normalise_back(
            grad, unit, rstd, gain
        )
        grad_residual_ref[...] = grad_residual
        grad_attn = grad_residual.astype(BF)
        grad_mixed = dot_nt(grad_attn, w_proj[...]).astype(BF)
        grad_mixed = dot_nt(grad_mixed, order_ref[...]).astype(BF)
        grad_one_ref[...] = grad_mixed[:, :GROUP]
        grad_two_ref[...] = grad_mixed[:, GROUP:]
        sent_proj_ref[...] = dot_tn(mixed_ref[:, half:], grad_attn).astype(BF)
        kept_proj_ref[...] = dot_tn(mixed_ref[:, :half], grad_attn).astype(BF)
        sums_ref[0:1, :] = jnp.sum(grad_attn.astype(F32), axis=0, keepdims=True)
        sums_ref[1:2, :] = jnp.sum(grad * unit, axis=0, keepdims=True)
        sums_ref[2:3, :] = jnp.sum(grad, axis=0, keepdims=True)
        sums_ref[3:4, :] = jnp.sum(branch[...].astype(F32), axis=0, keepdims=True)
        sums_ref[4:, :] = jnp.zeros((4, D), F32)
        if split_rows:
            for last_slot in range(2):
                for block in range(staged.shape[1]):
                    pltpu.make_async_copy(
                        staged.at[last_slot, block], kept_down_ref.at[0], sem.at[last_slot, block]
                    ).wait()


def natural_order(values, order):
    top = values.astype(BF)
    rest = (values - top.astype(F32)).astype(BF)
    return dot_nt(top, order) + dot_nt(rest, order)


TILE = 768
STEPS = FF // TILE


def whole(*shape):
    return pl.BlockSpec(shape, lambda step: (0,) * len(shape))


def struct(shape, dtype):
    return jax.ShapeDtypeStruct(shape, dtype)


def in_hbm(arrays):
    return [pltpu.with_memory_space_constraint(array, pltpu.HBM) for array in arrays]


def project(tokens, mixed, order, vectors, pieces):
    rows = tokens.shape[0]
    return pl.pallas_call(
        proj_kernel,
        in_specs=[VMEM] * 5 + [HBM] * PIECES,
        out_specs=[VMEM] * 4,
        out_shape=[
            struct((rows, D), F32),
            struct((rows, D), BF),
            struct((D, rows), BF),
            struct((rows, D), BF),
        ],
        scratch_shapes=[pltpu.VMEM((D, D), BF), pltpu.SemaphoreType.DMA((PIECES,))],
        cost_estimate=QUICK,
        compiler_params=pltpu.CompilerParams(vmem_limit_bytes=24 * 1024 * 1024),
        name="project",
    )(tokens, *mixed, order, vectors, *in_hbm(pieces))


def mlp(
    me, count, normed, turned, residual, mixed, live, out_grad, order, vectors, b_up, up_pieces, down_pieces
):
    rows = residual.shape[0]
    block_rows = FF // count
    split_rows = block_rows if block_rows % 16 == 0 else 0
    column = lambda height: pl.BlockSpec((height, TILE), lambda step: (0, step))
    inverse = np.argsort(np.array(sum_order(count)))
    places = jnp.take(jnp.asarray(inverse, jnp.int32), jnp.bitwise_xor(me, np.arange(count)))
    if split_rows:
        owners = tuple(tuple(masks) for _, masks in down_pieces)
        down_pieces = [stack.reshape(-1, D) for stack, _ in down_pieces]
        half = struct((count // 2, block_rows, D), BF)
        grad_specs, grad_shapes = [HBM] * 2, [half, half]
        staged = (2, TILE // block_rows, block_rows, D)
    else:
        down_pieces = place(down_pieces, ((0, 0, D, 0),), (D,), me, count)
        owners, me_down = ((0,),), jnp.zeros_like(me)
        grad_specs = [pl.BlockSpec((TILE, D), lambda step: (step, 0))]
        grad_shapes = [struct((FF, D), BF)]
        staged = (2, 1, 16, 128)
    wide, turn, square = (rows, D), (D, rows), (D, D)
    results = pl.pallas_call(
        functools.partial(mlp_kernel, split_rows, owners),
        grid=(STEPS,),
        in_specs=[
            SMEM,
            SMEM,
            whole(*wide),
            whole(*turn),
            whole(*wide),
            whole(*wide),
            whole(rows, 1),
            whole(*wide),
            whole(*square),
            whole(4, D),
            column(1),
        ]
        + [HBM] * (PIECES + len(down_pieces)),
        out_specs=[
            whole(*wide),
            whole(*wide),
            whole(rows, GROUP),
            whole(rows, GROUP),
            column(D // 2),
            column(D // 2),
            whole(D // 2, D),
            whole(D // 2, D),
            whole(8, D),
            column(1),
        ]
        + grad_specs,
        out_shape=[
            struct(wide, BF),
            struct(wide, F32),
            struct((rows, GROUP), BF),
            struct((rows, GROUP), BF),
            struct((D // 2, FF), BF),
            struct((D // 2, FF), BF),
            struct((D // 2, D), BF),
            struct((D // 2, D), BF),
            struct((8, D), F32),
            struct((1, FF), F32),
        ]
        + grad_shapes,
        scratch_shapes=[
            pltpu.VMEM(wide, BF),
            pltpu.VMEM(wide, F32),
            pltpu.VMEM(wide, F32),
            pltpu.VMEM((D, FF), BF),
            pltpu.VMEM((FF, D), BF),
            pltpu.VMEM(square, BF),
            pltpu.VMEM(staged, BF),
            pltpu.SemaphoreType.DMA(staged[:2]),
            pltpu.SemaphoreType.DMA((1 + STEPS, PIECES)),
            pltpu.SemaphoreType.DMA((sum(map(len, owners)),)),
        ],
        cost_estimate=QUICK,
        compiler_params=pltpu.CompilerParams(vmem_limit_bytes=48 * 1024 * 1024),
        name="mlp",
    )(
        places,
        (me if split_rows else me_down).reshape(1),
        normed,
        turned,
        residual,
        mixed,
        live,
        out_grad,
        order,
        vectors,
        b_up,
        *in_hbm(up_pieces),
        *in_hbm(down_pieces),
    )
    down = results[10:] if split_rows else pick(results[10], me, count)
    return tuple(results[:10]) + (tuple(down),)


def first_norm_kernel(
    grad_one_ref,
    grad_two_ref,
    tokens_ref,
    live_ref,
    gain_ref,
    order_ref,
    grad_residual_ref,
    mlp_sums_ref,
    grad_b_ref,
    tables_one_ref,
    tables_two_ref,
    *rest,
):
    pieces, (tokens_grad_ref, sums_ref, total, columns, weight, sem) = rest[:PIECES], rest[PIECES:]
    step = pl.program_id(0)

    def copies(index):
        group, block = index // 3, lax.rem(index, 3)
        return copy_rows(
            pieces,
            (pl.multiple_of(block * D + group * GROUP, 128), GROUP),
            weight,
            pl.multiple_of(index * GROUP, 128),
            sem.at[index],
        )

    @pl.when(step == 0)
    def _():
        for index in range(6):
            start_all(copies(jnp.int32(index)))
        total[...] = jnp.zeros_like(total)

    wait_all(copies(step))
    for group, grad_ref in ((0, grad_one_ref), (1, grad_two_ref)):

        @pl.when(step // 3 == group)
        def _():
            grad = grad_ref[...]
            at = pl.multiple_of(step * GROUP, 128)
            total[...] += dot_nt(grad, weight[:, pl.ds(at, GROUP)])
            columns[pl.ds(step, 1), :] = jnp.sum(grad.astype(F32), axis=0, keepdims=True)

    @pl.when(step == 5)
    def _():
        unit, rstd = normalise(tokens_ref[...].astype(F32))
        grad = natural_order(total[...], order_ref[...]) * live_ref[...]
        tokens_grad_ref[...] = (
            grad_residual_ref[...] + normalise_back(grad, unit, rstd, gain_ref[...])
        ).astype(BF)
        qkv = [
            columns[group * 3 + block : group * 3 + block + 1, :]
            for block in range(3)
            for group in range(GROUPS)
        ]
        vectors = [
            [jnp.sum(grad * unit, axis=0, keepdims=True)],
            [jnp.sum(grad, axis=0, keepdims=True)],
            qkv,
            [mlp_sums_ref[0:1, :]],
            [mlp_sums_ref[1:2, :]],
            [mlp_sums_ref[2:3, :]],
            [grad_b_ref[...]],
            [mlp_sums_ref[3:4, :]],
        ]
        at = 0
        for vector in vectors:
            for piece in vector:
                for lane in range(0, piece.shape[1], 128):
                    sums_ref[at : at + 1, :] = piece[:, lane : lane + 128]
                    at += 1
        sums_ref[at:TABLE_ROW, :] = jnp.zeros((TABLE_ROW - at, 128), F32)
        tables = (tables_one_ref[...] + tables_two_ref[...]) * (1.0 / SCALE)
        low = lax.broadcasted_iota(jnp.int32, (32, 128), 1) < 64
        sums_ref[TABLE_ROW:, :] = jnp.where(
            low,
            tables[64:96] + pltpu.roll(tables[:32], 64, 1),
            pltpu.roll(tables[96:], 64, 1) + tables[32:64],
        )


TABLE_ROW = 80
SUM_ROWS = TABLE_ROW + 32


def first_norm_back(grads, pieces, tokens, live, gain, order, grad_residual, sums, b_up, tables):
    rows = tokens.shape[0]
    first = lambda height: pl.BlockSpec((height, GROUP), lambda step: (0, jnp.minimum(step, 2)))
    second = lambda height: pl.BlockSpec((height, GROUP), lambda step: (0, jnp.maximum(step, 3) - 3))
    return pl.pallas_call(
        first_norm_kernel,
        grid=(6,),
        in_specs=[
            first(rows),
            second(rows),
            whole(rows, D),
            whole(rows, 1),
            whole(1, D),
            whole(D, D),
            whole(rows, D),
            whole(8, D),
            whole(1, FF),
            whole(128, 128),
            whole(128, 128),
        ]
        + [HBM] * PIECES,
        out_specs=[whole(rows, D), whole(SUM_ROWS, 128)],
        out_shape=[struct((rows, D), BF), struct((SUM_ROWS, 128), F32)],
        scratch_shapes=[
            pltpu.VMEM((rows, D), F32),
            pltpu.VMEM((8, GROUP), F32),
            pltpu.VMEM((D, 3 * D), BF),
            pltpu.SemaphoreType.DMA((6, PIECES)),
        ],
        cost_estimate=QUICK,
        compiler_params=pltpu.CompilerParams(vmem_limit_bytes=32 * 1024 * 1024),
        name="first_norm_back",
    )(*grads, tokens, live, gain, order, grad_residual, sums, b_up, *tables, *in_hbm(pieces))


def own_kernel(sizes, me_ref, sums_ref, *refs):
    outs, (table_h_ref, table_w_ref) = refs[:-2], refs[-2:]
    lane = lax.broadcasted_iota(jnp.int32, (1, 128), 1)
    row = 0
    for size, whole_size, out in zip(sizes, WHOLE_SIZES, outs):
        start = me_ref[0] * size
        at, shift = row + start // 128, lax.rem(start, 128)
        here = pltpu.roll(sums_ref[pl.ds(at, 1), :], lax.rem(128 - shift, 128), 1)
        there = pltpu.roll(sums_ref[pl.ds(at + 1, 1), :], lax.rem(128 - shift, 128), 1)
        out[...] = jnp.where(lane + shift < 128, here, there)[:, :size]
        row += whole_size // 128
    count = 2 * WIN - 1
    table_h_ref[...] = sums_ref[TABLE_ROW : TABLE_ROW + count, :HEAD_DIM]
    table_w_ref[...] = pltpu.roll(sums_ref[TABLE_ROW:, :], 64, 1)[:count, :HEAD_DIM]


WHOLE_SIZES = (D, D, 3 * D, D, D, D, FF, D)


def own_small(sums, me, sizes):
    table = struct((2 * WIN - 1, HEAD_DIM), F32)
    return pl.pallas_call(
        functools.partial(own_kernel, tuple(sizes)),
        in_specs=[
            pl.BlockSpec(memory_space=pltpu.SMEM),
            pl.BlockSpec(memory_space=pltpu.VMEM),
        ],
        out_specs=[pl.BlockSpec(memory_space=pltpu.VMEM)] * (len(sizes) + 2),
        out_shape=[struct((1, size), F32) for size in sizes] + [table, table],
        name="own_small",
    )(me.reshape(1), sums)


def hop(array, mask, count):
    return lax.ppermute(array, "fsdp", [(i, i ^ mask) for i in range(count)])


def hop_plan(count):
    far = count // 4
    return 2 * far, far, [1 << bit for bit in range(1, far.bit_length() - 1)]


def after(values, deps):
    if not deps:
        return list(values)
    return list(lax.optimization_barrier(tuple(values) + tuple(deps))[: len(values)])


def gather_stages(shard, count, pieces):
    farthest, far, middle = hop_plan(count)
    deps = yield
    (shard,) = after([shard], deps)
    got = hop(shard, farthest, count)
    deps = yield [shard]
    (got,) = after([got], deps)
    near = jnp.stack((shard, got))
    got = hop(near, far, count)
    deps = yield [near]
    (got,) = after([got], deps)
    stacks = [near, got]
    owners = [[0, farthest], [far, far ^ farthest]]
    for masks in zip(middle, middle[::-1]):
        got = [hop(stack, mask, count) for stack, mask in zip(stacks, masks)]
        deps = yield stacks
        if masks[0] != middle[-1]:
            got = after(got, deps)
            stacks = [jnp.concatenate(pair, axis=0) for pair in zip(stacks, got)]
            owners = [own + [o ^ m for o in own] for own, m in zip(owners, masks)]
    other = [hop(stack, 1, count) for stack in stacks]
    deps = yield stacks
    got = after(got, deps)
    late = [hop(stack, 1, count) for stack in got]
    for core, sides in ((0, (stacks, got)), (1, (other, late))):
        for stack, arrived, own, mask in zip(*sides, owners, masks):
            own = [o ^ core for o in own]
            pieces += [(stack, own), (arrived, [o ^ mask for o in own])]
    yield got


def start(stages):
    next(stages)
    return stages


def finish(stages):
    for _ in stages:
        pass


def place_kernel(owners, columns, me_ref, *refs):
    stacks, outs, sem = refs[: len(owners)], refs[len(owners) : -1], refs[-1]
    copies = []
    for stack, stack_owners in zip(stacks, owners):
        for index, mask in enumerate(stack_owners):
            owner = jnp.bitwise_xor(me_ref[0], mask)
            for out, lo, hi, to in columns:
                copies.append(
                    pltpu.make_async_copy(
                        stack.at[index, :, lo:hi],
                        outs[out].at[owner, :, to : to + hi - lo],
                        sem.at[len(copies)],
                    )
                )
                copies[-1].start()
    for copy in copies:
        copy.wait()


def place(pieces, columns, widths, me, count):
    stacks = [stack for stack, _ in pieces]
    rows = stacks[0].shape[1]
    outs = pl.pallas_call(
        functools.partial(place_kernel, tuple(tuple(o) for _, o in pieces), columns),
        in_specs=[pl.BlockSpec(memory_space=pltpu.SMEM)]
        + [pl.BlockSpec(memory_space=pl.ANY)] * len(stacks),
        out_specs=[pl.BlockSpec(memory_space=pltpu.VMEM)] * len(widths),
        out_shape=[jax.ShapeDtypeStruct((count, rows, width), BF) for width in widths],
        scratch_shapes=[pltpu.SemaphoreType.DMA((count * len(columns),))],
        cost_estimate=QUICK,
        compiler_params=pltpu.CompilerParams(vmem_limit_bytes=16 * 1024 * 1024),
        name="place",
    )(me.reshape(1), *stacks)
    return [out.reshape(count * rows, width) for out, width in zip(outs, widths)]


def sum_order(count):
    farthest, far, middle = hop_plan(count)
    order = []
    for masks, block in ((middle, [0, farthest]), (middle[::-1], [far, far ^ farthest])):
        for mask in masks:
            block = block + [owner ^ mask for owner in block]
        order += block
    return order + [owner ^ 1 for owner in order]


def order_matrix(me, count, rows):
    masks = np.repeat(np.array(sum_order(count), np.int32), rows)
    wanted = jnp.bitwise_xor(me, masks) * rows + np.tile(np.arange(rows, dtype=np.int32), count)
    features = lax.broadcasted_iota(jnp.int32, (count * rows, count * rows), 0)
    return (features == wanted[None, :]).astype(BF)


def pick_kernel(masks, me_ref, stack, kept, sent, sem):
    half = len(masks) // 2
    copies = []
    for index, mask in enumerate(masks):
        owner = jnp.bitwise_xor(me_ref[0], mask)
        out = kept if index < half else sent
        copies.append(
            pltpu.make_async_copy(stack.at[owner], out.at[index % half], sem.at[index])
        )
        copies[-1].start()
    for copy in copies:
        copy.wait()


def pick(array, me, count):
    stack = array.reshape(count, -1, array.shape[-1])
    half = jax.ShapeDtypeStruct((count // 2,) + stack.shape[1:], BF)
    return pl.pallas_call(
        functools.partial(pick_kernel, tuple(sum_order(count))),
        in_specs=[
            pl.BlockSpec(memory_space=pltpu.SMEM),
            pl.BlockSpec(memory_space=pl.ANY),
        ],
        out_specs=[pl.BlockSpec(memory_space=pltpu.VMEM)] * 2,
        out_shape=[half, half],
        scratch_shapes=[pltpu.SemaphoreType.DMA((count,))],
        cost_estimate=QUICK,
        compiler_params=pltpu.CompilerParams(vmem_limit_bytes=16 * 1024 * 1024),
        name="pick",
    )(me.reshape(1), stack)


def add_low(left, right):
    return (left.astype(F32) + right.astype(F32)).astype(BF)


def scatter_stages(parts, count, result):
    farthest, far, middle = hop_plan(count)
    blocks = count // 2
    half = blocks // 2
    shaped = [
        [side.reshape(blocks, -1, side.shape[-1]) for side in part] for part in parts
    ]
    deps = yield
    sent = after([sent for _, sent in shaped], deps)
    arrived = [hop(side, 1, count) for side in sent]
    deps = yield sent
    arrived = after(arrived, deps)
    pairs = [(kept, got) for (kept, _), got in zip(shaped, arrived)]

    def added(pairs, lo, hi):
        sums = [add_low(kept[lo:hi], got[lo:hi]) for kept, got in pairs]
        return sums[0] if len(sums) == 1 else jnp.concatenate(sums, axis=-1)

    sides = [(pairs, 0), (pairs, half)]
    size = half
    for masks in zip(middle[::-1], middle):
        size //= 2
        sends = [added(p, at + size, at + 2 * size) for p, at in sides]
        got = [hop(send, mask, count) for send, mask in zip(sends, masks)]
        kept = [added(p, at, at + size) for p, at in sides]
        deps = yield sends
        got = after(got, deps)
        sides = [([pair], 0) for pair in zip(kept, got)]
    (near, _), (back, _) = sides
    send = added(back, 0, 2)
    got = hop(send, far, count)
    kept = added(near, 0, 2)
    deps = yield [send]
    (got,) = after([got], deps)
    send = add_low(kept[1], got[1])
    arrived = hop(send, farthest, count)
    deps = yield [send]
    (arrived,) = after([arrived], deps)
    total = kept[0].astype(F32) + got[0].astype(F32) + arrived.astype(F32)
    result.append(total)
    yield [total]


def sum_stages(array, count, result):
    mask = 1
    deps = yield
    while mask < count:
        (array,) = after([array], deps)
        got = hop(array, mask, count)
        deps = yield [array]
        (got,) = after([got], deps)
        array = array + got
        mask *= 2
    result.append(array)
    yield [array]


def per_device(
    tokens,
    window_pos,
    norm1_gain,
    norm1_bias,
    qkv_weight,
    qkv_bias,
    rel_pos_h,
    rel_pos_w,
    proj_weight,
    proj_bias,
    norm2_gain,
    norm2_bias,
    lin1_weight,
    lin1_bias,
    lin2_weight,
    lin2_bias,
    out_grad,
):
    vectors = (
        norm1_gain,
        norm1_bias,
        qkv_bias,
        proj_bias,
        norm2_gain,
        norm2_bias,
        lin1_bias,
        lin2_bias,
    )
    sizes = [v.shape[0] for v in vectors]
    used = sum(sizes)
    shard_rows = qkv_weight.shape[0]
    count = lax.axis_size("fsdp")
    me = lax.axis_index("fsdp")

    packed = lax.optimization_barrier(jnp.concatenate(vectors))
    packed = jnp.pad(packed, (0, shard_rows * 128 - used)).reshape(shard_rows, 128)
    first_pieces, second_pieces, third_pieces = [], [], []
    first = start(
        gather_stages(jnp.concatenate((qkv_weight, packed), axis=1).astype(BF), count, first_pieces)
    )
    second = start(
        gather_stages(
            jnp.concatenate((proj_weight, lin1_weight), axis=1).astype(BF), count, second_pieces
        )
    )
    third = start(gather_stages(lin2_weight.astype(BF), count, third_pieces))
    middle = len(hop_plan(count)[2])
    first.send(None)
    sent = first.send(None)
    second.send(sent)
    for _ in range(middle):
        sent = first.send(sent)
        sent = second.send(sent)
    sent = first.send(sent)
    sent = sent + third.send(sent)
    sent = first.send(sent)
    sent = sent + third.send(sent)

    (small,) = place(
        [(stack[:, :, 3 * D :], own) for stack, own in first_pieces], ((0, 0, 128, 0),), (128,), me, count
    )
    small = small.reshape(count, shard_rows * 128)[:, :used].astype(F32)
    edges = np.cumsum([0] + sizes)
    gain_one, bias_one, b_qkv, b_proj, gain_two, bias_two, b_up, b_down = (
        small[:, lo:hi].reshape(-1) for lo, hi in zip(edges[:-1], edges[1:])
    )
    flat = lambda pieces: [stack.reshape(-1, stack.shape[-1]) for stack, _ in pieces]
    first_pieces = flat(first_pieces)
    order = order_matrix(me, count, shard_rows)
    onehot, shift = window_constants()
    onehot = jnp.asarray(onehot, BF)
    shift = jnp.asarray(shift)
    table = table_lanes(rel_pos_h, rel_pos_w)
    live = slot_mask(window_pos)

    ordered_one, *qkv = front(
        tokens, live, order, jnp.stack((gain_one, bias_one)), b_qkv.reshape(1, -1), first_pieces
    )
    sent = second.send(sent + [ordered_one])
    sent = sent + third.send(sent)
    (qkv[0],) = after([qkv[0]], sent)
    attended = [attention(qkv[0], table, onehot, shift)]
    sent = second.send([attended[0][0]])
    sent = sent + third.send(sent)
    (qkv[1],) = after([qkv[1]], sent)
    attended.append(attention(qkv[1], table, onehot, shift))
    sent = third.send([attended[1][0]])
    finish(second)
    second_pieces = flat(second_pieces)
    mixed = [m for m, _ in attended]
    (mixed[0],) = after([mixed[0]], sent)
    vectors = jnp.stack((b_proj, gain_two, bias_two, b_down))
    residual, normed_two, turned_two, ordered_mixed = project(
        tokens, mixed, order, vectors, second_pieces
    )
    third.send([residual])
    finish(third)

    own_down, own_up, own_first, own_second, all_small = [], [], [], [], []
    (
        output,
        grad_residual,
        grad_one,
        grad_two,
        kept_up,
        sent_up,
        kept_proj,
        sent_proj,
        mlp_sums,
        grad_b_up,
        down_parts,
    ) = mlp(
        me,
        count,
        normed_two,
        turned_two,
        residual,
        ordered_mixed,
        live,
        out_grad,
        order,
        vectors,
        b_up.reshape(1, FF),
        second_pieces,
        third_pieces,
    )
    down = start(scatter_stages([down_parts], count, own_down))
    up = start(scatter_stages([(kept_up, sent_up)], count, own_up))
    sent = down.send(None)
    sent = sent + up.send(sent)
    (grad_one,) = after([grad_one], sent)
    back = [attention_back(qkv[0], grad_one, attended[0][1], table, onehot, shift)]
    sent = down.send([back[0][0]])

    def qkv_part(grad_qkv):
        sent = dot_tn(ordered_one[:, D // 2 :], grad_qkv).astype(BF)
        return dot_tn(ordered_one[:, : D // 2], grad_qkv).astype(BF), sent

    first_sum = start(
        scatter_stages([qkv_part(back[0][0]), (kept_proj, sent_proj)], count, own_first)
    )
    sent = sent + first_sum.send(sent)
    (grad_two,) = after([grad_two], sent)
    back.append(attention_back(qkv[1], grad_two, attended[1][1], table, onehot, shift))
    sent = up.send([back[1][0]])
    second_sum = start(scatter_stages([qkv_part(back[1][0])], count, own_second))
    sent = sent + second_sum.send(sent)
    (grad_qkv,) = after([back[1][0]], sent)
    tokens_grad, small_sums = first_norm_back(
        (back[0][0], grad_qkv),
        first_pieces,
        tokens,
        live,
        gain_one.reshape(1, D),
        order,
        grad_residual,
        mlp_sums,
        grad_b_up,
        (back[0][1], back[1][1]),
    )
    sent = down.send([small_sums])
    small_stages = start(sum_stages(small_sums, count, all_small))
    sent = small_stages.send(sent)
    sent = first_sum.send(sent)
    sent = down.send(sent)
    sent = small_stages.send(sent)
    sent = up.send(sent)
    sent = down.send(sent)
    sent = second_sum.send(sent)
    sent = small_stages.send(sent)
    sent = up.send(sent)
    sent = first_sum.send(sent)
    sent = small_stages.send(sent)
    sent = up.send(sent)
    sent = second_sum.send(sent)
    sent = first_sum.send(sent)
    sent = small_stages.send(sent)
    sent = second_sum.send(sent)
    sent = first_sum.send(sent)
    sent = second_sum.send(sent)
    for stages in (down, up, first_sum, second_sum, small_stages):
        finish(stages)
    own_qkv = jnp.stack(
        [
            own.reshape(shard_rows, 3, GROUP)
            for own in (own_first[0][:, : 3 * GROUP], own_second[0])
        ],
        axis=2,
    ).reshape(shard_rows, 3 * D)
    own_proj = own_first[0][:, 3 * GROUP :]
    *owned, table_h, table_w = own_small(all_small[0], me, sizes)
    owned = [vector.reshape(-1) for vector in owned]

    return (
        output,
        tokens_grad,
        owned[0],
        owned[1],
        own_qkv,
        owned[2],
        table_h,
        table_w,
        own_proj,
        owned[3],
        owned[4],
        owned[5],
        own_up[0],
        owned[6],
        own_down[0],
        owned[7],
    )


def solution(mesh):
    rows = P("fsdp", None)
    line = P("fsdp")
    return jax.shard_map(
        per_device,
        mesh=mesh,
        in_specs=(
            rows,
            line,
            line,
            line,
            rows,
            line,
            P(),
            P(),
            rows,
            line,
            line,
            line,
            rows,
            line,
            rows,
            line,
            rows,
        ),
        out_specs=(
            rows,
            rows,
            line,
            line,
            rows,
            line,
            P(),
            P(),
            rows,
            line,
            line,
            line,
            rows,
            line,
            rows,
            line,
        ),
        check_vma=False,
    )
```

```python
import functools

import jax
import jax.numpy as jnp
import numpy as np
from jax import lax
from jax.experimental import pallas as pl
from jax.experimental.pallas import tpu as pltpu
from jax.sharding import PartitionSpec as P

D = 768
HEADS = 12
HEAD_DIM = 64
FF = 3072
WIN = 14
NWS = 5
EDGE = 8
LENGTH = WIN * WIN
PAIRS = HEADS // 2
BLOCK = 200
SCALE = HEAD_DIM ** (-0.5)
EPS = 1e-06
ATTENTION_VMEM = 60 * 1024 * 1024
KERNEL_VMEM = 60 * 1024 * 1024
QUICK = pl.CostEstimate(flops=1, bytes_accessed=1, transcendentals=0)
LONG = pl.CostEstimate(flops=100_000_000_000, bytes_accessed=1, transcendentals=0)
LANES = 256
BF = jnp.bfloat16
F32 = jnp.float32


def window_constants():
    onehot = np.zeros((2, BLOCK, 128), np.float32)
    shift = np.zeros((2, 16, LANES), np.int32)
    for win in range(2):
        for row in range(BLOCK):
            slot = row - 4 * win
            if not 0 <= slot < LENGTH:
                onehot[win, row, 63] = onehot[win, row, 127] = -1e30
                continue
            y, x = divmod(slot, WIN)
            for base in (0, 64):
                for lane in (0, 16):
                    onehot[win, row, base + lane + WIN - 1 - y] = 1.0
                    onehot[win, row, base + 32 + lane + WIN - 1 - x] = 1.0
            shift[win, :8, row] = y
            shift[win, 8:, row] = x
    return onehot, shift


def table_lanes(rel_pos_h, rel_pos_w):
    flip = jnp.concatenate(
        (
            jnp.pad(rel_pos_h, ((0, 5), (0, 0))),
            jnp.pad(rel_pos_w, ((0, 5), (0, 0))),
        ),
        axis=0,
    ).astype(BF) * BF(1.0 / SCALE)
    nothing = jnp.zeros_like(flip)
    return jnp.concatenate(
        (jnp.concatenate((nothing, flip), axis=1), jnp.concatenate((flip, nothing), axis=1)), axis=0
    )


def dot_nn(a, b):
    return jnp.dot(a, b, preferred_element_type=F32)


def dot_nt(a, b):
    return lax.dot_general(a, b, (((1,), (1,)), ((), ())), preferred_element_type=F32)


def dot_tn(a, b):
    return lax.dot_general(a, b, (((0,), (0,)), ((), ())), preferred_element_type=F32)


def low_half():
    return lax.broadcasted_iota(jnp.int32, (BLOCK, 128), 1) < 64


def row_valid(win):
    row = lax.broadcasted_iota(jnp.int32, (BLOCK, 128), 0)
    return row < LENGTH if win == 0 else row >= BLOCK - LENGTH


def merge_windows(first, second):
    return jnp.concatenate((first[:192], first[192:] + second[:8], second[8:]), axis=0)


def pad_rows(values):
    return jnp.concatenate((values, jnp.zeros((LANES - BLOCK, 128), F32)), axis=0)


def bit_masks(shift, rows):
    shift = jnp.broadcast_to(shift[:1], (rows, LANES))
    return [(shift & (1 << bit)) != 0 for bit in range(4)]


def skew(values, masks):
    values = jnp.where(masks[3], values[8:], values[:24])
    values = jnp.where(masks[2], pltpu.roll(values, 20, 0), values)
    values = jnp.where(masks[1], pltpu.roll(values, 22, 0), values)[:16]
    return jnp.where(masks[0][:16], pltpu.roll(values, 15, 0), values)


def unskew(values, masks):
    nothing = jnp.zeros((8, LANES), F32)
    values = jnp.concatenate((values, nothing), axis=0)
    for bit in range(3):
        values = jnp.where(masks[bit], pltpu.roll(values, 1 << bit, 0), values)
    return jnp.concatenate(
        (
            jnp.where(masks[3][:8], 0.0, values[:8]),
            jnp.where(masks[3][:16], values[:16], values[8:]),
            jnp.where(masks[3][:8], values[16:], 0.0),
        ),
        axis=0,
    )


def attn_fwd_kernel(q_ref, k_ref, v_ref, table_ref, onehot_ref, shift_ref, mixed_ref, probs_ref):
    low = low_half()
    last = lax.broadcasted_iota(jnp.int32, (16, LANES), 0) == 15
    mixed = []
    for win in range(2):
        rows = pl.ds(192 * win, BLOCK)
        queries = pad_rows(q_ref[rows, :].astype(F32) * SCALE).T
        k = k_ref[rows, :].astype(F32)
        v = v_ref[rows, :]
        rel = dot_nn(table_ref[...], queries.astype(BF))
        onehot = onehot_ref[win].astype(F32)
        by_row = bit_masks(shift_ref[win, :8], 24)
        by_col = bit_masks(shift_ref[win, 8:], 24)
        halves = []
        for head in range(2):
            base = 64 if head == 0 else 0
            from_row = skew(rel[base : base + 32], by_row)
            from_col = skew(rel[base + 32 : base + 64], by_col)
            row_top = from_row.astype(BF).astype(F32)
            col_top = from_col.astype(BF).astype(F32)
            extra = (row_top, from_row - row_top, col_top, jnp.where(last, 1.0, from_col - col_top))
            if head == 0:
                left = jnp.concatenate((queries[:64],) + extra, axis=0).astype(BF)
                right = jnp.where(low, k, onehot).astype(BF)
            else:
                left = jnp.concatenate(extra + (queries[64:],), axis=0).astype(BF)
                right = jnp.where(low, onehot, k).astype(BF)
            scores = dot_nn(right, left)
            expon = jnp.exp(scores - jnp.max(scores, axis=0, keepdims=True))
            probs = expon * (1.0 / jnp.sum(expon, axis=0, keepdims=True))
            probs_ref[0, 2 * win + head] = probs
            halves.append(dot_tn(v, probs.astype(BF)))
        both = jnp.concatenate((halves[0][:HEAD_DIM], halves[1][HEAD_DIM:]), axis=0).T[:BLOCK]
        mixed.append(jnp.where(row_valid(win), both, 0.0))
    mixed_ref[...] = merge_windows(*mixed).astype(BF)


def attn_bwd_kernel(
    q_ref,
    k_ref,
    v_ref,
    grad_ref,
    probs_ref,
    table_ref,
    onehot_ref,
    shift_ref,
    grad_qkv_ref,
    table_grad_ref,
):
    pair = pl.program_id(0)
    low = low_half()

    @pl.when(pair == 0)
    def _():
        table_grad_ref[...] = jnp.zeros_like(table_grad_ref)

    parts = ([], [], [])
    table_total = jnp.zeros((128, 128), F32)
    for win in range(2):
        rows = pl.ds(192 * win, BLOCK)
        q = pad_rows(q_ref[rows, :].astype(F32) * SCALE).astype(BF)
        k = k_ref[rows, :].astype(F32)
        v = v_ref[rows, :]
        grad = pad_rows(jnp.where(row_valid(win), grad_ref[rows, :].astype(F32), 0.0))
        grad_low = grad.astype(BF)
        wide_low = lax.broadcasted_iota(jnp.int32, (LANES, 128), 1) < 64
        onehot = onehot_ref[win].astype(F32)
        by_row = bit_masks(shift_ref[win, :8], 24)
        by_col = bit_masks(shift_ref[win, 8:], 24)
        by_query, by_key, by_value, rel = [], [], [], []
        for head in range(2):
            if head == 0:
                right = jnp.where(low, k, onehot).astype(BF)
                grad_own = jnp.where(wide_low, grad, 0.0).astype(BF)
            else:
                right = jnp.where(low, onehot, k).astype(BF)
                grad_own = jnp.where(wide_low, 0.0, grad).astype(BF)
            probs = probs_ref[0, 2 * win + head]
            grad_probs = dot_nt(v, grad_own)
            row_dot = jnp.sum(probs * grad_probs, axis=0, keepdims=True)
            grad_scores = (probs * (grad_probs - row_dot)).astype(BF)
            by_value.append(dot_nn(probs.astype(BF), grad_low))
            by_key.append(dot_nn(grad_scores, q))
            back = dot_tn(right, grad_scores)
            own, base = (back[:64], 64) if head == 0 else (back[64:], 0)
            by_query.append(own)
            rel.append(unskew(back[base : base + 16], by_row))
            rel.append(unskew(back[base + 32 : base + 48], by_col))
        rel = jnp.concatenate((rel[2], rel[3], rel[0], rel[1]), axis=0)
        rel_top = rel.astype(BF)
        rel_rest = (rel - rel_top.astype(F32)).astype(BF)
        table = table_ref[...]
        from_rel = dot_tn(table, rel_top) + dot_tn(table, rel_rest)
        table_total += dot_nn(rel_top, q) + dot_nn(rel_rest, q)
        parts[0].append((jnp.concatenate(by_query, axis=0) + from_rel).T[:BLOCK] * SCALE)
        parts[1].append(jnp.where(low, by_key[0], by_key[1]))
        parts[2].append(jnp.where(low, by_value[0], by_value[1]))
    for block in range(3):
        at = pl.multiple_of(block * D + pair * 128, 128)
        grad_qkv_ref[:, pl.ds(at, 128)] = merge_windows(*parts[block]).astype(BF)
    table_grad_ref[...] += table_total


def attention_specs(rows):
    column = lambda block: pl.BlockSpec((rows, 128), lambda pair: (0, block * PAIRS + pair))
    whole = lambda *shape: pl.BlockSpec(shape, lambda pair: (0,) * len(shape))
    return (
        [column(0), column(1), column(2)],
        [whole(128, 128), whole(2, BLOCK, 128), whole(2, 16, LANES)],
        pl.BlockSpec((1, 4, BLOCK, LANES), lambda pair: (pair, 0, 0, 0)),
        whole,
    )


def attention(qkv, table, onehot, shift):
    rows = qkv.shape[0]
    columns, constants, probs_spec, _ = attention_specs(rows)
    return pl.pallas_call(
        attn_fwd_kernel,
        grid=(PAIRS,),
        in_specs=columns + constants,
        out_specs=[pl.BlockSpec((rows, 128), lambda pair: (0, pair)), probs_spec],
        out_shape=[
            jax.ShapeDtypeStruct((rows, D), BF),
            jax.ShapeDtypeStruct((PAIRS, 4, BLOCK, LANES), F32),
        ],
        cost_estimate=QUICK,
        compiler_params=pltpu.CompilerParams(vmem_limit_bytes=ATTENTION_VMEM),
        name="attention",
    )(qkv, qkv, qkv, table, onehot, shift)


def attention_back(qkv, grad_mixed, probs, table, onehot, shift):
    rows = qkv.shape[0]
    columns, constants, probs_spec, whole = attention_specs(rows)
    return pl.pallas_call(
        attn_bwd_kernel,
        grid=(PAIRS,),
        in_specs=columns + [pl.BlockSpec((rows, 128), lambda pair: (0, pair)), probs_spec]
        + constants,
        out_specs=[whole(rows, 3 * D), whole(128, 128)],
        out_shape=[
            jax.ShapeDtypeStruct((rows, 3 * D), BF),
            jax.ShapeDtypeStruct((128, 128), F32),
        ],
        cost_estimate=QUICK,
        compiler_params=pltpu.CompilerParams(vmem_limit_bytes=ATTENTION_VMEM),
        name="attention_back",
    )(qkv, qkv, qkv, grad_mixed, probs, table, onehot, shift)


def slot_mask(window_pos):
    row_win = window_pos // NWS
    col_win = window_pos % NWS
    rows_ok = jnp.where(row_win == NWS - 1, EDGE, WIN)
    cols_ok = jnp.where(col_win == NWS - 1, EDGE, WIN)
    positions = jnp.arange(WIN, dtype=jnp.int32)
    inside = (positions[None, :, None] < rows_ok[:, None, None]) & (
        positions[None, None, :] < cols_ok[:, None, None]
    )
    return inside.reshape(-1, 1).astype(F32)


def normalise(values):
    centred = values - jnp.mean(values, axis=-1, keepdims=True)
    rstd = lax.rsqrt(jnp.mean(centred * centred, axis=-1, keepdims=True) + EPS)
    return centred * rstd, rstd


def normalise_back(grad, hat, rstd, gain):
    grad_hat = grad * gain
    return rstd * (
        grad_hat
        - jnp.mean(grad_hat, axis=-1, keepdims=True)
        - hat * jnp.mean(grad_hat * hat, axis=-1, keepdims=True)
    )


def normal_cdf(values):
    return 0.5 * (1.0 + lax.erf(values * np.float32(np.sqrt(0.5))))


def normal_pdf(values):
    return np.float32(1.0 / np.sqrt(2.0 * np.pi)) * jnp.exp(-0.5 * values * values)


def copy_rows(pieces, columns, out, to, sems):
    rows = pieces[0].shape[0]
    lo, width = columns
    return [
        pltpu.make_async_copy(
            piece.at[:, pl.ds(lo, width)],
            out.at[index * rows : (index + 1) * rows, pl.ds(to, width)],
            sems.at[index],
        )
        for index, piece in enumerate(pieces)
    ]


def start_all(copies):
    for copy in copies:
        copy.start()


def wait_all(copies):
    for copy in copies:
        copy.wait()


def front_kernel(tokens_ref, live_ref, order_ref, rows_ref, b_qkv_ref, *rest):
    pieces, (turned_ref, qkv_ref, weight, sem) = rest[:PIECES], rest[PIECES:]
    copies = [copy_rows(pieces, (block * D, D), weight, block * D, sem.at[block]) for block in range(3)]
    for block in copies:
        start_all(block)
    unit, _ = normalise(tokens_ref[...].astype(F32))
    normed = ((unit * rows_ref[0:1, :] + rows_ref[1:2, :]) * live_ref[...]).astype(BF)
    turned = dot_nn(normed, order_ref[...])
    normed = turned.astype(BF)
    turned_ref[...] = turned.T.astype(BF)
    for block in range(3):
        wait_all(copies[block])
        at = block * D
        values = dot_nn(normed, weight[:, at : at + D]) + b_qkv_ref[:, at : at + D]
        qkv_ref[:, at : at + D] = values.astype(BF)


PIECES = 2
HBM = pl.BlockSpec(memory_space=pl.ANY)
VMEM = pl.BlockSpec(memory_space=pltpu.VMEM)
SMEM = pl.BlockSpec(memory_space=pltpu.SMEM)


def front(tokens, live, order, vectors, b_qkv, pieces):
    rows = tokens.shape[0]
    return pl.pallas_call(
        front_kernel,
        in_specs=[VMEM] * 5 + [HBM] * PIECES,
        out_specs=[VMEM] * 2,
        out_shape=[struct((D, rows), BF), struct((rows, 3 * D), BF)],
        scratch_shapes=[pltpu.VMEM((D, 3 * D), BF), pltpu.SemaphoreType.DMA((3, PIECES))],
        cost_estimate=QUICK,
        compiler_params=pltpu.CompilerParams(vmem_limit_bytes=KERNEL_VMEM),
        name="front",
    )(tokens, live, order, vectors, b_qkv, *pieces)


def proj_kernel(tokens_ref, values_ref, order_ref, rows_ref, *rest):
    pieces, (residual_ref, normed_ref, turned_ref, mixed_ref, w_proj, sem) = rest[:PIECES], rest[PIECES:]
    b_proj, gain, bias = (rows_ref[i : i + 1, :] for i in range(3))
    copies = copy_rows(pieces, (3 * D, D), w_proj, 0, sem)
    start_all(copies)
    mixed = dot_nn(values_ref[...], order_ref[...]).astype(BF)
    mixed_ref[...] = mixed
    wait_all(copies)
    values = tokens_ref[...].astype(F32) + dot_nn(mixed, w_proj[...]) + b_proj
    residual_ref[...] = values
    low = (normalise(values)[0] * gain + bias).astype(BF)
    low = dot_nn(low, order_ref[...])
    normed_ref[...] = low.astype(BF)
    turned_ref[...] = low.T.astype(BF)


def down_copies(pieces, owners, me_ref, weight, sems):
    copies = []
    for piece, masks in zip(pieces, owners):
        rows = piece.shape[0] // len(masks)
        for index, mask in enumerate(masks):
            to = jnp.bitwise_xor(me_ref[0], mask) * rows
            copies.append(
                pltpu.make_async_copy(
                    piece.at[index * rows : (index + 1) * rows],
                    weight.at[pl.ds(pl.multiple_of(to, rows), rows)],
                    sems.at[len(copies)],
                )
            )
    return copies


def mlp_kernel(split_rows, owners, place_ref, me_ref, *rest):
    normed_ref, turned_ref, live_ref, out_grad_ref, residual_ref, rows_ref, b_up_ref, *rest = rest
    up_pieces, rest = rest[:PIECES], rest[PIECES:]
    down_pieces, rest = rest[: len(owners)], rest[len(owners) :]
    output_ref, grad_normed_ref, kept_ref, sent_ref, grad_b_ref, *rest = rest
    if split_rows:
        kept_down_ref, sent_down_ref, *rest = rest
    else:
        grad_down_ref, *rest = rest
    branch, total, w_up, w_down, staged, sem, up_sem, down_sem = rest
    step = pl.program_id(0)
    half = D // 2

    def up_copies(index):
        return copy_rows(up_pieces, (index * TILE, TILE), w_up, index * TILE, up_sem.at[index])

    @pl.when(step == 0)
    def _():
        start_all(up_copies(0))
        start_all(down_copies(down_pieces, owners, me_ref, w_down, down_sem))
        for index in range(1, STEPS):
            start_all(up_copies(index))
        branch[...] = (out_grad_ref[...].astype(F32) * live_ref[...]).astype(BF)
        grad_normed_ref[...] = jnp.zeros_like(grad_normed_ref)
        total[...] = residual_ref[...] + rows_ref[3:4, :]

    wait_all(up_copies(step))
    at = pl.multiple_of(step * TILE, TILE)
    weight_up = w_up[:, pl.ds(at, TILE)]
    hidden = dot_nn(normed_ref[...], weight_up) + b_up_ref[...]
    cdf = normal_cdf(hidden)
    active = (hidden * cdf).astype(BF)
    slope = cdf + hidden * normal_pdf(hidden)
    grad_down = dot_tn(active, branch[...]).astype(BF)

    @pl.when(step == 0)
    def _():
        wait_all(down_copies(down_pieces, owners, me_ref, w_down, down_sem))

    weight_down = w_down[pl.ds(at, TILE), :]
    grad_active = dot_nt(branch[...], weight_down)
    total[...] += dot_nn(active, weight_down)
    grad_hidden = (grad_active * slope).astype(BF)
    sent_ref[...] = dot_nn(turned_ref[half:, :], grad_hidden).astype(BF)
    kept_ref[...] = dot_nn(turned_ref[:half, :], grad_hidden).astype(BF)
    grad_normed_ref[...] += dot_nt(grad_hidden, weight_up)
    grad_b_ref[...] = jnp.sum(grad_hidden.astype(F32), axis=0, keepdims=True)

    @pl.when(step == STEPS - 1)
    def _():
        output_ref[...] = (total[...] * live_ref[...]).astype(BF)

    if not split_rows:
        grad_down_ref[...] = grad_down
        return

    slot = lax.rem(step, 2)
    blocks = staged.shape[1]

    def copy(slot, block, out, to):
        return pltpu.make_async_copy(staged.at[slot, block], out.at[to], sem.at[slot, block])

    @pl.when(step >= 2)
    def _():
        for block in range(blocks):
            copy(slot, block, kept_down_ref, 0).wait()

    staged[slot] = grad_down.reshape(blocks, split_rows, D)
    places = kept_down_ref.shape[0]
    for block in range(blocks):
        to = place_ref[step * blocks + block]

        @pl.when(to < places)
        def _():
            copy(slot, block, kept_down_ref, to).start()

        @pl.when(to >= places)
        def _():
            copy(slot, block, sent_down_ref, to - places).start()

    @pl.when(step == STEPS - 1)
    def _():
        for last_slot in range(2):
            for block in range(blocks):
                copy(last_slot, block, kept_down_ref, 0).wait()


def second_norm_kernel(
    grad_normed_ref, residual_ref, mixed_ref, live_ref, out_grad_ref, order_ref, rows_ref, *rest
):
    pieces, rest = rest[:PIECES], rest[PIECES:]
    grad_residual_ref, grad_mixed_ref, *rest = rest
    kept_proj_ref, sent_proj_ref, sums_ref, w_proj, sem = rest
    half = D // 2
    copies = copy_rows(pieces, (3 * D, D), w_proj, 0, sem)
    start_all(copies)
    grad = natural_order(grad_normed_ref[...], order_ref[...])
    unit, rstd = normalise(residual_ref[...])
    grad_out = out_grad_ref[...].astype(F32) * live_ref[...]
    grad_residual = grad_out + normalise_back(grad, unit, rstd, rows_ref[1:2, :])
    grad_residual_ref[...] = grad_residual
    grad_attn = grad_residual.astype(BF)
    wait_all(copies)
    grad_mixed = dot_nt(grad_attn, w_proj[...]).astype(BF)
    grad_mixed_ref[...] = dot_nt(grad_mixed, order_ref[...]).astype(BF)
    sent_proj_ref[...] = dot_tn(mixed_ref[:, half:], grad_attn).astype(BF)
    kept_proj_ref[...] = dot_tn(mixed_ref[:, :half], grad_attn).astype(BF)
    sums_ref[0:1, :] = jnp.sum(grad_attn.astype(F32), axis=0, keepdims=True)
    sums_ref[1:2, :] = jnp.sum(grad * unit, axis=0, keepdims=True)
    sums_ref[2:3, :] = jnp.sum(grad, axis=0, keepdims=True)
    sums_ref[3:4, :] = jnp.sum(grad_out.astype(BF).astype(F32), axis=0, keepdims=True)
    sums_ref[4:, :] = jnp.zeros((4, D), F32)


def natural_order(values, order):
    top = values.astype(BF)
    rest = (values - top.astype(F32)).astype(BF)
    return dot_nt(top, order) + dot_nt(rest, order)


TILE = 768
STEPS = FF // TILE


def whole(*shape):
    return pl.BlockSpec(shape, lambda step: (0,) * len(shape))


def struct(shape, dtype):
    return jax.ShapeDtypeStruct(shape, dtype)


def project(tokens, mixed, order, vectors, pieces):
    rows = tokens.shape[0]
    return pl.pallas_call(
        proj_kernel,
        in_specs=[VMEM] * 4 + [HBM] * PIECES,
        out_specs=[VMEM] * 4,
        out_shape=[
            struct((rows, D), F32),
            struct((rows, D), BF),
            struct((D, rows), BF),
            struct((rows, D), BF),
        ],
        scratch_shapes=[pltpu.VMEM((D, D), BF), pltpu.SemaphoreType.DMA((PIECES,))],
        cost_estimate=QUICK,
        compiler_params=pltpu.CompilerParams(vmem_limit_bytes=KERNEL_VMEM),
        name="project",
    )(tokens, mixed, order, vectors, *pieces)


def placed_down(pieces, me, count):
    if FF // count % 16:
        return place(pieces, ((0, 0, D, 0),), (D,), me, count), ((0,),), jnp.zeros((1,), jnp.int32)
    owners = tuple(tuple(masks) for _, masks in pieces)
    return [stack.reshape(-1, D) for stack, _ in pieces], owners, me.reshape(1)


def mlp(
    me, count, places, normed, turned, live, out_grad, residual, vectors, b_up, up_pieces, down
):
    rows = normed.shape[0]
    block_rows = FF // count
    split_rows = block_rows if block_rows % 16 == 0 else 0
    down_pieces, owners, me_down = down
    column = lambda height: pl.BlockSpec((height, TILE), lambda step: (0, step))
    if split_rows:
        half = struct((count // 2, block_rows, D), BF)
        grad_specs, grad_shapes = [HBM] * 2, [half, half]
        staged = (2, TILE // block_rows, block_rows, D)
    else:
        grad_specs = [pl.BlockSpec((TILE, D), lambda step: (step, 0))]
        grad_shapes = [struct((FF, D), BF)]
        staged = (2, 1, 16, 128)
    wide = (rows, D)
    results = pl.pallas_call(
        functools.partial(mlp_kernel, split_rows, owners),
        grid=(STEPS,),
        in_specs=[SMEM, SMEM, whole(*wide), whole(D, rows), whole(rows, 1)]
        + [whole(*wide), whole(*wide), whole(4, D), column(1)]
        + [HBM] * (len(up_pieces) + len(down_pieces)),
        out_specs=[whole(*wide), whole(*wide), column(D // 2), column(D // 2), column(1)]
        + grad_specs,
        out_shape=[
            struct(wide, BF),
            struct(wide, F32),
            struct((D // 2, FF), BF),
            struct((D // 2, FF), BF),
            struct((1, FF), F32),
        ]
        + grad_shapes,
        scratch_shapes=[
            pltpu.VMEM(wide, BF),
            pltpu.VMEM(wide, F32),
            pltpu.VMEM((D, FF), BF),
            pltpu.VMEM((FF, D), BF),
            pltpu.VMEM(staged, BF),
            pltpu.SemaphoreType.DMA(staged[:2]),
            pltpu.SemaphoreType.DMA((STEPS, PIECES)),
            pltpu.SemaphoreType.DMA((sum(map(len, owners)),)),
        ],
        cost_estimate=QUICK,
        compiler_params=pltpu.CompilerParams(vmem_limit_bytes=KERNEL_VMEM),
        name="mlp",
    )(
        places,
        me_down,
        normed,
        turned,
        live,
        out_grad,
        residual,
        vectors,
        b_up,
        *up_pieces,
        *down_pieces,
    )
    parts = results[5:] if split_rows else pick(results[5], me, count)
    return tuple(results[:5]) + (tuple(parts),)


def second_norm_back(grad_normed, residual, mixed, live, out_grad, order, vectors, pieces):
    rows = residual.shape[0]
    return pl.pallas_call(
        second_norm_kernel,
        in_specs=[VMEM] * 7 + [HBM] * PIECES,
        out_specs=[VMEM] * 5,
        out_shape=[
            struct((rows, D), F32),
            struct((rows, D), BF),
            struct((D // 2, D), BF),
            struct((D // 2, D), BF),
            struct((8, D), F32),
        ],
        scratch_shapes=[pltpu.VMEM((D, D), BF), pltpu.SemaphoreType.DMA((PIECES,))],
        cost_estimate=QUICK,
        compiler_params=pltpu.CompilerParams(vmem_limit_bytes=KERNEL_VMEM),
        name="second_norm_back",
    )(grad_normed, residual, mixed, live, out_grad, order, vectors, *pieces)


def marker_kernel(value_ref, out_ref):
    out_ref[...] = value_ref[...]


def marker(value):
    return pl.pallas_call(
        marker_kernel,
        in_specs=[VMEM],
        out_specs=VMEM,
        out_shape=struct(value.shape, value.dtype),
        cost_estimate=LONG,
        name="marker",
    )(value)


def join_kernel(sizes, *refs):
    ins, (*outs, sems) = refs[: sum(map(len, sizes))], refs[sum(map(len, sizes)) : -len(sizes)]
    spaces = refs[-len(sizes) :]
    inward, outward = [], []
    ins = list(ins)
    for out, space, parts in zip(outs, spaces, sizes):
        at = 0
        for size in parts:
            number = len(inward)
            to = pl.ds(at, size)
            inward.append(pltpu.make_async_copy(ins.pop(0), space.at[to], sems.at[0, number]))
            outward.append(pltpu.make_async_copy(space.at[to], out.at[to], sems.at[1, number]))
            inward[-1].start()
            at += size
    for first, second in zip(inward, outward):
        first.wait()
        second.start()
    wait_all(outward)


def join(groups):
    arrays = [array for group in groups for array in group]
    sizes = tuple(tuple(array.shape[0] for array in group) for group in groups)
    shapes = [(sum(parts),) + group[0].shape[1:] for parts, group in zip(sizes, groups)]
    results = pl.pallas_call(
        functools.partial(join_kernel, sizes),
        in_specs=[HBM] * len(arrays),
        out_specs=[HBM] * len(groups),
        out_shape=[struct(shape, BF) for shape in shapes],
        scratch_shapes=[pltpu.SemaphoreType.DMA((2, len(arrays)))]
        + [pltpu.VMEM(shape, BF) for shape in shapes],
        cost_estimate=QUICK,
        compiler_params=pltpu.CompilerParams(vmem_limit_bytes=KERNEL_VMEM),
        name="join",
    )(*arrays)
    return list(results)


def weight_kernel(turned_ref, grad_ref, kept_ref, sent_ref):
    half = D // 2
    sent_ref[...] = dot_nn(turned_ref[half:, :], grad_ref[...]).astype(BF)
    kept_ref[...] = dot_nn(turned_ref[:half, :], grad_ref[...]).astype(BF)


def weight_grad(turned, grad):
    rows, width = grad.shape
    column = lambda height: pl.BlockSpec((height, D), lambda step: (0, step))
    return pl.pallas_call(
        weight_kernel,
        grid=(width // D,),
        in_specs=[whole(D, rows), column(rows)],
        out_specs=[column(D // 2)] * 2,
        out_shape=[struct((D // 2, width), BF)] * 2,
        cost_estimate=QUICK,
        compiler_params=pltpu.CompilerParams(vmem_limit_bytes=KERNEL_VMEM),
        name="weight_grad",
    )(turned, grad)


def add_kernel(widths, outputs, *refs):
    count = sum(map(len, widths)) * 2
    ins, outs, (in_sem, out_sem, *spaces) = (
        refs[:count],
        refs[count : count + len(outputs)],
        refs[count + len(outputs) :],
    )
    firsts = np.cumsum([0] + [len(parts) for parts in widths])
    loads, stores = [], []
    for number, ranges in enumerate(outputs):
        here, below = [], 0
        for group, lo, hi in ranges:
            at = 0
            for part, width in enumerate(widths[group]):
                for side in range(2):
                    source = ins[2 * (firsts[group] + part) + side].at[lo:hi]
                    space = spaces[2 * number + side]
                    to = space.at[below : below + hi - lo, at : at + width]
                    sem = in_sem.at[number, len(here)]
                    here.append(pltpu.make_async_copy(source, to, sem))
                at += width
            below += hi - lo
        start_all(here)
        loads.append(here)
    for number in range(len(outputs)):
        wait_all(loads[number])
        left, right = spaces[2 * number], spaces[2 * number + 1]
        left[...] = (left[...].astype(F32) + right[...].astype(F32)).astype(BF)
        stores.append(pltpu.make_async_copy(left, outs[number], out_sem.at[number]))
        stores[-1].start()
    wait_all(stores)


def add_ranges(groups, outputs):
    rows = groups[0][0][0].shape[1]
    flat = [side.reshape(-1, side.shape[-1]) for group in groups for pair in group for side in pair]
    widths = tuple(tuple(pair[0].shape[-1] for pair in group) for group in groups)
    plan = tuple(tuple((g, lo * rows, hi * rows) for g, lo, hi in ranges) for ranges in outputs)
    shapes = [(sum(hi - lo for _, lo, hi in r), sum(widths[r[0][0]])) for r in plan]
    most = max(sum(2 * len(widths[g]) for g, _, _ in ranges) for ranges in plan)
    results = pl.pallas_call(
        functools.partial(add_kernel, widths, plan),
        in_specs=[HBM] * len(flat),
        out_specs=[HBM] * len(plan),
        out_shape=[struct(shape, BF) for shape in shapes],
        scratch_shapes=[
            pltpu.SemaphoreType.DMA((len(plan), most)),
            pltpu.SemaphoreType.DMA((len(plan),)),
        ]
        + [pltpu.VMEM(shape, BF) for shape in shapes for _ in range(2)],
        cost_estimate=QUICK,
        compiler_params=pltpu.CompilerParams(vmem_limit_bytes=KERNEL_VMEM),
        name="add_ranges",
    )(*flat)
    return [r.reshape(-1, rows, r.shape[-1]) for r in results]


def first_norm_kernel(
    grad_ref,
    tokens_ref,
    live_ref,
    gain_ref,
    order_ref,
    grad_residual_ref,
    mlp_sums_ref,
    grad_b_ref,
    tables_ref,
    *rest,
):
    pieces, (tokens_grad_ref, sums_ref, total, columns, weight, sem) = rest[:PIECES], rest[PIECES:]
    step = pl.program_id(0)

    def copies(index):
        return copy_rows(pieces, (index * D, D), weight, index * D, sem.at[index])

    @pl.when(step == 0)
    def _():
        for index in range(3):
            start_all(copies(index))
        total[...] = jnp.zeros_like(total)

    wait_all(copies(step))
    grad_qkv = grad_ref[...]
    at = pl.multiple_of(step * D, 128)
    total[...] += dot_nt(grad_qkv, weight[:, pl.ds(at, D)])
    columns[pl.ds(step, 1), :] = jnp.sum(grad_qkv.astype(F32), axis=0, keepdims=True)

    @pl.when(step == 2)
    def _():
        unit, rstd = normalise(tokens_ref[...].astype(F32))
        grad = natural_order(total[...], order_ref[...]) * live_ref[...]
        tokens_grad_ref[...] = (
            grad_residual_ref[...] + normalise_back(grad, unit, rstd, gain_ref[...])
        ).astype(BF)
        vectors = [
            [jnp.sum(grad * unit, axis=0, keepdims=True)],
            [jnp.sum(grad, axis=0, keepdims=True)],
            [columns[block : block + 1, :] for block in range(3)],
            [mlp_sums_ref[0:1, :]],
            [mlp_sums_ref[1:2, :]],
            [mlp_sums_ref[2:3, :]],
            [grad_b_ref[...]],
            [mlp_sums_ref[3:4, :]],
        ]
        at = 0
        for vector in vectors:
            for piece in vector:
                for lane in range(0, piece.shape[1], 128):
                    sums_ref[at : at + 1, :] = piece[:, lane : lane + 128]
                    at += 1
        sums_ref[at:TABLE_ROW, :] = jnp.zeros((TABLE_ROW - at, 128), F32)
        tables = tables_ref[...] * (1.0 / SCALE)
        low = lax.broadcasted_iota(jnp.int32, (32, 128), 1) < 64
        sums_ref[TABLE_ROW:, :] = jnp.where(
            low,
            tables[64:96] + pltpu.roll(tables[:32], 64, 1),
            pltpu.roll(tables[96:], 64, 1) + tables[32:64],
        )


TABLE_ROW = 80
SUM_ROWS = TABLE_ROW + 32


def first_norm_back(grad_qkv, pieces, tokens, live, gain, order, grad_residual, sums, b_up, tables):
    rows = tokens.shape[0]
    return pl.pallas_call(
        first_norm_kernel,
        grid=(3,),
        in_specs=[
            pl.BlockSpec((rows, D), lambda step: (0, step)),
            whole(rows, D),
            whole(rows, 1),
            whole(1, D),
            whole(D, D),
            whole(rows, D),
            whole(8, D),
            whole(1, FF),
            whole(128, 128),
        ]
        + [HBM] * PIECES,
        out_specs=[whole(rows, D), whole(SUM_ROWS, 128)],
        out_shape=[struct((rows, D), BF), struct((SUM_ROWS, 128), F32)],
        scratch_shapes=[
            pltpu.VMEM((rows, D), F32),
            pltpu.VMEM((8, D), F32),
            pltpu.VMEM((D, 3 * D), BF),
            pltpu.SemaphoreType.DMA((3, PIECES)),
        ],
        cost_estimate=LONG,
        compiler_params=pltpu.CompilerParams(vmem_limit_bytes=KERNEL_VMEM),
        name="first_norm_back",
    )(grad_qkv, tokens, live, gain, order, grad_residual, sums, b_up, tables, *pieces)


def own_kernel(sizes, me_ref, sums_ref, *refs):
    outs, (table_h_ref, table_w_ref) = refs[:-2], refs[-2:]
    lane = lax.broadcasted_iota(jnp.int32, (1, 128), 1)
    row = 0
    for size, whole_size, out in zip(sizes, WHOLE_SIZES, outs):
        start = me_ref[0] * size
        at, shift = row + start // 128, lax.rem(start, 128)
        here = pltpu.roll(sums_ref[pl.ds(at, 1), :], lax.rem(128 - shift, 128), 1)
        there = pltpu.roll(sums_ref[pl.ds(at + 1, 1), :], lax.rem(128 - shift, 128), 1)
        out[...] = jnp.where(lane + shift < 128, here, there)[:, :size]
        row += whole_size // 128
    count = 2 * WIN - 1
    table_h_ref[...] = sums_ref[TABLE_ROW : TABLE_ROW + count, :HEAD_DIM]
    table_w_ref[...] = pltpu.roll(sums_ref[TABLE_ROW:, :], 64, 1)[:count, :HEAD_DIM]


WHOLE_SIZES = (D, D, 3 * D, D, D, D, FF, D)


def own_small(sums, me, sizes):
    table = struct((2 * WIN - 1, HEAD_DIM), F32)
    return pl.pallas_call(
        functools.partial(own_kernel, tuple(sizes)),
        in_specs=[
            pl.BlockSpec(memory_space=pltpu.SMEM),
            pl.BlockSpec(memory_space=pltpu.VMEM),
        ],
        out_specs=[pl.BlockSpec(memory_space=pltpu.VMEM)] * (len(sizes) + 2),
        out_shape=[struct((1, size), F32) for size in sizes] + [table, table],
        name="own_small",
    )(me.reshape(1), sums)


def hop(array, mask, count):
    return lax.ppermute(array, "fsdp", [(i, i ^ mask) for i in range(count)])


def hop_plan(count):
    far = count // 4
    return 2 * far, far, [1 << bit for bit in range(1, far.bit_length() - 1)]


def after(values, deps):
    if not deps:
        return list(values)
    return list(lax.optimization_barrier(tuple(values) + tuple(deps))[: len(values)])


def gather_stages(shard, count, pieces, early=False):
    farthest, far, middle = hop_plan(count)
    deps = yield
    (shard,) = after([shard], deps)
    got = hop(shard, farthest, count)
    deps = yield [shard]
    (got,) = after([got], deps)
    near = jnp.stack((shard, got))
    got = hop(near, far, count)
    deps = yield [near]
    (got,) = after([got], deps)
    stacks = [near, got]
    for masks in zip(middle, middle[::-1]):
        got = [hop(stack, mask, count) for stack, mask in zip(stacks, masks)]
        deps = yield stacks
        got = after(got, deps or stacks)
        if masks[0] != middle[-1]:
            pairs = list(zip(stacks, got))
            stacks = [jnp.concatenate(p, axis=0) for p in pairs] if early else join(pairs)
    (own,) = join([(stacks[0], got[0], stacks[1], got[1])])
    other = hop(own, 1, count)
    order = sum_order(count)
    pieces += [(own, order[: count // 2]), (other, order[count // 2 :])]
    yield [own]


def start(stages):
    next(stages)
    return stages


def finish(stages):
    for _ in stages:
        pass


def place_kernel(owners, columns, me_ref, *refs):
    stacks, outs, sem = refs[: len(owners)], refs[len(owners) : -1], refs[-1]
    copies = []
    for stack, stack_owners in zip(stacks, owners):
        for index, mask in enumerate(stack_owners):
            owner = jnp.bitwise_xor(me_ref[0], mask)
            for out, lo, hi, to in columns:
                copies.append(
                    pltpu.make_async_copy(
                        stack.at[index, :, lo:hi],
                        outs[out].at[owner, :, to : to + hi - lo],
                        sem.at[len(copies)],
                    )
                )
                copies[-1].start()
    for copy in copies:
        copy.wait()


def place(pieces, columns, widths, me, count):
    stacks = [stack for stack, _ in pieces]
    rows = stacks[0].shape[1]
    outs = pl.pallas_call(
        functools.partial(place_kernel, tuple(tuple(o) for _, o in pieces), columns),
        in_specs=[pl.BlockSpec(memory_space=pltpu.SMEM)]
        + [pl.BlockSpec(memory_space=pl.ANY)] * len(stacks),
        out_specs=[pl.BlockSpec(memory_space=pltpu.VMEM)] * len(widths),
        out_shape=[jax.ShapeDtypeStruct((count, rows, width), BF) for width in widths],
        scratch_shapes=[pltpu.SemaphoreType.DMA((count * len(columns),))],
        cost_estimate=QUICK,
        compiler_params=pltpu.CompilerParams(vmem_limit_bytes=KERNEL_VMEM),
        name="place",
    )(me.reshape(1), *stacks)
    return [out.reshape(count * rows, width) for out, width in zip(outs, widths)]


def sum_order(count):
    farthest, far, middle = hop_plan(count)
    order = []
    for masks, block in ((middle, [0, farthest]), (middle[::-1], [far, far ^ farthest])):
        for mask in masks:
            block = block + [owner ^ mask for owner in block]
        order += block
    return order + [owner ^ 1 for owner in order]


def order_matrix(me, count, rows):
    masks = np.repeat(np.array(sum_order(count), np.int32), rows)
    wanted = jnp.bitwise_xor(me, masks) * rows + np.tile(np.arange(rows, dtype=np.int32), count)
    features = lax.broadcasted_iota(jnp.int32, (count * rows, count * rows), 0)
    return (features == wanted[None, :]).astype(BF)


def pick_kernel(masks, me_ref, stack, kept, sent, sem):
    half = len(masks) // 2
    copies = []
    for index, mask in enumerate(masks):
        owner = jnp.bitwise_xor(me_ref[0], mask)
        out = kept if index < half else sent
        copies.append(
            pltpu.make_async_copy(stack.at[owner], out.at[index % half], sem.at[index])
        )
        copies[-1].start()
    for copy in copies:
        copy.wait()


def pick(array, me, count):
    stack = array.reshape(count, -1, array.shape[-1])
    half = jax.ShapeDtypeStruct((count // 2,) + stack.shape[1:], BF)
    return pl.pallas_call(
        functools.partial(pick_kernel, tuple(sum_order(count))),
        in_specs=[
            pl.BlockSpec(memory_space=pltpu.SMEM),
            pl.BlockSpec(memory_space=pl.ANY),
        ],
        out_specs=[pl.BlockSpec(memory_space=pltpu.VMEM)] * 2,
        out_shape=[half, half],
        scratch_shapes=[pltpu.SemaphoreType.DMA((count,))],
        cost_estimate=QUICK,
        compiler_params=pltpu.CompilerParams(vmem_limit_bytes=16 * 1024 * 1024),
        name="pick",
    )(me.reshape(1), stack)


def add_low(left, right):
    return (left.astype(F32) + right.astype(F32)).astype(BF)


def scatter_stages(parts, count, result, late=(), direct=False, inbox=None):
    farthest, far, middle = hop_plan(count)
    blocks = count // 2
    half = blocks // 2
    shape = lambda side: side.reshape(blocks, -1, side.shape[-1])
    kept, sent = [shape(k) for k, _ in parts], [shape(s) for _, s in parts]
    deps = yield
    sent = after(sent, deps)
    arrived = [hop(side, 1, count) for side in sent]
    deps = yield sent
    arrived = after(arrived, deps)
    pairs = list(zip(kept, arrived)) + [(shape(k), shape(got)) for k, got in late]

    def added(groups, outputs):
        rows = groups[0][0][0].shape[1]
        if all(lo * rows % 16 == 0 and hi * rows % 16 == 0 for o in outputs for _, lo, hi in o):
            return add_ranges(groups, outputs)
        return [
            jnp.concatenate(
                [
                    jnp.concatenate([add_low(a[lo:hi], b[lo:hi]) for a, b in groups[g]], axis=-1)
                    for g, lo, hi in ranges
                ],
                axis=0,
            )
            for ranges in outputs
        ]

    groups, size = [pairs], half
    for masks in zip(middle[::-1], middle):
        size //= 2
        at = [(0, 0), (0, half)] if len(groups) == 1 else [(0, 0), (1, 0)]
        *sends, near, back = added(
            groups,
            [[(group, lo + size, lo + 2 * size)] for group, lo in at]
            + [[(group, lo, lo + size)] for group, lo in at],
        )
        got = [hop(send, mask, count) for send, mask in zip(sends, masks)]
        if inbox is not None:
            inbox[:] = got
        deps = yield sends
        got = after(got, deps)
        groups = [[(near, got[0])], [(back, got[1])]]
    if direct:
        near, back = (a.astype(F32) + b.astype(F32) for ((a, b),) in groups)
        sends = [block.astype(BF) for block in (near[1], back[0], back[1])]
        got = [hop(s, m, count) for s, m in zip(sends, (farthest, far, far ^ farthest))]
        deps = yield sends
        got = after(got, deps)
        total = near[0] + got[0].astype(F32) + got[1].astype(F32) + got[2].astype(F32)
        result.append(total)
        yield [total]
        return
    send, kept = added(groups, [[(1, 0, 2)], [(0, 0, 2)]])
    got = hop(send, far, count)
    deps = yield [send]
    (got,) = after([got], deps)
    send = add_low(kept[1], got[1])
    arrived = hop(send, farthest, count)
    deps = yield [send]
    (arrived,) = after([arrived], deps)
    total = kept[0].astype(F32) + got[0].astype(F32) + arrived.astype(F32)
    result.append(total)
    yield [total]


def sum_stages(array, count, result):
    bits = count.bit_length() - 1
    deps = yield
    for mask in [1 << bit for bit in [0, bits - 2, bits - 1] + list(range(1, bits - 2))]:
        (array,) = after([array], deps)
        got = hop(array, mask, count)
        deps = yield [array]
        (got,) = after([got], deps)
        array = array + got
    result.append(array)
    yield [array]


def per_device(
    tokens,
    window_pos,
    norm1_gain,
    norm1_bias,
    qkv_weight,
    qkv_bias,
    rel_pos_h,
    rel_pos_w,
    proj_weight,
    proj_bias,
    norm2_gain,
    norm2_bias,
    lin1_weight,
    lin1_bias,
    lin2_weight,
    lin2_bias,
    out_grad,
):
    vectors = (
        norm1_gain,
        norm1_bias,
        qkv_bias,
        proj_bias,
        norm2_gain,
        norm2_bias,
        lin1_bias,
        lin2_bias,
    )
    sizes = [v.shape[0] for v in vectors]
    used = sum(sizes)
    shard_rows = qkv_weight.shape[0]
    count = lax.axis_size("fsdp")
    me = lax.axis_index("fsdp")

    packed = lax.optimization_barrier(jnp.concatenate(vectors))
    packed = jnp.pad(packed, (0, shard_rows * 128 - used)).reshape(shard_rows, 128)
    middle = len(hop_plan(count)[2])
    first_pieces, second_pieces, third_pieces = [], [], []
    first = start(
        gather_stages(
            jnp.concatenate((qkv_weight, proj_weight, packed), axis=1).astype(BF), count, first_pieces, early=True
        )
    )
    second = start(gather_stages(lin1_weight.astype(BF), count, second_pieces))
    third = start(gather_stages(lin2_weight.astype(BF), count, third_pieces))
    onehot, shift = window_constants()
    onehot = jnp.asarray(onehot, BF)
    shift = jnp.asarray(shift)
    order = order_matrix(me, count, shard_rows)
    table = table_lanes(rel_pos_h, rel_pos_w)
    live = slot_mask(window_pos)
    inverse = np.argsort(np.array(sum_order(count)))
    places = jnp.take(jnp.asarray(inverse, jnp.int32), jnp.bitwise_xor(me, np.arange(count)))
    first.send(None)
    sent = first.send(None)
    first.send(None)
    second.send(sent)
    third.send(sent)
    for _ in range(middle - 1):
        sent = first.send(None)
    sent = second.send(sent) + third.send(sent)
    sent = second.send(sent) + third.send(sent)
    first.send(sent + [order, table, live, places])

    (small,) = place(
        first_pieces, ((0, 4 * D, 4 * D + 128, 0),), (128,), me, count
    )
    small = small.reshape(count, shard_rows * 128)[:, :used].astype(F32)
    edges = np.cumsum([0] + sizes)
    gain_one, bias_one, b_qkv, b_proj, gain_two, bias_two, b_up, b_down = (
        small[:, lo:hi].reshape(-1) for lo, hi in zip(edges[:-1], edges[1:])
    )
    flat = lambda pieces: [stack.reshape(-1, stack.shape[-1]) for stack, _ in pieces]
    first_pieces = flat(first_pieces)
    (gated_tokens,) = after([tokens], sent)
    turned_one, qkv = front(
        gated_tokens, live, order, jnp.stack((gain_one, bias_one)), b_qkv.reshape(1, -1), first_pieces
    )
    sent = [turned_one]
    for _ in range(middle - 1):
        sent = second.send(sent) + third.send(sent)
    (qkv,) = after([qkv], sent)
    mixed, probs = attention(qkv, table, onehot, shift)
    sent = third.send([mixed])
    b_up = b_up.reshape(1, FF)
    (mixed,) = after([mixed], sent + [b_up])
    vectors = jnp.stack((b_proj, gain_two, bias_two, b_down))
    residual, normed_two, turned_two, ordered_mixed = project(
        tokens, mixed, order, vectors, first_pieces
    )
    second.send([residual])

    own_down, own_up, own_third, all_small = [], [], [], []
    down_weight = placed_down(third_pieces, me, count)
    output, grad_normed, kept_up, sent_up, grad_b_up, down_parts = mlp(
        me,
        count,
        places,
        normed_two,
        turned_two,
        live,
        out_grad,
        residual,
        vectors,
        b_up,
        flat(second_pieces),
        down_weight,
    )
    late, got_up, got_down = [], [], []
    up = start(scatter_stages([(kept_up, sent_up)], count, own_up, late, inbox=got_up))
    down = start(scatter_stages([down_parts], count, own_down, inbox=got_down))
    sent = up.send(None)
    sent = down.send(sent)
    (grad_normed,) = after([grad_normed], sent)
    grad_residual, grad_mixed, kept_proj, sent_proj, mlp_sums = second_norm_back(
        grad_normed, residual, ordered_mixed, live, out_grad, order, vectors, first_pieces
    )
    late.append((kept_proj, hop(sent_proj, 1, count)))
    sent = up.send([grad_mixed])
    sent = down.send(sent)
    (grad_mixed,) = after([grad_mixed], sent)
    grad_qkv, tables = attention_back(qkv, grad_mixed, probs, table, onehot, shift)
    sent = [grad_qkv]
    for _ in range(middle - 1):
        sent = up.send(sent)
    (grad_qkv,) = after([grad_qkv], sent)
    kept_qkv, sent_qkv = weight_grad(turned_one, grad_qkv)
    third_sum = start(scatter_stages([(kept_qkv, sent_qkv)], count, own_third, direct=True))
    sent = third_sum.send(None)
    for _ in range(middle - 1):
        sent = down.send([kept_qkv] + sent)
    sent = up.send(sent)
    (grad_qkv,) = after([grad_qkv], sent)
    tokens_grad, small_sums = first_norm_back(
        grad_qkv,
        first_pieces,
        tokens,
        live,
        gain_one.reshape(1, D),
        order,
        grad_residual,
        mlp_sums,
        grad_b_up,
        tables,
    )
    small_stages = start(sum_stages(small_sums, count, all_small))
    sent = third_sum.send([small_sums] + got_down)
    sent = small_stages.send(sent)
    sent = down.send(sent)
    sent = up.send(sent)
    (gated_tables,) = after([tables], sent)
    sent = [marker(gated_tables)]
    sent = small_stages.send(sent)
    for _ in range(middle - 1):
        sent = third_sum.send(sent)
    sent = small_stages.send(sent)
    sent = down.send(sent)
    sent = small_stages.send(sent)
    sent = third_sum.send(sent)
    sent = up.send(sent)
    sent = small_stages.send(sent)
    for stages in (down, up, third_sum, small_stages):
        finish(stages)
    own_qkv, own_proj = own_third[0], own_up[0][:, FF:]
    *owned, table_h, table_w = own_small(all_small[0], me, sizes)
    owned = [vector.reshape(-1) for vector in owned]

    return (
        output,
        tokens_grad,
        owned[0],
        owned[1],
        own_qkv,
        owned[2],
        table_h,
        table_w,
        own_proj,
        owned[3],
        owned[4],
        owned[5],
        own_up[0][:, :FF],
        owned[6],
        own_down[0],
        owned[7],
    )


def solution(mesh):
    rows = P("fsdp", None)
    line = P("fsdp")
    return jax.shard_map(
        per_device,
        mesh=mesh,
        in_specs=(
            rows,
            line,
            line,
            line,
            rows,
            line,
            P(),
            P(),
            rows,
            line,
            line,
            line,
            rows,
            line,
            rows,
            line,
            rows,
        ),
        out_specs=(
            rows,
            rows,
            line,
            line,
            rows,
            line,
            P(),
            P(),
            rows,
            line,
            line,
            line,
            rows,
            line,
            rows,
            line,
        ),
        check_vma=False,
    )
```

```python
import functools

import jax
import jax.numpy as jnp
import numpy as np
from jax import lax
from jax.experimental import pallas as pl
from jax.experimental.pallas import tpu as pltpu
from jax.sharding import PartitionSpec as P

D = 768
HEADS = 12
HEAD_DIM = 64
FF = 3072
WIN = 14
NWS = 5
EDGE = 8
LENGTH = WIN * WIN
PAIRS = HEADS // 2
BLOCK = 200
SCALE = HEAD_DIM ** (-0.5)
EPS = 1e-06
ATTENTION_VMEM = 60 * 1024 * 1024
KERNEL_VMEM = 60 * 1024 * 1024
QUICK = pl.CostEstimate(flops=1, bytes_accessed=1, transcendentals=0)
LONG = pl.CostEstimate(flops=100_000_000_000, bytes_accessed=1, transcendentals=0)
LANES = 256
BF = jnp.bfloat16
F32 = jnp.float32


def window_constants():
    onehot = np.zeros((2, BLOCK, 128), np.float32)
    shift = np.zeros((2, 16, LANES), np.int32)
    for win in range(2):
        for row in range(BLOCK):
            slot = row - 4 * win
            if not 0 <= slot < LENGTH:
                onehot[win, row, 63] = onehot[win, row, 127] = -1e30
                continue
            y, x = divmod(slot, WIN)
            for base in (0, 64):
                for lane in (0, 16):
                    onehot[win, row, base + lane + WIN - 1 - y] = 1.0
                    onehot[win, row, base + 32 + lane + WIN - 1 - x] = 1.0
            shift[win, :8, row] = y
            shift[win, 8:, row] = x
    return onehot, shift


def table_lanes(rel_pos_h, rel_pos_w):
    flip = jnp.concatenate(
        (
            jnp.pad(rel_pos_h, ((0, 5), (0, 0))),
            jnp.pad(rel_pos_w, ((0, 5), (0, 0))),
        ),
        axis=0,
    ).astype(BF) * BF(1.0 / SCALE)
    nothing = jnp.zeros_like(flip)
    return jnp.concatenate(
        (jnp.concatenate((nothing, flip), axis=1), jnp.concatenate((flip, nothing), axis=1)), axis=0
    )


def dot_nn(a, b):
    return jnp.dot(a, b, preferred_element_type=F32)


def dot_nt(a, b):
    return lax.dot_general(a, b, (((1,), (1,)), ((), ())), preferred_element_type=F32)


def dot_tn(a, b):
    return lax.dot_general(a, b, (((0,), (0,)), ((), ())), preferred_element_type=F32)


def low_half():
    return lax.broadcasted_iota(jnp.int32, (BLOCK, 128), 1) < 64


def row_valid(win):
    row = lax.broadcasted_iota(jnp.int32, (BLOCK, 128), 0)
    return row < LENGTH if win == 0 else row >= BLOCK - LENGTH


def merge_windows(first, second):
    return jnp.concatenate((first[:192], first[192:] + second[:8], second[8:]), axis=0)


def pad_rows(values):
    return jnp.concatenate((values, jnp.zeros((LANES - BLOCK, 128), F32)), axis=0)


def bit_masks(shift, rows):
    shift = jnp.broadcast_to(shift[:1], (rows, LANES))
    return [(shift & (1 << bit)) != 0 for bit in range(4)]


def skew(values, masks):
    values = jnp.where(masks[3], values[8:], values[:24])
    values = jnp.where(masks[2], pltpu.roll(values, 20, 0), values)
    values = jnp.where(masks[1], pltpu.roll(values, 22, 0), values)[:16]
    return jnp.where(masks[0][:16], pltpu.roll(values, 15, 0), values)


def unskew(values, masks):
    nothing = jnp.zeros((8, LANES), F32)
    values = jnp.concatenate((values, nothing), axis=0)
    for bit in range(3):
        values = jnp.where(masks[bit], pltpu.roll(values, 1 << bit, 0), values)
    return jnp.concatenate(
        (
            jnp.where(masks[3][:8], 0.0, values[:8]),
            jnp.where(masks[3][:16], values[:16], values[8:]),
            jnp.where(masks[3][:8], values[16:], 0.0),
        ),
        axis=0,
    )


def attn_fwd_kernel(q_ref, k_ref, v_ref, table_ref, onehot_ref, shift_ref, mixed_ref, probs_ref):
    low = low_half()
    last = lax.broadcasted_iota(jnp.int32, (16, LANES), 0) == 15
    mixed = []
    for win in range(2):
        rows = pl.ds(192 * win, BLOCK)
        queries = pad_rows(q_ref[rows, :].astype(F32) * SCALE).T
        k = k_ref[rows, :].astype(F32)
        v = v_ref[rows, :]
        rel = dot_nn(table_ref[...], queries.astype(BF))
        onehot = onehot_ref[win].astype(F32)
        by_row = bit_masks(shift_ref[win, :8], 24)
        by_col = bit_masks(shift_ref[win, 8:], 24)
        halves = []
        for head in range(2):
            base = 64 if head == 0 else 0
            from_row = skew(rel[base : base + 32], by_row)
            from_col = skew(rel[base + 32 : base + 64], by_col)
            row_top = from_row.astype(BF).astype(F32)
            col_top = from_col.astype(BF).astype(F32)
            extra = (row_top, from_row - row_top, col_top, jnp.where(last, 1.0, from_col - col_top))
            if head == 0:
                left = jnp.concatenate((queries[:64],) + extra, axis=0).astype(BF)
                right = jnp.where(low, k, onehot).astype(BF)
            else:
                left = jnp.concatenate(extra + (queries[64:],), axis=0).astype(BF)
                right = jnp.where(low, onehot, k).astype(BF)
            scores = dot_nn(right, left)
            expon = jnp.exp(scores - jnp.max(scores, axis=0, keepdims=True))
            probs = expon * (1.0 / jnp.sum(expon, axis=0, keepdims=True))
            probs_ref[0, 2 * win + head] = probs
            halves.append(dot_tn(v, probs.astype(BF)))
        both = jnp.concatenate((halves[0][:HEAD_DIM], halves[1][HEAD_DIM:]), axis=0).T[:BLOCK]
        mixed.append(jnp.where(row_valid(win), both, 0.0))
    mixed_ref[...] = merge_windows(*mixed).astype(BF)


def attn_bwd_kernel(
    q_ref,
    k_ref,
    v_ref,
    grad_ref,
    probs_ref,
    table_ref,
    onehot_ref,
    shift_ref,
    grad_qkv_ref,
    table_grad_ref,
):
    pair = pl.program_id(0)
    low = low_half()

    @pl.when(pair == 0)
    def _():
        table_grad_ref[...] = jnp.zeros_like(table_grad_ref)

    parts = ([], [], [])
    table_total = jnp.zeros((128, 128), F32)
    for win in range(2):
        rows = pl.ds(192 * win, BLOCK)
        q = pad_rows(q_ref[rows, :].astype(F32) * SCALE).astype(BF)
        k = k_ref[rows, :].astype(F32)
        v = v_ref[rows, :]
        grad = pad_rows(jnp.where(row_valid(win), grad_ref[rows, :].astype(F32), 0.0))
        grad_low = grad.astype(BF)
        wide_low = lax.broadcasted_iota(jnp.int32, (LANES, 128), 1) < 64
        onehot = onehot_ref[win].astype(F32)
        by_row = bit_masks(shift_ref[win, :8], 24)
        by_col = bit_masks(shift_ref[win, 8:], 24)
        by_query, by_key, by_value, rel = [], [], [], []
        for head in range(2):
            if head == 0:
                right = jnp.where(low, k, onehot).astype(BF)
                grad_own = jnp.where(wide_low, grad, 0.0).astype(BF)
            else:
                right = jnp.where(low, onehot, k).astype(BF)
                grad_own = jnp.where(wide_low, 0.0, grad).astype(BF)
            probs = probs_ref[0, 2 * win + head]
            grad_probs = dot_nt(v, grad_own)
            row_dot = jnp.sum(probs * grad_probs, axis=0, keepdims=True)
            grad_scores = (probs * (grad_probs - row_dot)).astype(BF)
            by_value.append(dot_nn(probs.astype(BF), grad_low))
            by_key.append(dot_nn(grad_scores, q))
            back = dot_tn(right, grad_scores)
            own, base = (back[:64], 64) if head == 0 else (back[64:], 0)
            by_query.append(own)
            rel.append(unskew(back[base : base + 16], by_row))
            rel.append(unskew(back[base + 32 : base + 48], by_col))
        rel = jnp.concatenate((rel[2], rel[3], rel[0], rel[1]), axis=0)
        rel_top = rel.astype(BF)
        rel_rest = (rel - rel_top.astype(F32)).astype(BF)
        table = table_ref[...]
        from_rel = dot_tn(table, rel_top) + dot_tn(table, rel_rest)
        table_total += dot_nn(rel_top, q) + dot_nn(rel_rest, q)
        parts[0].append((jnp.concatenate(by_query, axis=0) + from_rel).T[:BLOCK] * SCALE)
        parts[1].append(jnp.where(low, by_key[0], by_key[1]))
        parts[2].append(jnp.where(low, by_value[0], by_value[1]))
    for block in range(3):
        at = pl.multiple_of(block * D + pair * 128, 128)
        grad_qkv_ref[:, pl.ds(at, 128)] = merge_windows(*parts[block]).astype(BF)
    table_grad_ref[...] += table_total


def attention_specs(rows):
    column = lambda block: pl.BlockSpec((rows, 128), lambda pair: (0, block * PAIRS + pair))
    whole = lambda *shape: pl.BlockSpec(shape, lambda pair: (0,) * len(shape))
    return (
        [column(0), column(1), column(2)],
        [whole(128, 128), whole(2, BLOCK, 128), whole(2, 16, LANES)],
        pl.BlockSpec((1, 4, BLOCK, LANES), lambda pair: (pair, 0, 0, 0)),
        whole,
    )


def attention(qkv, table, onehot, shift):
    rows = qkv.shape[0]
    columns, constants, probs_spec, _ = attention_specs(rows)
    return pl.pallas_call(
        attn_fwd_kernel,
        grid=(PAIRS,),
        in_specs=columns + constants,
        out_specs=[pl.BlockSpec((rows, 128), lambda pair: (0, pair)), probs_spec],
        out_shape=[
            jax.ShapeDtypeStruct((rows, D), BF),
            jax.ShapeDtypeStruct((PAIRS, 4, BLOCK, LANES), F32),
        ],
        cost_estimate=QUICK,
        compiler_params=pltpu.CompilerParams(vmem_limit_bytes=ATTENTION_VMEM),
        name="attention",
    )(qkv, qkv, qkv, table, onehot, shift)


def attention_back(qkv, grad_mixed, probs, table, onehot, shift):
    rows = qkv.shape[0]
    columns, constants, probs_spec, whole = attention_specs(rows)
    return pl.pallas_call(
        attn_bwd_kernel,
        grid=(PAIRS,),
        in_specs=columns + [pl.BlockSpec((rows, 128), lambda pair: (0, pair)), probs_spec]
        + constants,
        out_specs=[whole(rows, 3 * D), whole(128, 128)],
        out_shape=[
            jax.ShapeDtypeStruct((rows, 3 * D), BF),
            jax.ShapeDtypeStruct((128, 128), F32),
        ],
        cost_estimate=QUICK,
        compiler_params=pltpu.CompilerParams(vmem_limit_bytes=ATTENTION_VMEM),
        name="attention_back",
    )(qkv, qkv, qkv, grad_mixed, probs, table, onehot, shift)


def slot_mask(window_pos):
    row_win = window_pos // NWS
    col_win = window_pos % NWS
    rows_ok = jnp.where(row_win == NWS - 1, EDGE, WIN)
    cols_ok = jnp.where(col_win == NWS - 1, EDGE, WIN)
    positions = jnp.arange(WIN, dtype=jnp.int32)
    inside = (positions[None, :, None] < rows_ok[:, None, None]) & (
        positions[None, None, :] < cols_ok[:, None, None]
    )
    return inside.reshape(-1, 1).astype(F32)


def normalise(values):
    centred = values - jnp.mean(values, axis=-1, keepdims=True)
    rstd = lax.rsqrt(jnp.mean(centred * centred, axis=-1, keepdims=True) + EPS)
    return centred * rstd, rstd


def normalise_back(grad, hat, rstd, gain):
    grad_hat = grad * gain
    return rstd * (
        grad_hat
        - jnp.mean(grad_hat, axis=-1, keepdims=True)
        - hat * jnp.mean(grad_hat * hat, axis=-1, keepdims=True)
    )


def normal_cdf(values):
    return 0.5 * (1.0 + lax.erf(values * np.float32(np.sqrt(0.5))))


def normal_pdf(values):
    return np.float32(1.0 / np.sqrt(2.0 * np.pi)) * jnp.exp(-0.5 * values * values)


def copy_rows(pieces, columns, out, to, sems):
    rows = pieces[0].shape[0]
    lo, width = columns
    return [
        pltpu.make_async_copy(
            piece.at[:, pl.ds(lo, width)],
            out.at[index * rows : (index + 1) * rows, pl.ds(to, width)],
            sems.at[index],
        )
        for index, piece in enumerate(pieces)
    ]


def start_all(copies):
    for copy in copies:
        copy.start()


def wait_all(copies):
    for copy in copies:
        copy.wait()


def front_kernel(tokens_ref, live_ref, order_ref, rows_ref, b_qkv_ref, *rest):
    pieces, (turned_ref, qkv_ref, weight, sem) = rest[:PIECES], rest[PIECES:]
    copies = [copy_rows(pieces, (block * D, D), weight, block * D, sem.at[block]) for block in range(3)]
    for block in copies:
        start_all(block)
    unit, _ = normalise(tokens_ref[...].astype(F32))
    normed = ((unit * rows_ref[0:1, :] + rows_ref[1:2, :]) * live_ref[:, :1]).astype(BF)
    turned = dot_nn(normed, order_ref[...])
    normed = turned.astype(BF)
    turned_ref[...] = turned.T.astype(BF)
    for block in range(3):
        wait_all(copies[block])
        at = block * D
        values = dot_nn(normed, weight[:, at : at + D]) + b_qkv_ref[:, at : at + D]
        qkv_ref[:, at : at + D] = values.astype(BF)


PIECES = 2
HBM = pl.BlockSpec(memory_space=pl.ANY)
VMEM = pl.BlockSpec(memory_space=pltpu.VMEM)
SMEM = pl.BlockSpec(memory_space=pltpu.SMEM)


def front(tokens, live, order, vectors, b_qkv, pieces):
    rows = tokens.shape[0]
    return pl.pallas_call(
        front_kernel,
        in_specs=[VMEM] * 5 + [HBM] * PIECES,
        out_specs=[VMEM] * 2,
        out_shape=[struct((D, rows), BF), struct((rows, 3 * D), BF)],
        scratch_shapes=[pltpu.VMEM((D, 3 * D), BF), pltpu.SemaphoreType.DMA((3, PIECES))],
        cost_estimate=QUICK,
        compiler_params=pltpu.CompilerParams(vmem_limit_bytes=KERNEL_VMEM),
        name="front",
    )(tokens, live, order, vectors, b_qkv, *pieces)


def proj_kernel(tokens_ref, values_ref, order_ref, rows_ref, *rest):
    pieces, (residual_ref, normed_ref, turned_ref, mixed_ref, w_proj, sem) = rest[:PIECES], rest[PIECES:]
    b_proj, gain, bias = (rows_ref[i : i + 1, :] for i in range(3))
    copies = copy_rows(pieces, (3 * D, D), w_proj, 0, sem)
    start_all(copies)
    mixed = dot_nn(values_ref[...], order_ref[...]).astype(BF)
    mixed_ref[...] = mixed
    wait_all(copies)
    values = tokens_ref[...].astype(F32) + dot_nn(mixed, w_proj[...]) + b_proj
    residual_ref[...] = values
    low = (normalise(values)[0] * gain + bias).astype(BF)
    low = dot_nn(low, order_ref[...])
    normed_ref[...] = low.astype(BF)
    turned_ref[...] = low.T.astype(BF)


def down_copies(pieces, owners, me_ref, weight, sems):
    copies = []
    for piece, masks in zip(pieces, owners):
        rows = piece.shape[0] // len(masks)
        for index, mask in enumerate(masks):
            to = jnp.bitwise_xor(me_ref[0], mask) * rows
            copies.append(
                pltpu.make_async_copy(
                    piece.at[index * rows : (index + 1) * rows],
                    weight.at[pl.ds(pl.multiple_of(to, rows), rows)],
                    sems.at[len(copies)],
                )
            )
    return copies


def mlp_kernel(split_rows, owners, place_ref, me_ref, *rest):
    normed_ref, turned_ref, live_ref, out_grad_ref, residual_ref, rows_ref, b_up_ref, *rest = rest
    up_pieces, rest = rest[:PIECES], rest[PIECES:]
    down_pieces, rest = rest[: len(owners)], rest[len(owners) :]
    output_ref, grad_normed_ref, kept_ref, sent_ref, grad_b_ref, *rest = rest
    if split_rows:
        kept_down_ref, sent_down_ref, *rest = rest
    else:
        grad_down_ref, *rest = rest
    branch, actives, grads, w_up, w_down, staged, sem, up_sem, down_sem = rest
    step = pl.program_id(0)
    half = D // 2

    def up_copies(index):
        return copy_rows(up_pieces, (index * TILE, TILE), w_up, index * TILE, up_sem.at[index])

    @pl.when(step == 0)
    def _():
        start_all(up_copies(0))
        start_all(down_copies(down_pieces, owners, me_ref, w_down, down_sem))
        for index in range(1, STEPS):
            start_all(up_copies(index))
        branch[...] = (out_grad_ref[...].astype(F32) * live_ref[:, :1]).astype(BF)

    wait_all(up_copies(step))
    at = pl.multiple_of(step * TILE, TILE)
    hidden = dot_nn(normed_ref[...], w_up[:, pl.ds(at, TILE)]) + b_up_ref[...]
    cdf = normal_cdf(hidden)
    active = (hidden * cdf).astype(BF)
    slope = cdf + hidden * normal_pdf(hidden)
    grad_down = dot_tn(active, branch[...]).astype(BF)

    @pl.when(step == 0)
    def _():
        wait_all(down_copies(down_pieces, owners, me_ref, w_down, down_sem))

    grad_active = dot_nt(branch[...], w_down[pl.ds(at, TILE), :])
    grad_hidden = (grad_active * slope).astype(BF)
    sent_ref[...] = dot_nn(turned_ref[half:, :], grad_hidden).astype(BF)
    kept_ref[...] = dot_nn(turned_ref[:half, :], grad_hidden).astype(BF)
    actives[:, pl.ds(at, TILE)] = active
    grads[:, pl.ds(at, TILE)] = grad_hidden
    grad_b_ref[...] = jnp.sum(grad_hidden.astype(F32), axis=0, keepdims=True)

    def finish_sums():
        grad_normed_ref[...] = dot_nt(grads[...], w_up[...])
        total = residual_ref[...] + rows_ref[3:4, :] + dot_nn(actives[...], w_down[...])
        output_ref[...] = (total * live_ref[:, :1]).astype(BF)

    if not split_rows:
        grad_down_ref[...] = grad_down
        pl.when(step == STEPS - 1)(finish_sums)
        return

    slot = lax.rem(step, 2)
    blocks = staged.shape[1]

    def copy(slot, block, out, to):
        return pltpu.make_async_copy(staged.at[slot, block], out.at[to], sem.at[slot, block])

    @pl.when(step >= 2)
    def _():
        for block in range(blocks):
            copy(slot, block, kept_down_ref, 0).wait()

    staged[slot] = grad_down.reshape(blocks, split_rows, D)
    places = kept_down_ref.shape[0]
    for block in range(blocks):
        to = place_ref[step * blocks + block]

        @pl.when(to < places)
        def _():
            copy(slot, block, kept_down_ref, to).start()

        @pl.when(to >= places)
        def _():
            copy(slot, block, sent_down_ref, to - places).start()

    @pl.when(step == STEPS - 1)
    def _():
        finish_sums()
        for last_slot in range(2):
            for block in range(blocks):
                copy(last_slot, block, kept_down_ref, 0).wait()


def second_norm_kernel(
    grad_normed_ref, residual_ref, mixed_ref, live_ref, out_grad_ref, order_ref, rows_ref, *rest
):
    pieces, rest = rest[:PIECES], rest[PIECES:]
    grad_residual_ref, grad_mixed_ref, *rest = rest
    kept_proj_ref, sent_proj_ref, sums_ref, w_proj, sem = rest
    half = D // 2
    copies = copy_rows(pieces, (3 * D, D), w_proj, 0, sem)
    start_all(copies)
    grad = natural_order(grad_normed_ref[...], order_ref[...])
    unit, rstd = normalise(residual_ref[...])
    grad_out = out_grad_ref[...].astype(F32) * live_ref[:, :1]
    grad_residual = grad_out + normalise_back(grad, unit, rstd, rows_ref[1:2, :])
    grad_residual_ref[...] = grad_residual
    grad_attn = grad_residual.astype(BF)
    wait_all(copies)
    grad_mixed = dot_nt(grad_attn, w_proj[...]).astype(BF)
    grad_mixed_ref[...] = dot_nt(grad_mixed, order_ref[...]).astype(BF)
    sent_proj_ref[...] = dot_tn(mixed_ref[:, half:], grad_attn).astype(BF)
    kept_proj_ref[...] = dot_tn(mixed_ref[:, :half], grad_attn).astype(BF)
    sums_ref[0:1, :] = jnp.sum(grad_attn.astype(F32), axis=0, keepdims=True)
    sums_ref[1:2, :] = jnp.sum(grad * unit, axis=0, keepdims=True)
    sums_ref[2:3, :] = jnp.sum(grad, axis=0, keepdims=True)
    sums_ref[3:4, :] = jnp.sum(grad_out.astype(BF).astype(F32), axis=0, keepdims=True)
    sums_ref[4:, :] = jnp.zeros((4, D), F32)


def natural_order(values, order):
    top = values.astype(BF)
    rest = (values - top.astype(F32)).astype(BF)
    return dot_nt(top, order) + dot_nt(rest, order)


TILE = 768
STEPS = FF // TILE


def whole(*shape):
    return pl.BlockSpec(shape, lambda step: (0,) * len(shape))


def struct(shape, dtype):
    return jax.ShapeDtypeStruct(shape, dtype)


def project(tokens, mixed, order, vectors, pieces):
    rows = tokens.shape[0]
    return pl.pallas_call(
        proj_kernel,
        in_specs=[VMEM] * 4 + [HBM] * PIECES,
        out_specs=[VMEM] * 4,
        out_shape=[
            struct((rows, D), F32),
            struct((rows, D), BF),
            struct((D, rows), BF),
            struct((rows, D), BF),
        ],
        scratch_shapes=[pltpu.VMEM((D, D), BF), pltpu.SemaphoreType.DMA((PIECES,))],
        cost_estimate=QUICK,
        compiler_params=pltpu.CompilerParams(vmem_limit_bytes=KERNEL_VMEM),
        name="project",
    )(tokens, mixed, order, vectors, *pieces)


def placed_down(pieces, me, count):
    if FF // count % 16:
        return place(pieces, ((0, 0, D, 0),), (D,), me, count), ((0,),), jnp.zeros((1,), jnp.int32)
    owners = tuple(tuple(masks) for _, masks in pieces)
    return [stack.reshape(-1, D) for stack, _ in pieces], owners, me.reshape(1)


def mlp(
    me, count, places, normed, turned, live, out_grad, residual, vectors, b_up, up_pieces, down
):
    rows = normed.shape[0]
    block_rows = FF // count
    split_rows = block_rows if block_rows % 16 == 0 else 0
    down_pieces, owners, me_down = down
    column = lambda height: pl.BlockSpec((height, TILE), lambda step: (0, step))
    if split_rows:
        half = struct((count // 2, block_rows, D), BF)
        grad_specs, grad_shapes = [HBM] * 2, [half, half]
        staged = (2, TILE // block_rows, block_rows, D)
    else:
        grad_specs = [pl.BlockSpec((TILE, D), lambda step: (step, 0))]
        grad_shapes = [struct((FF, D), BF)]
        staged = (2, 1, 16, 128)
    wide = (rows, D)
    results = pl.pallas_call(
        functools.partial(mlp_kernel, split_rows, owners),
        grid=(STEPS,),
        in_specs=[SMEM, SMEM, whole(*wide), whole(D, rows), whole(rows, 128)]
        + [whole(*wide), whole(*wide), whole(4, D), column(1)]
        + [HBM] * (len(up_pieces) + len(down_pieces)),
        out_specs=[whole(*wide), whole(*wide), column(D // 2), column(D // 2), column(1)]
        + grad_specs,
        out_shape=[
            struct(wide, BF),
            struct(wide, F32),
            struct((D // 2, FF), BF),
            struct((D // 2, FF), BF),
            struct((1, FF), F32),
        ]
        + grad_shapes,
        scratch_shapes=[
            pltpu.VMEM(wide, BF),
            pltpu.VMEM((rows, FF), BF),
            pltpu.VMEM((rows, FF), BF),
            pltpu.VMEM((D, FF), BF),
            pltpu.VMEM((FF, D), BF),
            pltpu.VMEM(staged, BF),
            pltpu.SemaphoreType.DMA(staged[:2]),
            pltpu.SemaphoreType.DMA((STEPS, PIECES)),
            pltpu.SemaphoreType.DMA((sum(map(len, owners)),)),
        ],
        cost_estimate=QUICK,
        compiler_params=pltpu.CompilerParams(vmem_limit_bytes=KERNEL_VMEM),
        name="mlp",
    )(
        places,
        me_down,
        normed,
        turned,
        live,
        out_grad,
        residual,
        vectors,
        b_up,
        *up_pieces,
        *down_pieces,
    )
    parts = results[5:] if split_rows else pick(results[5], me, count)
    return tuple(results[:5]) + (tuple(parts),)


def second_norm_back(grad_normed, residual, mixed, live, out_grad, order, vectors, pieces):
    rows = residual.shape[0]
    return pl.pallas_call(
        second_norm_kernel,
        in_specs=[VMEM] * 7 + [HBM] * PIECES,
        out_specs=[VMEM] * 5,
        out_shape=[
            struct((rows, D), F32),
            struct((rows, D), BF),
            struct((D // 2, D), BF),
            struct((D // 2, D), BF),
            struct((8, D), F32),
        ],
        scratch_shapes=[pltpu.VMEM((D, D), BF), pltpu.SemaphoreType.DMA((PIECES,))],
        cost_estimate=QUICK,
        compiler_params=pltpu.CompilerParams(vmem_limit_bytes=KERNEL_VMEM),
        name="second_norm_back",
    )(grad_normed, residual, mixed, live, out_grad, order, vectors, *pieces)


def marker_kernel(value_ref, out_ref):
    out_ref[...] = value_ref[...]


def marker(value):
    return pl.pallas_call(
        marker_kernel,
        in_specs=[VMEM],
        out_specs=VMEM,
        out_shape=struct(value.shape, value.dtype),
        cost_estimate=LONG,
        name="marker",
    )(value)


def join_kernel(sizes, *refs):
    ins, (*outs, sems) = refs[: sum(map(len, sizes))], refs[sum(map(len, sizes)) : -len(sizes)]
    spaces = refs[-len(sizes) :]
    inward, outward = [], []
    ins = list(ins)
    for out, space, parts in zip(outs, spaces, sizes):
        at = 0
        for size in parts:
            number = len(inward)
            to = pl.ds(at, size)
            inward.append(pltpu.make_async_copy(ins.pop(0), space.at[to], sems.at[0, number]))
            outward.append(pltpu.make_async_copy(space.at[to], out.at[to], sems.at[1, number]))
            inward[-1].start()
            at += size
    for first, second in zip(inward, outward):
        first.wait()
        second.start()
    wait_all(outward)


def join(groups):
    arrays = [array for group in groups for array in group]
    sizes = tuple(tuple(array.shape[0] for array in group) for group in groups)
    shapes = [(sum(parts),) + group[0].shape[1:] for parts, group in zip(sizes, groups)]
    results = pl.pallas_call(
        functools.partial(join_kernel, sizes),
        in_specs=[HBM] * len(arrays),
        out_specs=[HBM] * len(groups),
        out_shape=[struct(shape, BF) for shape in shapes],
        scratch_shapes=[pltpu.SemaphoreType.DMA((2, len(arrays)))]
        + [pltpu.VMEM(shape, BF) for shape in shapes],
        cost_estimate=QUICK,
        compiler_params=pltpu.CompilerParams(vmem_limit_bytes=KERNEL_VMEM),
        name="join",
    )(*arrays)
    return list(results)


def weight_kernel(turned_ref, grad_ref, kept_ref, sent_ref):
    half = D // 2
    sent_ref[...] = dot_nn(turned_ref[half:, :], grad_ref[...]).astype(BF)
    kept_ref[...] = dot_nn(turned_ref[:half, :], grad_ref[...]).astype(BF)


def weight_grad(turned, grad):
    rows, width = grad.shape
    column = lambda height: pl.BlockSpec((height, D), lambda step: (0, step))
    return pl.pallas_call(
        weight_kernel,
        grid=(width // D,),
        in_specs=[whole(D, rows), column(rows)],
        out_specs=[column(D // 2)] * 2,
        out_shape=[struct((D // 2, width), BF)] * 2,
        cost_estimate=QUICK,
        compiler_params=pltpu.CompilerParams(vmem_limit_bytes=KERNEL_VMEM),
        name="weight_grad",
    )(turned, grad)


def add_kernel(widths, outputs, *refs):
    count = sum(map(len, widths)) * 2
    ins, outs, (in_sem, out_sem, *spaces) = (
        refs[:count],
        refs[count : count + len(outputs)],
        refs[count + len(outputs) :],
    )
    firsts = np.cumsum([0] + [len(parts) for parts in widths])
    loads, stores = [], []
    for number, ranges in enumerate(outputs):
        here, below = [], 0
        for group, lo, hi in ranges:
            at = 0
            for part, width in enumerate(widths[group]):
                for side in range(2):
                    source = ins[2 * (firsts[group] + part) + side].at[lo:hi]
                    space = spaces[2 * number + side]
                    to = space.at[below : below + hi - lo, at : at + width]
                    sem = in_sem.at[number, len(here)]
                    here.append(pltpu.make_async_copy(source, to, sem))
                at += width
            below += hi - lo
        start_all(here)
        loads.append(here)
    for number in range(len(outputs)):
        wait_all(loads[number])
        left, right = spaces[2 * number], spaces[2 * number + 1]
        left[...] = (left[...].astype(F32) + right[...].astype(F32)).astype(BF)
        stores.append(pltpu.make_async_copy(left, outs[number], out_sem.at[number]))
        stores[-1].start()
    wait_all(stores)


def add_ranges(groups, outputs, cost):
    rows = groups[0][0][0].shape[1]
    flat = [side.reshape(-1, side.shape[-1]) for group in groups for pair in group for side in pair]
    widths = tuple(tuple(pair[0].shape[-1] for pair in group) for group in groups)
    plan = tuple(tuple((g, lo * rows, hi * rows) for g, lo, hi in ranges) for ranges in outputs)
    shapes = [(sum(hi - lo for _, lo, hi in r), sum(widths[r[0][0]])) for r in plan]
    most = max(sum(2 * len(widths[g]) for g, _, _ in ranges) for ranges in plan)
    results = pl.pallas_call(
        functools.partial(add_kernel, widths, plan),
        in_specs=[HBM] * len(flat),
        out_specs=[HBM] * len(plan),
        out_shape=[struct(shape, BF) for shape in shapes],
        scratch_shapes=[
            pltpu.SemaphoreType.DMA((len(plan), most)),
            pltpu.SemaphoreType.DMA((len(plan),)),
        ]
        + [pltpu.VMEM(shape, BF) for shape in shapes for _ in range(2)],
        cost_estimate=cost,
        compiler_params=pltpu.CompilerParams(vmem_limit_bytes=KERNEL_VMEM),
        name="add_ranges",
    )(*flat)
    return [r.reshape(-1, rows, r.shape[-1]) for r in results]


def first_norm_kernel(
    grad_ref,
    tokens_ref,
    live_ref,
    gain_ref,
    order_ref,
    grad_residual_ref,
    mlp_sums_ref,
    grad_b_ref,
    tables_ref,
    *rest,
):
    pieces, (tokens_grad_ref, sums_ref, total, columns, weight, sem) = rest[:PIECES], rest[PIECES:]
    step = pl.program_id(0)

    def copies(index):
        return copy_rows(pieces, (index * D, D), weight, index * D, sem.at[index])

    @pl.when(step == 0)
    def _():
        for index in range(3):
            start_all(copies(index))
        total[...] = jnp.zeros_like(total)

    wait_all(copies(step))
    grad_qkv = grad_ref[...]
    at = pl.multiple_of(step * D, 128)
    total[...] += dot_nt(grad_qkv, weight[:, pl.ds(at, D)])
    columns[pl.ds(step, 1), :] = jnp.sum(grad_qkv.astype(F32), axis=0, keepdims=True)

    @pl.when(step == 2)
    def _():
        unit, rstd = normalise(tokens_ref[...].astype(F32))
        grad = natural_order(total[...], order_ref[...]) * live_ref[:, :1]
        tokens_grad_ref[...] = (
            grad_residual_ref[...] + normalise_back(grad, unit, rstd, gain_ref[...])
        ).astype(BF)
        vectors = [
            [jnp.sum(grad * unit, axis=0, keepdims=True)],
            [jnp.sum(grad, axis=0, keepdims=True)],
            [columns[block : block + 1, :] for block in range(3)],
            [mlp_sums_ref[0:1, :]],
            [mlp_sums_ref[1:2, :]],
            [mlp_sums_ref[2:3, :]],
            [grad_b_ref[...]],
            [mlp_sums_ref[3:4, :]],
        ]
        at = 0
        for vector in vectors:
            for piece in vector:
                for lane in range(0, piece.shape[1], 128):
                    sums_ref[at : at + 1, :] = piece[:, lane : lane + 128]
                    at += 1
        sums_ref[at:TABLE_ROW, :] = jnp.zeros((TABLE_ROW - at, 128), F32)
        tables = tables_ref[...] * (1.0 / SCALE)
        low = lax.broadcasted_iota(jnp.int32, (32, 128), 1) < 64
        sums_ref[TABLE_ROW:, :] = jnp.where(
            low,
            tables[64:96] + pltpu.roll(tables[:32], 64, 1),
            pltpu.roll(tables[96:], 64, 1) + tables[32:64],
        )


TABLE_ROW = 80
SUM_ROWS = TABLE_ROW + 32


def first_norm_back(grad_qkv, pieces, tokens, live, gain, order, grad_residual, sums, b_up, tables):
    rows = tokens.shape[0]
    return pl.pallas_call(
        first_norm_kernel,
        grid=(3,),
        in_specs=[
            pl.BlockSpec((rows, D), lambda step: (0, step)),
            whole(rows, D),
            whole(rows, 128),
            whole(1, D),
            whole(D, D),
            whole(rows, D),
            whole(8, D),
            whole(1, FF),
            whole(128, 128),
        ]
        + [HBM] * PIECES,
        out_specs=[whole(rows, D), whole(SUM_ROWS, 128)],
        out_shape=[struct((rows, D), BF), struct((SUM_ROWS, 128), F32)],
        scratch_shapes=[
            pltpu.VMEM((rows, D), F32),
            pltpu.VMEM((8, D), F32),
            pltpu.VMEM((D, 3 * D), BF),
            pltpu.SemaphoreType.DMA((3, PIECES)),
        ],
        cost_estimate=QUICK,
        compiler_params=pltpu.CompilerParams(vmem_limit_bytes=KERNEL_VMEM),
        name="first_norm_back",
    )(grad_qkv, tokens, live, gain, order, grad_residual, sums, b_up, tables, *pieces)


def own_kernel(sizes, me_ref, sums_ref, *refs):
    outs, (table_h_ref, table_w_ref) = refs[:-2], refs[-2:]
    lane = lax.broadcasted_iota(jnp.int32, (1, 128), 1)
    row = 0
    for size, whole_size, out in zip(sizes, WHOLE_SIZES, outs):
        start = me_ref[0] * size
        at, shift = row + start // 128, lax.rem(start, 128)
        here = pltpu.roll(sums_ref[pl.ds(at, 1), :], lax.rem(128 - shift, 128), 1)
        there = pltpu.roll(sums_ref[pl.ds(at + 1, 1), :], lax.rem(128 - shift, 128), 1)
        out[...] = jnp.where(lane + shift < 128, here, there)[:, :size]
        row += whole_size // 128
    count = 2 * WIN - 1
    table_h_ref[...] = sums_ref[TABLE_ROW : TABLE_ROW + count, :HEAD_DIM]
    table_w_ref[...] = pltpu.roll(sums_ref[TABLE_ROW:, :], 64, 1)[:count, :HEAD_DIM]


WHOLE_SIZES = (D, D, 3 * D, D, D, D, FF, D)


def own_small(sums, me, sizes):
    table = struct((2 * WIN - 1, HEAD_DIM), F32)
    return pl.pallas_call(
        functools.partial(own_kernel, tuple(sizes)),
        in_specs=[
            pl.BlockSpec(memory_space=pltpu.SMEM),
            pl.BlockSpec(memory_space=pltpu.VMEM),
        ],
        out_specs=[pl.BlockSpec(memory_space=pltpu.VMEM)] * (len(sizes) + 2),
        out_shape=[struct((1, size), F32) for size in sizes] + [table, table],
        name="own_small",
    )(me.reshape(1), sums)


def hop(array, mask, count):
    return lax.ppermute(array, "fsdp", [(i, i ^ mask) for i in range(count)])


def hop_plan(count):
    far = count // 4
    return 2 * far, far, [1 << bit for bit in range(1, far.bit_length() - 1)]


def after(values, deps):
    if not deps:
        return list(values)
    return list(lax.optimization_barrier(tuple(values) + tuple(deps))[: len(values)])


def gather_stages(shard, count, pieces, early=False):
    farthest, far, middle = hop_plan(count)
    deps = yield
    (shard,) = after([shard], deps)
    got = hop(shard, farthest, count)
    deps = yield [shard]
    (got,) = after([got], deps)
    near = jnp.stack((shard, got))
    got = hop(near, far, count)
    deps = yield [near]
    (got,) = after([got], deps)
    stacks = [near, got]
    for masks in zip(middle, middle[::-1]):
        got = [hop(stack, mask, count) for stack, mask in zip(stacks, masks)]
        deps = yield stacks
        got = after(got, deps or stacks)
        if masks[0] != middle[-1]:
            pairs = list(zip(stacks, got))
            stacks = [jnp.concatenate(p, axis=0) for p in pairs] if early else join(pairs)
    (own,) = join([(stacks[0], got[0], stacks[1], got[1])])
    other = hop(own, 1, count)
    order = sum_order(count)
    pieces += [(own, order[: count // 2]), (other, order[count // 2 :])]
    yield [own]


def start(stages):
    next(stages)
    return stages


def finish(stages):
    for _ in stages:
        pass


def place_kernel(owners, columns, me_ref, *refs):
    stacks, outs, sem = refs[: len(owners)], refs[len(owners) : -1], refs[-1]
    copies = []
    for stack, stack_owners in zip(stacks, owners):
        for index, mask in enumerate(stack_owners):
            owner = jnp.bitwise_xor(me_ref[0], mask)
            for out, lo, hi, to in columns:
                copies.append(
                    pltpu.make_async_copy(
                        stack.at[index, :, lo:hi],
                        outs[out].at[owner, :, to : to + hi - lo],
                        sem.at[len(copies)],
                    )
                )
                copies[-1].start()
    for copy in copies:
        copy.wait()


def place(pieces, columns, widths, me, count):
    stacks = [stack for stack, _ in pieces]
    rows = stacks[0].shape[1]
    outs = pl.pallas_call(
        functools.partial(place_kernel, tuple(tuple(o) for _, o in pieces), columns),
        in_specs=[pl.BlockSpec(memory_space=pltpu.SMEM)]
        + [pl.BlockSpec(memory_space=pl.ANY)] * len(stacks),
        out_specs=[pl.BlockSpec(memory_space=pltpu.VMEM)] * len(widths),
        out_shape=[jax.ShapeDtypeStruct((count, rows, width), BF) for width in widths],
        scratch_shapes=[pltpu.SemaphoreType.DMA((count * len(columns),))],
        cost_estimate=QUICK,
        compiler_params=pltpu.CompilerParams(vmem_limit_bytes=KERNEL_VMEM),
        name="place",
    )(me.reshape(1), *stacks)
    return [out.reshape(count * rows, width) for out, width in zip(outs, widths)]


def sum_order(count):
    farthest, far, middle = hop_plan(count)
    order = []
    for masks, block in ((middle, [0, farthest]), (middle[::-1], [far, far ^ farthest])):
        for mask in masks:
            block = block + [owner ^ mask for owner in block]
        order += block
    return order + [owner ^ 1 for owner in order]


def order_matrix(me, count, rows):
    masks = np.repeat(np.array(sum_order(count), np.int32), rows)
    wanted = jnp.bitwise_xor(me, masks) * rows + np.tile(np.arange(rows, dtype=np.int32), count)
    features = lax.broadcasted_iota(jnp.int32, (count * rows, count * rows), 0)
    return (features == wanted[None, :]).astype(BF)


def pick_kernel(masks, me_ref, stack, kept, sent, sem):
    half = len(masks) // 2
    copies = []
    for index, mask in enumerate(masks):
        owner = jnp.bitwise_xor(me_ref[0], mask)
        out = kept if index < half else sent
        copies.append(
            pltpu.make_async_copy(stack.at[owner], out.at[index % half], sem.at[index])
        )
        copies[-1].start()
    for copy in copies:
        copy.wait()


def pick(array, me, count):
    stack = array.reshape(count, -1, array.shape[-1])
    half = jax.ShapeDtypeStruct((count // 2,) + stack.shape[1:], BF)
    return pl.pallas_call(
        functools.partial(pick_kernel, tuple(sum_order(count))),
        in_specs=[
            pl.BlockSpec(memory_space=pltpu.SMEM),
            pl.BlockSpec(memory_space=pl.ANY),
        ],
        out_specs=[pl.BlockSpec(memory_space=pltpu.VMEM)] * 2,
        out_shape=[half, half],
        scratch_shapes=[pltpu.SemaphoreType.DMA((count,))],
        cost_estimate=QUICK,
        compiler_params=pltpu.CompilerParams(vmem_limit_bytes=16 * 1024 * 1024),
        name="pick",
    )(me.reshape(1), stack)


def add_low(left, right):
    return (left.astype(F32) + right.astype(F32)).astype(BF)


def scatter_stages(parts, count, result, late=(), direct=False, inbox=None, costs=()):
    farthest, far, middle = hop_plan(count)
    blocks = count // 2
    half = blocks // 2
    shape = lambda side: side.reshape(blocks, -1, side.shape[-1])
    kept, sent = [shape(k) for k, _ in parts], [shape(s) for _, s in parts]
    deps = yield
    sent = after(sent, deps)
    arrived = [hop(side, 1, count) for side in sent]
    deps = yield sent
    arrived = after(arrived, deps)
    pairs = list(zip(kept, arrived)) + [(shape(k), shape(got)) for k, got in late]

    costs = list(costs)

    def added(groups, outputs):
        cost = costs.pop(0) if costs else QUICK
        rows = groups[0][0][0].shape[1]
        if all(lo * rows % 16 == 0 and hi * rows % 16 == 0 for o in outputs for _, lo, hi in o):
            return add_ranges(groups, outputs, cost)
        return [
            jnp.concatenate(
                [
                    jnp.concatenate([add_low(a[lo:hi], b[lo:hi]) for a, b in groups[g]], axis=-1)
                    for g, lo, hi in ranges
                ],
                axis=0,
            )
            for ranges in outputs
        ]

    groups, size = [pairs], half
    for masks in zip(middle[::-1], middle):
        size //= 2
        at = [(0, 0), (0, half)] if len(groups) == 1 else [(0, 0), (1, 0)]
        *sends, near, back = added(
            groups,
            [[(group, lo + size, lo + 2 * size)] for group, lo in at]
            + [[(group, lo, lo + size)] for group, lo in at],
        )
        got = [hop(send, mask, count) for send, mask in zip(sends, masks)]
        if inbox is not None:
            inbox[:] = got
        deps = yield sends
        got = after(got, deps)
        groups = [[(near, got[0])], [(back, got[1])]]
    if direct:
        near, back = (a.astype(F32) + b.astype(F32) for ((a, b),) in groups)
        sends = [block.astype(BF) for block in (near[1], back[0], back[1])]
        got = [hop(s, m, count) for s, m in zip(sends, (farthest, far, far ^ farthest))]
        deps = yield sends
        got = after(got, deps)
        total = near[0] + got[0].astype(F32) + got[1].astype(F32) + got[2].astype(F32)
        result.append(total)
        yield [total]
        return
    send, kept = added(groups, [[(1, 0, 2)], [(0, 0, 2)]])
    got = hop(send, far, count)
    deps = yield [send]
    (got,) = after([got], deps)
    send = add_low(kept[1], got[1])
    arrived = hop(send, farthest, count)
    deps = yield [send]
    (arrived,) = after([arrived], deps)
    total = kept[0].astype(F32) + got[0].astype(F32) + arrived.astype(F32)
    result.append(total)
    yield [total]


def sum_stages(array, count, result):
    bits = count.bit_length() - 1
    deps = yield
    for mask in [1 << bit for bit in [bits - 2, bits - 1, 0] + list(range(1, bits - 2))]:
        (array,) = after([array], deps)
        got = hop(array, mask, count)
        deps = yield [array]
        (got,) = after([got], deps)
        array = array + got
    result.append(array)
    yield [array]


def per_device(
    tokens,
    window_pos,
    norm1_gain,
    norm1_bias,
    qkv_weight,
    qkv_bias,
    rel_pos_h,
    rel_pos_w,
    proj_weight,
    proj_bias,
    norm2_gain,
    norm2_bias,
    lin1_weight,
    lin1_bias,
    lin2_weight,
    lin2_bias,
    out_grad,
):
    vectors = (
        norm1_gain,
        norm1_bias,
        qkv_bias,
        proj_bias,
        norm2_gain,
        norm2_bias,
        lin1_bias,
        lin2_bias,
    )
    sizes = [v.shape[0] for v in vectors]
    used = sum(sizes)
    shard_rows = qkv_weight.shape[0]
    count = lax.axis_size("fsdp")
    me = lax.axis_index("fsdp")

    packed = lax.optimization_barrier(jnp.concatenate(vectors))
    packed = jnp.pad(packed, (0, shard_rows * 128 - used)).reshape(shard_rows, 128)
    middle = len(hop_plan(count)[2])
    first_pieces, second_pieces, third_pieces = [], [], []
    first = start(
        gather_stages(
            jnp.concatenate((qkv_weight, proj_weight, packed), axis=1).astype(BF), count, first_pieces, early=True
        )
    )
    second = start(gather_stages(lin1_weight.astype(BF), count, second_pieces))
    third = start(gather_stages(lin2_weight.astype(BF), count, third_pieces))
    onehot, shift = window_constants()
    onehot = jnp.asarray(onehot, BF)
    shift = jnp.asarray(shift)
    order = order_matrix(me, count, shard_rows)
    table = table_lanes(rel_pos_h, rel_pos_w)
    live = jnp.broadcast_to(slot_mask(window_pos), (tokens.shape[0], 128))
    inverse = np.argsort(np.array(sum_order(count)))
    places = jnp.take(jnp.asarray(inverse, jnp.int32), jnp.bitwise_xor(me, np.arange(count)))
    first.send(None)
    sent = first.send(None)
    first.send(None)
    second.send(sent)
    third.send(sent)
    for _ in range(middle - 1):
        sent = first.send(None)
    sent = second.send(sent) + third.send(sent)
    sent = second.send(sent) + third.send(sent)
    first.send(sent + [order, table, live, places])

    (small,) = place(
        first_pieces, ((0, 4 * D, 4 * D + 128, 0),), (128,), me, count
    )
    small = small.reshape(count, shard_rows * 128)[:, :used].astype(F32)
    edges = np.cumsum([0] + sizes)
    gain_one, bias_one, b_qkv, b_proj, gain_two, bias_two, b_up, b_down = (
        small[:, lo:hi].reshape(-1) for lo, hi in zip(edges[:-1], edges[1:])
    )
    flat = lambda pieces: [stack.reshape(-1, stack.shape[-1]) for stack, _ in pieces]
    first_pieces = flat(first_pieces)
    (gated_tokens,) = after([tokens], sent)
    turned_one, qkv = front(
        gated_tokens, live, order, jnp.stack((gain_one, bias_one)), b_qkv.reshape(1, -1), first_pieces
    )
    sent = [turned_one]
    for _ in range(middle - 1):
        sent = second.send(sent) + third.send(sent)
    (qkv,) = after([qkv], sent)
    mixed, probs = attention(qkv, table, onehot, shift)
    sent = third.send([mixed])
    b_up = b_up.reshape(1, FF)
    (mixed,) = after([mixed], sent + [b_up])
    vectors = jnp.stack((b_proj, gain_two, bias_two, b_down))
    residual, normed_two, turned_two, ordered_mixed = project(
        tokens, mixed, order, vectors, first_pieces
    )
    second.send([residual])

    own_down, own_up, own_third, all_small = [], [], [], []
    down_weight = placed_down(third_pieces, me, count)
    output, grad_normed, kept_up, sent_up, grad_b_up, down_parts = mlp(
        me,
        count,
        places,
        normed_two,
        turned_two,
        live,
        out_grad,
        residual,
        vectors,
        b_up,
        flat(second_pieces),
        down_weight,
    )
    late, got_up, got_down = [], [], []
    up = start(scatter_stages([(kept_up, sent_up)], count, own_up, late, inbox=got_up))
    down = start(
        scatter_stages([down_parts], count, own_down, inbox=got_down, costs=(QUICK, LONG))
    )
    sent = up.send(None)
    sent = down.send(sent)
    (grad_normed,) = after([grad_normed], sent)
    grad_residual, grad_mixed, kept_proj, sent_proj, mlp_sums = second_norm_back(
        grad_normed, residual, ordered_mixed, live, out_grad, order, vectors, first_pieces
    )
    late.append((kept_proj, hop(sent_proj, 1, count)))
    sent = up.send([grad_mixed])
    sent = down.send(sent)
    (grad_mixed,) = after([grad_mixed], sent)
    grad_qkv, tables = attention_back(qkv, grad_mixed, probs, table, onehot, shift)
    sent = [grad_qkv]
    for _ in range(middle - 1):
        sent = up.send(sent)
    (grad_qkv,) = after([grad_qkv], sent)
    kept_qkv, sent_qkv = weight_grad(turned_one, grad_qkv)
    third_sum = start(scatter_stages([(kept_qkv, sent_qkv)], count, own_third, direct=True))
    sent = third_sum.send(None)
    (grad_qkv,) = after([grad_qkv], sent)
    tokens_grad, small_sums = first_norm_back(
        grad_qkv,
        first_pieces,
        tokens,
        live,
        gain_one.reshape(1, D),
        order,
        grad_residual,
        mlp_sums,
        grad_b_up,
        tables,
    )
    small_stages = start(sum_stages(small_sums, count, all_small))
    sent = small_stages.send(None)
    for _ in range(middle - 1):
        sent = down.send([small_sums] + sent + got_up)
    sent = third_sum.send(sent)
    sent = up.send(sent)
    (gated_tables,) = after([tables], sent)
    sent = [marker(gated_tables)]
    sent = small_stages.send(sent)
    sent = down.send(sent)
    for _ in range(middle - 1):
        sent = third_sum.send(sent)
    sent = up.send(sent)
    sent = small_stages.send(sent)
    sent = third_sum.send(sent)
    sent = small_stages.send(sent)
    sent = down.send(sent)
    sent = small_stages.send(sent)
    sent = up.send(sent)
    for stages in (down, up, third_sum, small_stages):
        finish(stages)
    own_qkv, own_proj = own_third[0], own_up[0][:, FF:]
    *owned, table_h, table_w = own_small(all_small[0], me, sizes)
    owned = [vector.reshape(-1) for vector in owned]

    return (
        output,
        tokens_grad,
        owned[0],
        owned[1],
        own_qkv,
        owned[2],
        table_h,
        table_w,
        own_proj,
        owned[3],
        owned[4],
        owned[5],
        own_up[0][:, :FF],
        owned[6],
        own_down[0],
        owned[7],
    )


def solution(mesh):
    rows = P("fsdp", None)
    line = P("fsdp")
    return jax.shard_map(
        per_device,
        mesh=mesh,
        in_specs=(
            rows,
            line,
            line,
            line,
            rows,
            line,
            P(),
            P(),
            rows,
            line,
            line,
            line,
            rows,
            line,
            rows,
            line,
            rows,
        ),
        out_specs=(
            rows,
            rows,
            line,
            line,
            rows,
            line,
            P(),
            P(),
            rows,
            line,
            line,
            line,
            rows,
            line,
            rows,
            line,
        ),
        check_vma=False,
    )
```

```python
import functools

import jax
import jax.numpy as jnp
import numpy as np
from jax import lax
from jax.experimental import pallas as pl
from jax.experimental.pallas import tpu as pltpu
from jax.sharding import PartitionSpec as P

D = 768
HEADS = 12
HEAD_DIM = 64
FF = 3072
WIN = 14
NWS = 5
EDGE = 8
LENGTH = WIN * WIN
PAIRS = HEADS // 2
BLOCK = 200
SCALE = HEAD_DIM ** (-0.5)
EPS = 1e-06
ATTENTION_VMEM = 60 * 1024 * 1024
KERNEL_VMEM = 60 * 1024 * 1024
QUICK = pl.CostEstimate(flops=1, bytes_accessed=1, transcendentals=0)
LONG = pl.CostEstimate(flops=100_000_000_000, bytes_accessed=1, transcendentals=0)
LANES = 256
BF = jnp.bfloat16
F32 = jnp.float32


def window_constants():
    onehot = np.zeros((2, BLOCK, 128), np.float32)
    shift = np.zeros((2, 16, LANES), np.int32)
    for win in range(2):
        for row in range(BLOCK):
            slot = row - 4 * win
            if not 0 <= slot < LENGTH:
                onehot[win, row, 63] = onehot[win, row, 127] = -1e30
                continue
            y, x = divmod(slot, WIN)
            for base in (0, 64):
                for lane in (0, 16):
                    onehot[win, row, base + lane + WIN - 1 - y] = 1.0
                    onehot[win, row, base + 32 + lane + WIN - 1 - x] = 1.0
            shift[win, :8, row] = y
            shift[win, 8:, row] = x
    return onehot, shift


def table_lanes(rel_pos_h, rel_pos_w):
    flip = jnp.concatenate(
        (
            jnp.pad(rel_pos_h, ((0, 5), (0, 0))),
            jnp.pad(rel_pos_w, ((0, 5), (0, 0))),
        ),
        axis=0,
    ).astype(BF) * BF(1.0 / SCALE)
    nothing = jnp.zeros_like(flip)
    return jnp.concatenate(
        (jnp.concatenate((nothing, flip), axis=1), jnp.concatenate((flip, nothing), axis=1)), axis=0
    )


def dot_nn(a, b):
    return jnp.dot(a, b, preferred_element_type=F32)


def dot_nt(a, b):
    return lax.dot_general(a, b, (((1,), (1,)), ((), ())), preferred_element_type=F32)


def dot_tn(a, b):
    return lax.dot_general(a, b, (((0,), (0,)), ((), ())), preferred_element_type=F32)


def low_half():
    return lax.broadcasted_iota(jnp.int32, (BLOCK, 128), 1) < 64


def row_valid(win):
    row = lax.broadcasted_iota(jnp.int32, (BLOCK, 128), 0)
    return row < LENGTH if win == 0 else row >= BLOCK - LENGTH


def merge_windows(first, second):
    return jnp.concatenate((first[:192], first[192:] + second[:8], second[8:]), axis=0)


def pad_rows(values):
    return jnp.concatenate((values, jnp.zeros((LANES - BLOCK, 128), F32)), axis=0)


def bit_masks(shift, rows):
    shift = jnp.broadcast_to(shift[:1], (rows, LANES))
    return [(shift & (1 << bit)) != 0 for bit in range(4)]


def skew(values, masks):
    values = jnp.where(masks[3], values[8:], values[:24])
    values = jnp.where(masks[2], pltpu.roll(values, 20, 0), values)
    values = jnp.where(masks[1], pltpu.roll(values, 22, 0), values)[:16]
    return jnp.where(masks[0][:16], pltpu.roll(values, 15, 0), values)


def unskew(values, masks):
    nothing = jnp.zeros((8, LANES), F32)
    values = jnp.concatenate((values, nothing), axis=0)
    for bit in range(3):
        values = jnp.where(masks[bit], pltpu.roll(values, 1 << bit, 0), values)
    return jnp.concatenate(
        (
            jnp.where(masks[3][:8], 0.0, values[:8]),
            jnp.where(masks[3][:16], values[:16], values[8:]),
            jnp.where(masks[3][:8], values[16:], 0.0),
        ),
        axis=0,
    )


def attn_fwd_kernel(q_ref, k_ref, v_ref, table_ref, onehot_ref, shift_ref, mixed_ref, probs_ref):
    low = low_half()
    last = lax.broadcasted_iota(jnp.int32, (16, LANES), 0) == 15
    mixed = []
    for win in range(2):
        rows = pl.ds(192 * win, BLOCK)
        queries = pad_rows(q_ref[rows, :].astype(F32) * SCALE).T
        k = k_ref[rows, :].astype(F32)
        v = v_ref[rows, :].astype(F32)
        rel = dot_nn(table_ref[...], queries.astype(BF))
        onehot = onehot_ref[win].astype(F32)
        by_row = bit_masks(shift_ref[win, :8], 24)
        by_col = bit_masks(shift_ref[win, 8:], 24)
        halves = []
        for head in range(2):
            base = 64 if head == 0 else 0
            from_row = skew(rel[base : base + 32], by_row)
            from_col = skew(rel[base + 32 : base + 64], by_col)
            row_top = from_row.astype(BF).astype(F32)
            col_top = from_col.astype(BF).astype(F32)
            extra = (row_top, from_row - row_top, col_top, jnp.where(last, 1.0, from_col - col_top))
            if head == 0:
                left = jnp.concatenate((queries[:64],) + extra, axis=0).astype(BF)
                right = jnp.where(low, k, onehot).astype(BF)
            else:
                left = jnp.concatenate(extra + (queries[64:],), axis=0).astype(BF)
                right = jnp.where(low, onehot, k).astype(BF)
            scores = dot_nn(right, left)
            expon = jnp.exp(scores - jnp.max(scores, axis=0, keepdims=True))
            probs = expon * (1.0 / jnp.sum(expon, axis=0, keepdims=True))
            probs_ref[0, 2 * win + head] = probs
            halves.append(probs)
        values = jnp.concatenate((jnp.where(low, v, 0.0), jnp.where(low, 0.0, v)), axis=0)
        both = dot_tn(values.astype(BF), jnp.concatenate(halves, axis=0).astype(BF)).T[:BLOCK]
        mixed.append(jnp.where(row_valid(win), both, 0.0))
    mixed_ref[...] = merge_windows(*mixed).astype(BF)


def attn_bwd_kernel(
    q_ref,
    k_ref,
    v_ref,
    grad_ref,
    probs_ref,
    table_ref,
    onehot_ref,
    shift_ref,
    grad_qkv_ref,
    table_grad_ref,
):
    pair = pl.program_id(0)
    low = low_half()

    @pl.when(pair == 0)
    def _():
        table_grad_ref[...] = jnp.zeros_like(table_grad_ref)

    parts = ([], [], [])
    table_total = jnp.zeros((128, 128), F32)
    for win in range(2):
        rows = pl.ds(192 * win, BLOCK)
        q = pad_rows(q_ref[rows, :].astype(F32) * SCALE)
        k = k_ref[rows, :].astype(F32)
        v = v_ref[rows, :]
        grad = pad_rows(jnp.where(row_valid(win), grad_ref[rows, :].astype(F32), 0.0))
        wide_low = lax.broadcasted_iota(jnp.int32, (LANES, 128), 1) < 64

        def by_head(values):
            return jnp.concatenate(
                (jnp.where(wide_low, values, 0.0), jnp.where(wide_low, 0.0, values)), axis=0
            ).astype(BF)

        grads, queries = by_head(grad), by_head(q)
        q = q.astype(BF)
        onehot = onehot_ref[win].astype(F32)
        by_row = bit_masks(shift_ref[win, :8], 24)
        by_col = bit_masks(shift_ref[win, 8:], 24)
        probs = jnp.concatenate((probs_ref[0, 2 * win], probs_ref[0, 2 * win + 1]), axis=1)
        grad_probs = dot_nt(v, grads)
        row_dot = jnp.sum(probs * grad_probs, axis=0, keepdims=True)
        grad_scores = (probs * (grad_probs - row_dot)).astype(BF)
        parts[2].append(dot_nn(probs.astype(BF), grads))
        parts[1].append(dot_nn(grad_scores, queries))
        by_query, rel = [], []
        for head in range(2):
            right = (jnp.where(low, k, onehot) if head == 0 else jnp.where(low, onehot, k)).astype(BF)
            back = dot_tn(right, grad_scores[:, head * LANES : (head + 1) * LANES])
            own, base = (back[:64], 64) if head == 0 else (back[64:], 0)
            by_query.append(own)
            rel.append(unskew(back[base : base + 16], by_row))
            rel.append(unskew(back[base + 32 : base + 48], by_col))
        rel = jnp.concatenate((rel[2], rel[3], rel[0], rel[1]), axis=0)
        rel_top = rel.astype(BF).astype(F32)
        rel = jnp.concatenate((rel_top, rel - rel_top), axis=0).astype(BF)
        table = table_ref[...]
        from_rel = dot_tn(jnp.concatenate((table, table), axis=0), rel)
        table_parts = dot_nn(rel, q)
        table_total += table_parts[:128] + table_parts[128:]
        parts[0].append((jnp.concatenate(by_query, axis=0) + from_rel).T[:BLOCK] * SCALE)
    for block in range(3):
        at = pl.multiple_of(block * D + pair * 128, 128)
        grad_qkv_ref[:, pl.ds(at, 128)] = merge_windows(*parts[block]).astype(BF)
    table_grad_ref[...] += table_total


def attention_specs(rows):
    column = lambda block: pl.BlockSpec((rows, 128), lambda pair: (0, block * PAIRS + pair))
    whole = lambda *shape: pl.BlockSpec(shape, lambda pair: (0,) * len(shape))
    return (
        [column(0), column(1), column(2)],
        [whole(128, 128), whole(2, BLOCK, 128), whole(2, 16, LANES)],
        pl.BlockSpec((1, 4, BLOCK, LANES), lambda pair: (pair, 0, 0, 0)),
        whole,
    )


def attention(qkv, table, onehot, shift):
    rows = qkv.shape[0]
    columns, constants, probs_spec, _ = attention_specs(rows)
    return pl.pallas_call(
        attn_fwd_kernel,
        grid=(PAIRS,),
        in_specs=columns + constants,
        out_specs=[pl.BlockSpec((rows, 128), lambda pair: (0, pair)), probs_spec],
        out_shape=[
            jax.ShapeDtypeStruct((rows, D), BF),
            jax.ShapeDtypeStruct((PAIRS, 4, BLOCK, LANES), F32),
        ],
        cost_estimate=QUICK,
        compiler_params=pltpu.CompilerParams(vmem_limit_bytes=ATTENTION_VMEM),
        name="attention",
    )(qkv, qkv, qkv, table, onehot, shift)


def attention_back(qkv, grad_mixed, probs, table, onehot, shift):
    rows = qkv.shape[0]
    columns, constants, probs_spec, whole = attention_specs(rows)
    return pl.pallas_call(
        attn_bwd_kernel,
        grid=(PAIRS,),
        in_specs=columns + [pl.BlockSpec((rows, 128), lambda pair: (0, pair)), probs_spec]
        + constants,
        out_specs=[whole(rows, 3 * D), whole(128, 128)],
        out_shape=[
            jax.ShapeDtypeStruct((rows, 3 * D), BF),
            jax.ShapeDtypeStruct((128, 128), F32),
        ],
        cost_estimate=QUICK,
        compiler_params=pltpu.CompilerParams(vmem_limit_bytes=ATTENTION_VMEM),
        name="attention_back",
    )(qkv, qkv, qkv, grad_mixed, probs, table, onehot, shift)


def slot_mask(window_pos):
    row_win = window_pos // NWS
    col_win = window_pos % NWS
    rows_ok = jnp.where(row_win == NWS - 1, EDGE, WIN)
    cols_ok = jnp.where(col_win == NWS - 1, EDGE, WIN)
    positions = jnp.arange(WIN, dtype=jnp.int32)
    inside = (positions[None, :, None] < rows_ok[:, None, None]) & (
        positions[None, None, :] < cols_ok[:, None, None]
    )
    return inside.reshape(-1, 1).astype(F32)


def normalise(values):
    centred = values - jnp.mean(values, axis=-1, keepdims=True)
    rstd = lax.rsqrt(jnp.mean(centred * centred, axis=-1, keepdims=True) + EPS)
    return centred * rstd, rstd


def normalise_back(grad, hat, rstd, gain):
    grad_hat = grad * gain
    return rstd * (
        grad_hat
        - jnp.mean(grad_hat, axis=-1, keepdims=True)
        - hat * jnp.mean(grad_hat * hat, axis=-1, keepdims=True)
    )


def normal_cdf(values):
    return 0.5 * (1.0 + lax.erf(values * np.float32(np.sqrt(0.5))))


def normal_pdf(values):
    return np.float32(1.0 / np.sqrt(2.0 * np.pi)) * jnp.exp(-0.5 * values * values)


def copy_rows(pieces, columns, out, to, sems):
    rows = pieces[0].shape[0]
    lo, width = columns
    return [
        pltpu.make_async_copy(
            piece.at[:, pl.ds(lo, width)],
            out.at[index * rows : (index + 1) * rows, pl.ds(to, width)],
            sems.at[index],
        )
        for index, piece in enumerate(pieces)
    ]


def start_all(copies):
    for copy in copies:
        copy.start()


def wait_all(copies):
    for copy in copies:
        copy.wait()


def front_kernel(tokens_ref, live_ref, order_ref, rows_ref, b_qkv_ref, *rest):
    pieces, (turned_ref, qkv_ref, weight, sem) = rest[:PIECES], rest[PIECES:]
    copies = [copy_rows(pieces, (block * D, D), weight, block * D, sem.at[block]) for block in range(3)]
    for block in copies:
        start_all(block)
    unit, _ = normalise(tokens_ref[...].astype(F32))
    normed = ((unit * rows_ref[0:1, :] + rows_ref[1:2, :]) * live_ref[:, :1]).astype(BF)
    turned = dot_nn(normed, order_ref[...])
    normed = turned.astype(BF)
    turned_ref[...] = turned.T.astype(BF)
    for block in range(3):
        wait_all(copies[block])
        at = block * D
        values = dot_nn(normed, weight[:, at : at + D]) + b_qkv_ref[:, at : at + D]
        qkv_ref[:, at : at + D] = values.astype(BF)


PIECES = 2
HBM = pl.BlockSpec(memory_space=pl.ANY)
VMEM = pl.BlockSpec(memory_space=pltpu.VMEM)
SMEM = pl.BlockSpec(memory_space=pltpu.SMEM)


def front(tokens, live, order, vectors, b_qkv, pieces):
    rows = tokens.shape[0]
    return pl.pallas_call(
        front_kernel,
        in_specs=[VMEM] * 5 + [HBM] * PIECES,
        out_specs=[VMEM] * 2,
        out_shape=[struct((D, rows), BF), struct((rows, 3 * D), BF)],
        scratch_shapes=[pltpu.VMEM((D, 3 * D), BF), pltpu.SemaphoreType.DMA((3, PIECES))],
        cost_estimate=QUICK,
        compiler_params=pltpu.CompilerParams(vmem_limit_bytes=KERNEL_VMEM),
        name="front",
    )(tokens, live, order, vectors, b_qkv, *pieces)


def proj_kernel(tokens_ref, values_ref, order_ref, rows_ref, *rest):
    pieces, (residual_ref, normed_ref, turned_ref, mixed_ref, w_proj, sem) = rest[:PIECES], rest[PIECES:]
    b_proj, gain, bias = (rows_ref[i : i + 1, :] for i in range(3))
    copies = copy_rows(pieces, (3 * D, D), w_proj, 0, sem)
    start_all(copies)
    mixed = dot_nn(values_ref[...], order_ref[...]).astype(BF)
    mixed_ref[...] = mixed
    wait_all(copies)
    values = tokens_ref[...].astype(F32) + dot_nn(mixed, w_proj[...]) + b_proj
    residual_ref[...] = values
    low = (normalise(values)[0] * gain + bias).astype(BF)
    low = dot_nn(low, order_ref[...])
    normed_ref[...] = low.astype(BF)
    turned_ref[...] = low.T.astype(BF)


def down_copies(pieces, owners, me_ref, weight, sems):
    copies = []
    for piece, masks in zip(pieces, owners):
        rows = piece.shape[0] // len(masks)
        for index, mask in enumerate(masks):
            to = jnp.bitwise_xor(me_ref[0], mask) * rows
            copies.append(
                pltpu.make_async_copy(
                    piece.at[index * rows : (index + 1) * rows],
                    weight.at[pl.ds(pl.multiple_of(to, rows), rows)],
                    sems.at[len(copies)],
                )
            )
    return copies


def mlp_kernel(split_rows, owners, place_ref, me_ref, *rest):
    normed_ref, turned_ref, live_ref, out_grad_ref, residual_ref, rows_ref, b_up_ref, *rest = rest
    up_pieces, rest = rest[:PIECES], rest[PIECES:]
    down_pieces, rest = rest[: len(owners)], rest[len(owners) :]
    output_ref, grad_normed_ref, kept_ref, sent_ref, grad_b_ref, *rest = rest
    if split_rows:
        kept_down_ref, sent_down_ref, *rest = rest
    else:
        grad_down_ref, *rest = rest
    branch, actives, grads, w_up, w_down, staged, sem, up_sem, down_sem = rest
    step = pl.program_id(0)
    half = D // 2

    def up_copies(index):
        return copy_rows(up_pieces, (index * TILE, TILE), w_up, index * TILE, up_sem.at[index])

    @pl.when(step == 0)
    def _():
        start_all(up_copies(0))
        start_all(down_copies(down_pieces, owners, me_ref, w_down, down_sem))
        for index in range(1, STEPS):
            start_all(up_copies(index))
        branch[...] = (out_grad_ref[...].astype(F32) * live_ref[:, :1]).astype(BF)

    wait_all(up_copies(step))
    at = pl.multiple_of(step * TILE, TILE)
    hidden = dot_nn(normed_ref[...], w_up[:, pl.ds(at, TILE)]) + b_up_ref[...]
    cdf = normal_cdf(hidden)
    active = (hidden * cdf).astype(BF)
    slope = cdf + hidden * normal_pdf(hidden)
    grad_down = dot_tn(active, branch[...]).astype(BF)

    @pl.when(step == 0)
    def _():
        wait_all(down_copies(down_pieces, owners, me_ref, w_down, down_sem))

    grad_active = dot_nt(branch[...], w_down[pl.ds(at, TILE), :])
    grad_hidden = (grad_active * slope).astype(BF)
    grad_up = dot_nn(turned_ref[...], grad_hidden).astype(BF)
    kept_ref[...] = grad_up[:half]
    sent_ref[...] = grad_up[half:]
    actives[:, pl.ds(at, TILE)] = active
    grads[:, pl.ds(at, TILE)] = grad_hidden
    grad_b_ref[...] = jnp.sum(grad_hidden.astype(F32), axis=0, keepdims=True)

    def finish_sums():
        grad_normed_ref[...] = dot_nt(grads[...], w_up[...])
        total = residual_ref[...] + rows_ref[3:4, :] + dot_nn(actives[...], w_down[...])
        output_ref[...] = (total * live_ref[:, :1]).astype(BF)

    if not split_rows:
        grad_down_ref[...] = grad_down
        pl.when(step == STEPS - 1)(finish_sums)
        return

    slot = lax.rem(step, 2)
    blocks = staged.shape[1]

    def copy(slot, block, out, to):
        return pltpu.make_async_copy(staged.at[slot, block], out.at[to], sem.at[slot, block])

    @pl.when(step >= 2)
    def _():
        for block in range(blocks):
            copy(slot, block, kept_down_ref, 0).wait()

    staged[slot] = grad_down.reshape(blocks, split_rows, D)
    places = kept_down_ref.shape[0]
    for block in range(blocks):
        to = place_ref[step * blocks + block]

        @pl.when(to < places)
        def _():
            copy(slot, block, kept_down_ref, to).start()

        @pl.when(to >= places)
        def _():
            copy(slot, block, sent_down_ref, to - places).start()

    @pl.when(step == STEPS - 1)
    def _():
        finish_sums()
        for last_slot in range(2):
            for block in range(blocks):
                copy(last_slot, block, kept_down_ref, 0).wait()


def second_norm_kernel(
    grad_normed_ref, residual_ref, mixed_ref, live_ref, out_grad_ref, order_ref, rows_ref, *rest
):
    pieces, rest = rest[:PIECES], rest[PIECES:]
    grad_residual_ref, grad_mixed_ref, *rest = rest
    kept_proj_ref, sent_proj_ref, sums_ref, w_proj, sem = rest
    half = D // 2
    copies = copy_rows(pieces, (3 * D, D), w_proj, 0, sem)
    start_all(copies)
    grad = natural_order(grad_normed_ref[...], order_ref[...])
    unit, rstd = normalise(residual_ref[...])
    grad_out = out_grad_ref[...].astype(F32) * live_ref[:, :1]
    grad_residual = grad_out + normalise_back(grad, unit, rstd, rows_ref[1:2, :])
    grad_residual_ref[...] = grad_residual
    grad_attn = grad_residual.astype(BF)
    wait_all(copies)
    grad_mixed = dot_nt(grad_attn, w_proj[...]).astype(BF)
    grad_mixed_ref[...] = dot_nt(grad_mixed, order_ref[...]).astype(BF)
    sent_proj_ref[...] = dot_tn(mixed_ref[:, half:], grad_attn).astype(BF)
    kept_proj_ref[...] = dot_tn(mixed_ref[:, :half], grad_attn).astype(BF)
    sums_ref[0:1, :] = jnp.sum(grad_attn.astype(F32), axis=0, keepdims=True)
    sums_ref[1:2, :] = jnp.sum(grad * unit, axis=0, keepdims=True)
    sums_ref[2:3, :] = jnp.sum(grad, axis=0, keepdims=True)
    sums_ref[3:4, :] = jnp.sum(grad_out.astype(BF).astype(F32), axis=0, keepdims=True)
    sums_ref[4:, :] = jnp.zeros((4, D), F32)


def natural_order(values, order):
    top = values.astype(BF).astype(F32)
    rows = values.shape[0]
    both = dot_nt(jnp.concatenate((top, values - top), axis=0).astype(BF), order)
    return both[:rows] + both[rows:]


TILE = 768
STEPS = FF // TILE


def whole(*shape):
    return pl.BlockSpec(shape, lambda step: (0,) * len(shape))


def struct(shape, dtype):
    return jax.ShapeDtypeStruct(shape, dtype)


def project(tokens, mixed, order, vectors, pieces):
    rows = tokens.shape[0]
    return pl.pallas_call(
        proj_kernel,
        in_specs=[VMEM] * 4 + [HBM] * PIECES,
        out_specs=[VMEM] * 4,
        out_shape=[
            struct((rows, D), F32),
            struct((rows, D), BF),
            struct((D, rows), BF),
            struct((rows, D), BF),
        ],
        scratch_shapes=[pltpu.VMEM((D, D), BF), pltpu.SemaphoreType.DMA((PIECES,))],
        cost_estimate=QUICK,
        compiler_params=pltpu.CompilerParams(vmem_limit_bytes=KERNEL_VMEM),
        name="project",
    )(tokens, mixed, order, vectors, *pieces)


def placed_down(pieces, me, count):
    if FF // count % 16:
        return place(pieces, ((0, 0, D, 0),), (D,), me, count), ((0,),), jnp.zeros((1,), jnp.int32)
    owners = tuple(tuple(masks) for _, masks in pieces)
    return [stack.reshape(-1, D) for stack, _ in pieces], owners, me.reshape(1)


def mlp(
    me, count, places, normed, turned, live, out_grad, residual, vectors, b_up, up_pieces, down
):
    rows = normed.shape[0]
    block_rows = FF // count
    split_rows = block_rows if block_rows % 16 == 0 else 0
    down_pieces, owners, me_down = down
    column = lambda height: pl.BlockSpec((height, TILE), lambda step: (0, step))
    if split_rows:
        half = struct((count // 2, block_rows, D), BF)
        grad_specs, grad_shapes = [HBM] * 2, [half, half]
        staged = (2, TILE // block_rows, block_rows, D)
    else:
        grad_specs = [pl.BlockSpec((TILE, D), lambda step: (step, 0))]
        grad_shapes = [struct((FF, D), BF)]
        staged = (2, 1, 16, 128)
    wide = (rows, D)
    results = pl.pallas_call(
        functools.partial(mlp_kernel, split_rows, owners),
        grid=(STEPS,),
        in_specs=[SMEM, SMEM, whole(*wide), whole(D, rows), whole(rows, 128)]
        + [whole(*wide), whole(*wide), whole(4, D), column(1)]
        + [HBM] * (len(up_pieces) + len(down_pieces)),
        out_specs=[whole(*wide), whole(*wide), column(D // 2), column(D // 2), column(1)]
        + grad_specs,
        out_shape=[
            struct(wide, BF),
            struct(wide, F32),
            struct((D // 2, FF), BF),
            struct((D // 2, FF), BF),
            struct((1, FF), F32),
        ]
        + grad_shapes,
        scratch_shapes=[
            pltpu.VMEM(wide, BF),
            pltpu.VMEM((rows, FF), BF),
            pltpu.VMEM((rows, FF), BF),
            pltpu.VMEM((D, FF), BF),
            pltpu.VMEM((FF, D), BF),
            pltpu.VMEM(staged, BF),
            pltpu.SemaphoreType.DMA(staged[:2]),
            pltpu.SemaphoreType.DMA((STEPS, PIECES)),
            pltpu.SemaphoreType.DMA((sum(map(len, owners)),)),
        ],
        cost_estimate=QUICK,
        compiler_params=pltpu.CompilerParams(vmem_limit_bytes=KERNEL_VMEM),
        name="mlp",
    )(
        places,
        me_down,
        normed,
        turned,
        live,
        out_grad,
        residual,
        vectors,
        b_up,
        *up_pieces,
        *down_pieces,
    )
    parts = results[5:] if split_rows else pick(results[5], me, count)
    return tuple(results[:5]) + (tuple(parts),)


def second_norm_back(grad_normed, residual, mixed, live, out_grad, order, vectors, pieces):
    rows = residual.shape[0]
    return pl.pallas_call(
        second_norm_kernel,
        in_specs=[VMEM] * 7 + [HBM] * PIECES,
        out_specs=[VMEM] * 5,
        out_shape=[
            struct((rows, D), F32),
            struct((rows, D), BF),
            struct((D // 2, D), BF),
            struct((D // 2, D), BF),
            struct((8, D), F32),
        ],
        scratch_shapes=[pltpu.VMEM((D, D), BF), pltpu.SemaphoreType.DMA((PIECES,))],
        cost_estimate=QUICK,
        compiler_params=pltpu.CompilerParams(vmem_limit_bytes=KERNEL_VMEM),
        name="second_norm_back",
    )(grad_normed, residual, mixed, live, out_grad, order, vectors, *pieces)


def marker_kernel(value_ref, out_ref):
    out_ref[...] = value_ref[...]


def marker(value):
    return pl.pallas_call(
        marker_kernel,
        in_specs=[VMEM],
        out_specs=VMEM,
        out_shape=struct(value.shape, value.dtype),
        cost_estimate=LONG,
        name="marker",
    )(value)


def join_kernel(sizes, *refs):
    ins, (*outs, sems) = refs[: sum(map(len, sizes))], refs[sum(map(len, sizes)) : -len(sizes)]
    spaces = refs[-len(sizes) :]
    inward, outward = [], []
    ins = list(ins)
    for out, space, parts in zip(outs, spaces, sizes):
        at = 0
        for size in parts:
            number = len(inward)
            to = pl.ds(at, size)
            inward.append(pltpu.make_async_copy(ins.pop(0), space.at[to], sems.at[0, number]))
            outward.append(pltpu.make_async_copy(space.at[to], out.at[to], sems.at[1, number]))
            inward[-1].start()
            at += size
    for first, second in zip(inward, outward):
        first.wait()
        second.start()
    wait_all(outward)


def join(groups):
    arrays = [array for group in groups for array in group]
    sizes = tuple(tuple(array.shape[0] for array in group) for group in groups)
    shapes = [(sum(parts),) + group[0].shape[1:] for parts, group in zip(sizes, groups)]
    results = pl.pallas_call(
        functools.partial(join_kernel, sizes),
        in_specs=[HBM] * len(arrays),
        out_specs=[HBM] * len(groups),
        out_shape=[struct(shape, BF) for shape in shapes],
        scratch_shapes=[pltpu.SemaphoreType.DMA((2, len(arrays)))]
        + [pltpu.VMEM(shape, BF) for shape in shapes],
        cost_estimate=QUICK,
        compiler_params=pltpu.CompilerParams(vmem_limit_bytes=KERNEL_VMEM),
        name="join",
    )(*arrays)
    return list(results)


def weight_kernel(turned_ref, grad_ref, kept_ref, sent_ref):
    total = dot_nn(turned_ref[...], grad_ref[...]).astype(BF)
    kept_ref[...] = total[: D // 2]
    sent_ref[...] = total[D // 2 :]


def weight_grad(turned, grad):
    rows, width = grad.shape
    column = lambda height: pl.BlockSpec((height, D), lambda step: (0, step))
    return pl.pallas_call(
        weight_kernel,
        grid=(width // D,),
        in_specs=[whole(D, rows), column(rows)],
        out_specs=[column(D // 2)] * 2,
        out_shape=[struct((D // 2, width), BF)] * 2,
        cost_estimate=QUICK,
        compiler_params=pltpu.CompilerParams(vmem_limit_bytes=KERNEL_VMEM),
        name="weight_grad",
    )(turned, grad)


def add_kernel(widths, outputs, *refs):
    count = sum(map(len, widths)) * 2
    ins, outs, (in_sem, out_sem, *spaces) = (
        refs[:count],
        refs[count : count + len(outputs)],
        refs[count + len(outputs) :],
    )
    firsts = np.cumsum([0] + [len(parts) for parts in widths])
    loads, stores = [], []
    for number, ranges in enumerate(outputs):
        here, below = [], 0
        for group, lo, hi in ranges:
            at = 0
            for part, width in enumerate(widths[group]):
                for side in range(2):
                    source = ins[2 * (firsts[group] + part) + side].at[lo:hi]
                    space = spaces[2 * number + side]
                    to = space.at[below : below + hi - lo, at : at + width]
                    sem = in_sem.at[number, len(here)]
                    here.append(pltpu.make_async_copy(source, to, sem))
                at += width
            below += hi - lo
        start_all(here)
        loads.append(here)
    for number in range(len(outputs)):
        wait_all(loads[number])
        left, right = spaces[2 * number], spaces[2 * number + 1]
        left[...] = (left[...].astype(F32) + right[...].astype(F32)).astype(BF)
        stores.append(pltpu.make_async_copy(left, outs[number], out_sem.at[number]))
        stores[-1].start()
    wait_all(stores)


def add_ranges(groups, outputs, cost):
    rows = groups[0][0][0].shape[1]
    flat = [side.reshape(-1, side.shape[-1]) for group in groups for pair in group for side in pair]
    widths = tuple(tuple(pair[0].shape[-1] for pair in group) for group in groups)
    plan = tuple(tuple((g, lo * rows, hi * rows) for g, lo, hi in ranges) for ranges in outputs)
    shapes = [(sum(hi - lo for _, lo, hi in r), sum(widths[r[0][0]])) for r in plan]
    most = max(sum(2 * len(widths[g]) for g, _, _ in ranges) for ranges in plan)
    results = pl.pallas_call(
        functools.partial(add_kernel, widths, plan),
        in_specs=[HBM] * len(flat),
        out_specs=[HBM] * len(plan),
        out_shape=[struct(shape, BF) for shape in shapes],
        scratch_shapes=[
            pltpu.SemaphoreType.DMA((len(plan), most)),
            pltpu.SemaphoreType.DMA((len(plan),)),
        ]
        + [pltpu.VMEM(shape, BF) for shape in shapes for _ in range(2)],
        cost_estimate=cost,
        compiler_params=pltpu.CompilerParams(vmem_limit_bytes=KERNEL_VMEM),
        name="add_ranges",
    )(*flat)
    return [r.reshape(-1, rows, r.shape[-1]) for r in results]


def first_norm_kernel(
    grad_ref,
    tokens_ref,
    live_ref,
    gain_ref,
    order_ref,
    grad_residual_ref,
    mlp_sums_ref,
    grad_b_ref,
    tables_ref,
    *rest,
):
    pieces, (tokens_grad_ref, sums_ref, total, columns, weight, sem) = rest[:PIECES], rest[PIECES:]
    step = pl.program_id(0)

    def copies(index):
        return copy_rows(pieces, (index * D, D), weight, index * D, sem.at[index])

    @pl.when(step == 0)
    def _():
        for index in range(3):
            start_all(copies(index))
        total[...] = jnp.zeros_like(total)

    wait_all(copies(step))
    grad_qkv = grad_ref[...]
    at = pl.multiple_of(step * D, 128)
    total[...] += dot_nt(grad_qkv, weight[:, pl.ds(at, D)])
    columns[pl.ds(step, 1), :] = jnp.sum(grad_qkv.astype(F32), axis=0, keepdims=True)

    @pl.when(step == 2)
    def _():
        unit, rstd = normalise(tokens_ref[...].astype(F32))
        grad = natural_order(total[...], order_ref[...]) * live_ref[:, :1]
        tokens_grad_ref[...] = (
            grad_residual_ref[...] + normalise_back(grad, unit, rstd, gain_ref[...])
        ).astype(BF)
        vectors = [
            [jnp.sum(grad * unit, axis=0, keepdims=True)],
            [jnp.sum(grad, axis=0, keepdims=True)],
            [columns[block : block + 1, :] for block in range(3)],
            [mlp_sums_ref[0:1, :]],
            [mlp_sums_ref[1:2, :]],
            [mlp_sums_ref[2:3, :]],
            [grad_b_ref[...]],
            [mlp_sums_ref[3:4, :]],
        ]
        at = 0
        for vector in vectors:
            for piece in vector:
                for lane in range(0, piece.shape[1], 128):
                    sums_ref[at : at + 1, :] = piece[:, lane : lane + 128]
                    at += 1
        sums_ref[at:TABLE_ROW, :] = jnp.zeros((TABLE_ROW - at, 128), F32)
        tables = tables_ref[...] * (1.0 / SCALE)
        low = lax.broadcasted_iota(jnp.int32, (32, 128), 1) < 64
        sums_ref[TABLE_ROW:, :] = jnp.where(
            low,
            tables[64:96] + pltpu.roll(tables[:32], 64, 1),
            pltpu.roll(tables[96:], 64, 1) + tables[32:64],
        )


TABLE_ROW = 80
SUM_ROWS = TABLE_ROW + 32


def first_norm_back(grad_qkv, pieces, tokens, live, gain, order, grad_residual, sums, b_up, tables):
    rows = tokens.shape[0]
    return pl.pallas_call(
        first_norm_kernel,
        grid=(3,),
        in_specs=[
            pl.BlockSpec((rows, D), lambda step: (0, step)),
            whole(rows, D),
            whole(rows, 128),
            whole(1, D),
            whole(D, D),
            whole(rows, D),
            whole(8, D),
            whole(1, FF),
            whole(128, 128),
        ]
        + [HBM] * PIECES,
        out_specs=[whole(rows, D), whole(SUM_ROWS, 128)],
        out_shape=[struct((rows, D), BF), struct((SUM_ROWS, 128), F32)],
        scratch_shapes=[
            pltpu.VMEM((rows, D), F32),
            pltpu.VMEM((8, D), F32),
            pltpu.VMEM((D, 3 * D), BF),
            pltpu.SemaphoreType.DMA((3, PIECES)),
        ],
        cost_estimate=QUICK,
        compiler_params=pltpu.CompilerParams(vmem_limit_bytes=KERNEL_VMEM),
        name="first_norm_back",
    )(grad_qkv, tokens, live, gain, order, grad_residual, sums, b_up, tables, *pieces)


def own_kernel(sizes, me_ref, sums_ref, *refs):
    outs, (table_h_ref, table_w_ref) = refs[:-2], refs[-2:]
    lane = lax.broadcasted_iota(jnp.int32, (1, 128), 1)
    row = 0
    for size, whole_size, out in zip(sizes, WHOLE_SIZES, outs):
        start = me_ref[0] * size
        at, shift = row + start // 128, lax.rem(start, 128)
        here = pltpu.roll(sums_ref[pl.ds(at, 1), :], lax.rem(128 - shift, 128), 1)
        there = pltpu.roll(sums_ref[pl.ds(at + 1, 1), :], lax.rem(128 - shift, 128), 1)
        out[...] = jnp.where(lane + shift < 128, here, there)[:, :size]
        row += whole_size // 128
    count = 2 * WIN - 1
    table_h_ref[...] = sums_ref[TABLE_ROW : TABLE_ROW + count, :HEAD_DIM]
    table_w_ref[...] = pltpu.roll(sums_ref[TABLE_ROW:, :], 64, 1)[:count, :HEAD_DIM]


WHOLE_SIZES = (D, D, 3 * D, D, D, D, FF, D)


def own_small(sums, me, sizes):
    table = struct((2 * WIN - 1, HEAD_DIM), F32)
    return pl.pallas_call(
        functools.partial(own_kernel, tuple(sizes)),
        in_specs=[
            pl.BlockSpec(memory_space=pltpu.SMEM),
            pl.BlockSpec(memory_space=pltpu.VMEM),
        ],
        out_specs=[pl.BlockSpec(memory_space=pltpu.VMEM)] * (len(sizes) + 2),
        out_shape=[struct((1, size), F32) for size in sizes] + [table, table],
        name="own_small",
    )(me.reshape(1), sums)


def hop(array, mask, count):
    return lax.ppermute(array, "fsdp", [(i, i ^ mask) for i in range(count)])


def hop_plan(count):
    far = count // 4
    return 2 * far, far, [1 << bit for bit in range(1, far.bit_length() - 1)]


def after(values, deps):
    if not deps:
        return list(values)
    return list(lax.optimization_barrier(tuple(values) + tuple(deps))[: len(values)])


def gather_stages(shard, count, pieces, early=False):
    farthest, far, middle = hop_plan(count)
    deps = yield
    (shard,) = after([shard], deps)
    got = hop(shard, farthest, count)
    deps = yield [shard]
    (got,) = after([got], deps)
    near = jnp.stack((shard, got))
    got = hop(near, far, count)
    deps = yield [near]
    (got,) = after([got], deps)
    stacks = [near, got]
    for masks in zip(middle, middle[::-1]):
        got = [hop(stack, mask, count) for stack, mask in zip(stacks, masks)]
        deps = yield stacks
        got = after(got, deps or stacks)
        if masks[0] != middle[-1]:
            pairs = list(zip(stacks, got))
            stacks = [jnp.concatenate(p, axis=0) for p in pairs] if early else join(pairs)
    (own,) = join([(stacks[0], got[0], stacks[1], got[1])])
    other = hop(own, 1, count)
    order = sum_order(count)
    pieces += [(own, order[: count // 2]), (other, order[count // 2 :])]
    yield [own]


def start(stages):
    next(stages)
    return stages


def finish(stages):
    for _ in stages:
        pass


def place_kernel(owners, columns, me_ref, *refs):
    stacks, outs, sem = refs[: len(owners)], refs[len(owners) : -1], refs[-1]
    copies = []
    for stack, stack_owners in zip(stacks, owners):
        for index, mask in enumerate(stack_owners):
            owner = jnp.bitwise_xor(me_ref[0], mask)
            for out, lo, hi, to in columns:
                copies.append(
                    pltpu.make_async_copy(
                        stack.at[index, :, lo:hi],
                        outs[out].at[owner, :, to : to + hi - lo],
                        sem.at[len(copies)],
                    )
                )
                copies[-1].start()
    for copy in copies:
        copy.wait()


def place(pieces, columns, widths, me, count):
    stacks = [stack for stack, _ in pieces]
    rows = stacks[0].shape[1]
    outs = pl.pallas_call(
        functools.partial(place_kernel, tuple(tuple(o) for _, o in pieces), columns),
        in_specs=[pl.BlockSpec(memory_space=pltpu.SMEM)]
        + [pl.BlockSpec(memory_space=pl.ANY)] * len(stacks),
        out_specs=[pl.BlockSpec(memory_space=pltpu.VMEM)] * len(widths),
        out_shape=[jax.ShapeDtypeStruct((count, rows, width), BF) for width in widths],
        scratch_shapes=[pltpu.SemaphoreType.DMA((count * len(columns),))],
        cost_estimate=QUICK,
        compiler_params=pltpu.CompilerParams(vmem_limit_bytes=KERNEL_VMEM),
        name="place",
    )(me.reshape(1), *stacks)
    return [out.reshape(count * rows, width) for out, width in zip(outs, widths)]


def sum_order(count):
    farthest, far, middle = hop_plan(count)
    order = []
    for masks, block in ((middle, [0, farthest]), (middle[::-1], [far, far ^ farthest])):
        for mask in masks:
            block = block + [owner ^ mask for owner in block]
        order += block
    return order + [owner ^ 1 for owner in order]


def order_matrix(me, count, rows):
    masks = np.repeat(np.array(sum_order(count), np.int32), rows)
    wanted = jnp.bitwise_xor(me, masks) * rows + np.tile(np.arange(rows, dtype=np.int32), count)
    features = lax.broadcasted_iota(jnp.int32, (count * rows, count * rows), 0)
    return (features == wanted[None, :]).astype(BF)


def pick_kernel(masks, me_ref, stack, kept, sent, sem):
    half = len(masks) // 2
    copies = []
    for index, mask in enumerate(masks):
        owner = jnp.bitwise_xor(me_ref[0], mask)
        out = kept if index < half else sent
        copies.append(
            pltpu.make_async_copy(stack.at[owner], out.at[index % half], sem.at[index])
        )
        copies[-1].start()
    for copy in copies:
        copy.wait()


def pick(array, me, count):
    stack = array.reshape(count, -1, array.shape[-1])
    half = jax.ShapeDtypeStruct((count // 2,) + stack.shape[1:], BF)
    return pl.pallas_call(
        functools.partial(pick_kernel, tuple(sum_order(count))),
        in_specs=[
            pl.BlockSpec(memory_space=pltpu.SMEM),
            pl.BlockSpec(memory_space=pl.ANY),
        ],
        out_specs=[pl.BlockSpec(memory_space=pltpu.VMEM)] * 2,
        out_shape=[half, half],
        scratch_shapes=[pltpu.SemaphoreType.DMA((count,))],
        cost_estimate=QUICK,
        compiler_params=pltpu.CompilerParams(vmem_limit_bytes=16 * 1024 * 1024),
        name="pick",
    )(me.reshape(1), stack)


def add_low(left, right):
    return (left.astype(F32) + right.astype(F32)).astype(BF)


def scatter_stages(parts, count, result, late=(), direct=False, inbox=None, costs=()):
    farthest, far, middle = hop_plan(count)
    blocks = count // 2
    half = blocks // 2
    shape = lambda side: side.reshape(blocks, -1, side.shape[-1])
    kept, sent = [shape(k) for k, _ in parts], [shape(s) for _, s in parts]
    deps = yield
    sent = after(sent, deps)
    arrived = [hop(side, 1, count) for side in sent]
    deps = yield sent
    arrived = after(arrived, deps)
    pairs = list(zip(kept, arrived)) + [(shape(k), shape(got)) for k, got in late]

    costs = list(costs)

    def added(groups, outputs):
        cost = costs.pop(0) if costs else QUICK
        rows = groups[0][0][0].shape[1]
        if all(lo * rows % 16 == 0 and hi * rows % 16 == 0 for o in outputs for _, lo, hi in o):
            return add_ranges(groups, outputs, cost)
        return [
            jnp.concatenate(
                [
                    jnp.concatenate([add_low(a[lo:hi], b[lo:hi]) for a, b in groups[g]], axis=-1)
                    for g, lo, hi in ranges
                ],
                axis=0,
            )
            for ranges in outputs
        ]

    groups, size = [pairs], half
    for masks in zip(middle[::-1], middle):
        size //= 2
        at = [(0, 0), (0, half)] if len(groups) == 1 else [(0, 0), (1, 0)]
        *sends, near, back = added(
            groups,
            [[(group, lo + size, lo + 2 * size)] for group, lo in at]
            + [[(group, lo, lo + size)] for group, lo in at],
        )
        got = [hop(send, mask, count) for send, mask in zip(sends, masks)]
        if inbox is not None:
            inbox[:] = got
        deps = yield sends
        got = after(got, deps)
        groups = [[(near, got[0])], [(back, got[1])]]
    if direct:
        near, back = (a.astype(F32) + b.astype(F32) for ((a, b),) in groups)
        sends = [block.astype(BF) for block in (near[1], back[0], back[1])]
        got = [hop(s, m, count) for s, m in zip(sends, (farthest, far, far ^ farthest))]
        deps = yield sends
        got = after(got, deps)
        total = near[0] + got[0].astype(F32) + got[1].astype(F32) + got[2].astype(F32)
        result.append(total)
        yield [total]
        return
    send, kept = added(groups, [[(1, 0, 2)], [(0, 0, 2)]])
    got = hop(send, far, count)
    deps = yield [send]
    (got,) = after([got], deps)
    send = add_low(kept[1], got[1])
    arrived = hop(send, farthest, count)
    deps = yield [send]
    (arrived,) = after([arrived], deps)
    total = kept[0].astype(F32) + got[0].astype(F32) + arrived.astype(F32)
    result.append(total)
    yield [total]


def sum_stages(array, count, result):
    bits = count.bit_length() - 1
    deps = yield
    for mask in [1 << bit for bit in [bits - 2, bits - 1, 0] + list(range(1, bits - 2))]:
        (array,) = after([array], deps)
        got = hop(array, mask, count)
        deps = yield [array]
        (got,) = after([got], deps)
        array = array + got
    result.append(array)
    yield [array]


def per_device(
    tokens,
    window_pos,
    norm1_gain,
    norm1_bias,
    qkv_weight,
    qkv_bias,
    rel_pos_h,
    rel_pos_w,
    proj_weight,
    proj_bias,
    norm2_gain,
    norm2_bias,
    lin1_weight,
    lin1_bias,
    lin2_weight,
    lin2_bias,
    out_grad,
):
    vectors = (
        norm1_gain,
        norm1_bias,
        qkv_bias,
        proj_bias,
        norm2_gain,
        norm2_bias,
        lin1_bias,
        lin2_bias,
    )
    sizes = [v.shape[0] for v in vectors]
    used = sum(sizes)
    shard_rows = qkv_weight.shape[0]
    count = lax.axis_size("fsdp")
    me = lax.axis_index("fsdp")

    packed = lax.optimization_barrier(jnp.concatenate(vectors))
    packed = jnp.pad(packed, (0, shard_rows * 128 - used)).reshape(shard_rows, 128)
    middle = len(hop_plan(count)[2])
    first_pieces, second_pieces, third_pieces = [], [], []
    first = start(
        gather_stages(
            jnp.concatenate((qkv_weight, proj_weight, packed), axis=1).astype(BF), count, first_pieces, early=True
        )
    )
    second = start(gather_stages(lin1_weight.astype(BF), count, second_pieces))
    third = start(gather_stages(lin2_weight.astype(BF), count, third_pieces))
    onehot, shift = window_constants()
    onehot = jnp.asarray(onehot, BF)
    shift = jnp.asarray(shift)
    order = order_matrix(me, count, shard_rows)
    table = table_lanes(rel_pos_h, rel_pos_w)
    live = jnp.broadcast_to(slot_mask(window_pos), (tokens.shape[0], 128))
    inverse = np.argsort(np.array(sum_order(count)))
    places = jnp.take(jnp.asarray(inverse, jnp.int32), jnp.bitwise_xor(me, np.arange(count)))
    first.send(None)
    sent = first.send(None)
    first.send(None)
    second.send(sent)
    third.send(sent)
    for _ in range(middle - 1):
        sent = first.send(None)
    sent = second.send(sent) + third.send(sent)
    sent = second.send(sent) + third.send(sent)
    first.send(sent + [order, table, live, places])

    (small,) = place(
        first_pieces, ((0, 4 * D, 4 * D + 128, 0),), (128,), me, count
    )
    small = small.reshape(count, shard_rows * 128)[:, :used].astype(F32)
    edges = np.cumsum([0] + sizes)
    gain_one, bias_one, b_qkv, b_proj, gain_two, bias_two, b_up, b_down = (
        small[:, lo:hi].reshape(-1) for lo, hi in zip(edges[:-1], edges[1:])
    )
    flat = lambda pieces: [stack.reshape(-1, stack.shape[-1]) for stack, _ in pieces]
    first_pieces = flat(first_pieces)
    (gated_tokens,) = after([tokens], sent)
    turned_one, qkv = front(
        gated_tokens, live, order, jnp.stack((gain_one, bias_one)), b_qkv.reshape(1, -1), first_pieces
    )
    sent = [turned_one]
    for _ in range(middle - 1):
        sent = second.send(sent) + third.send(sent)
    (qkv,) = after([qkv], sent)
    mixed, probs = attention(qkv, table, onehot, shift)
    sent = third.send([mixed])
    b_up = b_up.reshape(1, FF)
    (mixed,) = after([mixed], sent + [b_up])
    vectors = jnp.stack((b_proj, gain_two, bias_two, b_down))
    residual, normed_two, turned_two, ordered_mixed = project(
        tokens, mixed, order, vectors, first_pieces
    )
    second.send([residual])

    own_down, own_up, own_third, all_small = [], [], [], []
    down_weight = placed_down(third_pieces, me, count)
    output, grad_normed, kept_up, sent_up, grad_b_up, down_parts = mlp(
        me,
        count,
        places,
        normed_two,
        turned_two,
        live,
        out_grad,
        residual,
        vectors,
        b_up,
        flat(second_pieces),
        down_weight,
    )
    late, got_up, got_down = [], [], []
    up = start(scatter_stages([(kept_up, sent_up)], count, own_up, late, inbox=got_up))
    down = start(
        scatter_stages([down_parts], count, own_down, inbox=got_down, costs=(QUICK, LONG))
    )
    sent = up.send(None)
    sent = down.send(sent)
    (grad_normed,) = after([grad_normed], sent)
    grad_residual, grad_mixed, kept_proj, sent_proj, mlp_sums = second_norm_back(
        grad_normed, residual, ordered_mixed, live, out_grad, order, vectors, first_pieces
    )
    late.append((kept_proj, hop(sent_proj, 1, count)))
    sent = up.send([grad_mixed])
    sent = down.send(sent)
    (grad_mixed,) = after([grad_mixed], sent)
    grad_qkv, tables = attention_back(qkv, grad_mixed, probs, table, onehot, shift)
    sent = [grad_qkv]
    for _ in range(middle - 1):
        sent = up.send(sent)
    (grad_qkv,) = after([grad_qkv], sent)
    kept_qkv, sent_qkv = weight_grad(turned_one, grad_qkv)
    third_sum = start(scatter_stages([(kept_qkv, sent_qkv)], count, own_third, direct=True))
    sent = third_sum.send(None)
    (grad_qkv,) = after([grad_qkv], sent)
    tokens_grad, small_sums = first_norm_back(
        grad_qkv,
        first_pieces,
        tokens,
        live,
        gain_one.reshape(1, D),
        order,
        grad_residual,
        mlp_sums,
        grad_b_up,
        tables,
    )
    small_stages = start(sum_stages(small_sums, count, all_small))
    sent = small_stages.send(None)
    for _ in range(middle - 1):
        sent = down.send([small_sums] + sent + got_up)
    sent = third_sum.send(sent)
    sent = up.send(sent)
    (gated_tables,) = after([tables], sent)
    sent = [marker(gated_tables)]
    sent = small_stages.send(sent)
    sent = down.send(sent)
    for _ in range(middle - 1):
        sent = third_sum.send(sent)
    sent = up.send(sent)
    sent = small_stages.send(sent)
    sent = third_sum.send(sent)
    sent = small_stages.send(sent)
    sent = down.send(sent)
    sent = small_stages.send(sent)
    sent = up.send(sent)
    for stages in (down, up, third_sum, small_stages):
        finish(stages)
    own_qkv, own_proj = own_third[0], own_up[0][:, FF:]
    *owned, table_h, table_w = own_small(all_small[0], me, sizes)
    owned = [vector.reshape(-1) for vector in owned]

    return (
        output,
        tokens_grad,
        owned[0],
        owned[1],
        own_qkv,
        owned[2],
        table_h,
        table_w,
        own_proj,
        owned[3],
        owned[4],
        owned[5],
        own_up[0][:, :FF],
        owned[6],
        own_down[0],
        owned[7],
    )


def solution(mesh):
    rows = P("fsdp", None)
    line = P("fsdp")
    return jax.shard_map(
        per_device,
        mesh=mesh,
        in_specs=(
            rows,
            line,
            line,
            line,
            rows,
            line,
            P(),
            P(),
            rows,
            line,
            line,
            line,
            rows,
            line,
            rows,
            line,
            rows,
        ),
        out_specs=(
            rows,
            rows,
            line,
            line,
            rows,
            line,
            P(),
            P(),
            rows,
            line,
            line,
            line,
            rows,
            line,
            rows,
            line,
        ),
        check_vma=False,
    )
```

```python
import functools

import jax
import jax.numpy as jnp
import numpy as np
from jax import lax
from jax.experimental import pallas as pl
from jax.experimental.pallas import tpu as pltpu
from jax.sharding import PartitionSpec as P

D = 768
HEADS = 12
HEAD_DIM = 64
FF = 3072
WIN = 14
NWS = 5
EDGE = 8
LENGTH = WIN * WIN
PAIRS = HEADS // 2
BLOCK = 200
SCALE = HEAD_DIM ** (-0.5)
EPS = 1e-06
ATTENTION_VMEM = 60 * 1024 * 1024
KERNEL_VMEM = 60 * 1024 * 1024
QUICK = pl.CostEstimate(flops=1, bytes_accessed=1, transcendentals=0)
LONG = pl.CostEstimate(flops=100_000_000_000, bytes_accessed=1, transcendentals=0)
LANES = 256
BF = jnp.bfloat16
F32 = jnp.float32


def window_constants():
    onehot = np.zeros((2, BLOCK, 128), np.float32)
    shift = np.zeros((2, 16, LANES), np.int32)
    for win in range(2):
        for row in range(BLOCK):
            slot = row - 4 * win
            if not 0 <= slot < LENGTH:
                onehot[win, row, 63] = onehot[win, row, 127] = -1e30
                continue
            y, x = divmod(slot, WIN)
            for base in (0, 64):
                for lane in (0, 16):
                    onehot[win, row, base + lane + WIN - 1 - y] = 1.0
                    onehot[win, row, base + 32 + lane + WIN - 1 - x] = 1.0
            shift[win, :8, row] = y
            shift[win, 8:, row] = x
    return onehot, shift


def table_lanes(rel_pos_h, rel_pos_w):
    flip = jnp.concatenate(
        (
            jnp.pad(rel_pos_h, ((0, 5), (0, 0))),
            jnp.pad(rel_pos_w, ((0, 5), (0, 0))),
        ),
        axis=0,
    ).astype(BF) * BF(1.0 / SCALE)
    nothing = jnp.zeros_like(flip)
    return jnp.concatenate(
        (jnp.concatenate((nothing, flip), axis=1), jnp.concatenate((flip, nothing), axis=1)), axis=0
    )


def dot_nn(a, b):
    return jnp.dot(a, b, preferred_element_type=F32)


def dot_nt(a, b):
    return lax.dot_general(a, b, (((1,), (1,)), ((), ())), preferred_element_type=F32)


def dot_tn(a, b):
    return lax.dot_general(a, b, (((0,), (0,)), ((), ())), preferred_element_type=F32)


def low_half():
    return lax.broadcasted_iota(jnp.int32, (BLOCK, 128), 1) < 64


def row_valid(win):
    row = lax.broadcasted_iota(jnp.int32, (BLOCK, 128), 0)
    return row < LENGTH if win == 0 else row >= BLOCK - LENGTH


def merge_windows(first, second):
    return jnp.concatenate((first[:192], first[192:] + second[:8], second[8:]), axis=0)


def pad_rows(values):
    return jnp.concatenate((values, jnp.zeros((LANES - BLOCK, 128), F32)), axis=0)


def bit_masks(shift, rows):
    shift = jnp.broadcast_to(shift[:1], (rows, LANES))
    return [(shift & (1 << bit)) != 0 for bit in range(4)]


def skew(values, masks):
    values = jnp.where(masks[3], values[8:], values[:24])
    values = jnp.where(masks[2], pltpu.roll(values, 20, 0), values)
    values = jnp.where(masks[1], pltpu.roll(values, 22, 0), values)[:16]
    return jnp.where(masks[0][:16], pltpu.roll(values, 15, 0), values)


def unskew(values, masks):
    nothing = jnp.zeros((8, LANES), F32)
    values = jnp.concatenate((values, nothing), axis=0)
    for bit in range(3):
        values = jnp.where(masks[bit], pltpu.roll(values, 1 << bit, 0), values)
    return jnp.concatenate(
        (
            jnp.where(masks[3][:8], 0.0, values[:8]),
            jnp.where(masks[3][:16], values[:16], values[8:]),
            jnp.where(masks[3][:8], values[16:], 0.0),
        ),
        axis=0,
    )


def attn_fwd_kernel(q_ref, k_ref, v_ref, table_ref, onehot_ref, shift_ref, mixed_ref, probs_ref):
    low = low_half()
    last = lax.broadcasted_iota(jnp.int32, (16, LANES), 0) == 15
    mixed = []
    for win in range(2):
        rows = pl.ds(192 * win, BLOCK)
        queries = pad_rows(q_ref[rows, :].astype(F32) * SCALE).T
        k = k_ref[rows, :].astype(F32)
        v = v_ref[rows, :].astype(F32)
        rel = dot_nn(table_ref[...], queries.astype(BF))
        onehot = onehot_ref[win].astype(F32)
        by_row = bit_masks(shift_ref[win, :8], 24)
        by_col = bit_masks(shift_ref[win, 8:], 24)
        halves = []
        for head in range(2):
            base = 64 if head == 0 else 0
            from_row = skew(rel[base : base + 32], by_row)
            from_col = skew(rel[base + 32 : base + 64], by_col)
            row_top = from_row.astype(BF).astype(F32)
            col_top = from_col.astype(BF).astype(F32)
            extra = (row_top, from_row - row_top, col_top, jnp.where(last, 1.0, from_col - col_top))
            if head == 0:
                left = jnp.concatenate((queries[:64],) + extra, axis=0).astype(BF)
                right = jnp.where(low, k, onehot).astype(BF)
            else:
                left = jnp.concatenate(extra + (queries[64:],), axis=0).astype(BF)
                right = jnp.where(low, onehot, k).astype(BF)
            scores = dot_nn(right, left)
            expon = jnp.exp(scores - jnp.max(scores, axis=0, keepdims=True))
            probs = expon * (1.0 / jnp.sum(expon, axis=0, keepdims=True))
            probs_ref[0, 2 * win + head] = probs
            halves.append(probs)
        values = jnp.concatenate((jnp.where(low, v, 0.0), jnp.where(low, 0.0, v)), axis=0)
        both = dot_tn(values.astype(BF), jnp.concatenate(halves, axis=0).astype(BF)).T[:BLOCK]
        mixed.append(jnp.where(row_valid(win), both, 0.0))
    mixed_ref[...] = merge_windows(*mixed).astype(BF)


def attn_bwd_kernel(
    q_ref,
    k_ref,
    v_ref,
    grad_ref,
    probs_ref,
    table_ref,
    onehot_ref,
    shift_ref,
    grad_qkv_ref,
    table_grad_ref,
):
    pair = pl.program_id(0)
    low = low_half()

    @pl.when(pair == 0)
    def _():
        table_grad_ref[...] = jnp.zeros_like(table_grad_ref)

    parts = ([], [], [])
    table_total = jnp.zeros((128, 128), F32)
    for win in range(2):
        rows = pl.ds(192 * win, BLOCK)
        q = pad_rows(q_ref[rows, :].astype(F32) * SCALE)
        k = k_ref[rows, :].astype(F32)
        v = v_ref[rows, :]
        grad = pad_rows(jnp.where(row_valid(win), grad_ref[rows, :].astype(F32), 0.0))
        wide_low = lax.broadcasted_iota(jnp.int32, (LANES, 128), 1) < 64

        def by_head(values):
            return jnp.concatenate(
                (jnp.where(wide_low, values, 0.0), jnp.where(wide_low, 0.0, values)), axis=0
            ).astype(BF)

        grads, queries = by_head(grad), by_head(q)
        q = q.astype(BF)
        onehot = onehot_ref[win].astype(F32)
        by_row = bit_masks(shift_ref[win, :8], 24)
        by_col = bit_masks(shift_ref[win, 8:], 24)
        probs = jnp.concatenate((probs_ref[0, 2 * win], probs_ref[0, 2 * win + 1]), axis=1)
        grad_probs = dot_nt(v, grads)
        row_dot = jnp.sum(probs * grad_probs, axis=0, keepdims=True)
        grad_scores = (probs * (grad_probs - row_dot)).astype(BF)
        parts[2].append(dot_nn(probs.astype(BF), grads))
        parts[1].append(dot_nn(grad_scores, queries))
        by_query, rel = [], []
        for head in range(2):
            right = (jnp.where(low, k, onehot) if head == 0 else jnp.where(low, onehot, k)).astype(BF)
            back = dot_tn(right, grad_scores[:, head * LANES : (head + 1) * LANES])
            own, base = (back[:64], 64) if head == 0 else (back[64:], 0)
            by_query.append(own)
            rel.append(unskew(back[base : base + 16], by_row))
            rel.append(unskew(back[base + 32 : base + 48], by_col))
        rel = jnp.concatenate((rel[2], rel[3], rel[0], rel[1]), axis=0)
        rel_top = rel.astype(BF).astype(F32)
        rel = jnp.concatenate((rel_top, rel - rel_top), axis=0).astype(BF)
        table = table_ref[...]
        from_rel = dot_tn(jnp.concatenate((table, table), axis=0), rel)
        table_parts = dot_nn(rel, q)
        table_total += table_parts[:128] + table_parts[128:]
        parts[0].append((jnp.concatenate(by_query, axis=0) + from_rel).T[:BLOCK] * SCALE)
    for block in range(3):
        at = pl.multiple_of(block * D + pair * 128, 128)
        grad_qkv_ref[:, pl.ds(at, 128)] = merge_windows(*parts[block]).astype(BF)
    table_grad_ref[...] += table_total


def attention_specs(rows):
    column = lambda block: pl.BlockSpec((rows, 128), lambda pair: (0, block * PAIRS + pair))
    whole = lambda *shape: pl.BlockSpec(shape, lambda pair: (0,) * len(shape))
    return (
        [column(0), column(1), column(2)],
        [whole(128, 128), whole(2, BLOCK, 128), whole(2, 16, LANES)],
        pl.BlockSpec((1, 4, BLOCK, LANES), lambda pair: (pair, 0, 0, 0)),
        whole,
    )


def attention(qkv, table, onehot, shift):
    rows = qkv.shape[0]
    columns, constants, probs_spec, _ = attention_specs(rows)
    return pl.pallas_call(
        attn_fwd_kernel,
        grid=(PAIRS,),
        in_specs=columns + constants,
        out_specs=[pl.BlockSpec((rows, 128), lambda pair: (0, pair)), probs_spec],
        out_shape=[
            jax.ShapeDtypeStruct((rows, D), BF),
            jax.ShapeDtypeStruct((PAIRS, 4, BLOCK, LANES), F32),
        ],
        cost_estimate=QUICK,
        compiler_params=pltpu.CompilerParams(vmem_limit_bytes=ATTENTION_VMEM),
        name="attention",
    )(qkv, qkv, qkv, table, onehot, shift)


def attention_back(qkv, grad_mixed, probs, table, onehot, shift):
    rows = qkv.shape[0]
    columns, constants, probs_spec, whole = attention_specs(rows)
    return pl.pallas_call(
        attn_bwd_kernel,
        grid=(PAIRS,),
        in_specs=columns + [pl.BlockSpec((rows, 128), lambda pair: (0, pair)), probs_spec]
        + constants,
        out_specs=[whole(rows, 3 * D), whole(128, 128)],
        out_shape=[
            jax.ShapeDtypeStruct((rows, 3 * D), BF),
            jax.ShapeDtypeStruct((128, 128), F32),
        ],
        cost_estimate=QUICK,
        compiler_params=pltpu.CompilerParams(vmem_limit_bytes=ATTENTION_VMEM),
        name="attention_back",
    )(qkv, qkv, qkv, grad_mixed, probs, table, onehot, shift)


def slot_mask(window_pos):
    row_win = window_pos // NWS
    col_win = window_pos % NWS
    rows_ok = jnp.where(row_win == NWS - 1, EDGE, WIN)
    cols_ok = jnp.where(col_win == NWS - 1, EDGE, WIN)
    positions = jnp.arange(WIN, dtype=jnp.int32)
    inside = (positions[None, :, None] < rows_ok[:, None, None]) & (
        positions[None, None, :] < cols_ok[:, None, None]
    )
    return inside.reshape(-1, 1).astype(F32)


def normalise(values):
    centred = values - jnp.mean(values, axis=-1, keepdims=True)
    rstd = lax.rsqrt(jnp.mean(centred * centred, axis=-1, keepdims=True) + EPS)
    return centred * rstd, rstd


def normalise_back(grad, hat, rstd, gain):
    grad_hat = grad * gain
    return rstd * (
        grad_hat
        - jnp.mean(grad_hat, axis=-1, keepdims=True)
        - hat * jnp.mean(grad_hat * hat, axis=-1, keepdims=True)
    )


def normal_cdf(values):
    return 0.5 * (1.0 + lax.erf(values * np.float32(np.sqrt(0.5))))


def normal_pdf(values):
    return np.float32(1.0 / np.sqrt(2.0 * np.pi)) * jnp.exp(-0.5 * values * values)


def copy_rows(pieces, columns, out, to, sems):
    rows = pieces[0].shape[0]
    lo, width = columns
    return [
        pltpu.make_async_copy(
            piece.at[:, pl.ds(lo, width)],
            out.at[index * rows : (index + 1) * rows, pl.ds(to, width)],
            sems.at[index],
        )
        for index, piece in enumerate(pieces)
    ]


def start_all(copies):
    for copy in copies:
        copy.start()


def wait_all(copies):
    for copy in copies:
        copy.wait()


def front_kernel(tokens_ref, live_ref, order_ref, rows_ref, b_qkv_ref, *rest):
    pieces, (turned_ref, qkv_ref, weight, sem) = rest[:PIECES], rest[PIECES:]
    copies = [copy_rows(pieces, (block * D, D), weight, block * D, sem.at[block]) for block in range(3)]
    for block in copies:
        start_all(block)
    unit, _ = normalise(tokens_ref[...].astype(F32))
    normed = ((unit * rows_ref[0:1, :] + rows_ref[1:2, :]) * live_ref[:, :1]).astype(BF)
    turned = dot_nn(normed, order_ref[...])
    normed = turned.astype(BF)
    turned_ref[...] = turned.T.astype(BF)
    for block in range(3):
        wait_all(copies[block])
        at = block * D
        values = dot_nn(normed, weight[:, at : at + D]) + b_qkv_ref[:, at : at + D]
        qkv_ref[:, at : at + D] = values.astype(BF)


PIECES = 2
HBM = pl.BlockSpec(memory_space=pl.ANY)
VMEM = pl.BlockSpec(memory_space=pltpu.VMEM)
SMEM = pl.BlockSpec(memory_space=pltpu.SMEM)


def front(tokens, live, order, vectors, b_qkv, pieces):
    rows = tokens.shape[0]
    return pl.pallas_call(
        front_kernel,
        in_specs=[VMEM] * 5 + [HBM] * PIECES,
        out_specs=[VMEM] * 2,
        out_shape=[struct((D, rows), BF), struct((rows, 3 * D), BF)],
        scratch_shapes=[pltpu.VMEM((D, 3 * D), BF), pltpu.SemaphoreType.DMA((3, PIECES))],
        cost_estimate=QUICK,
        compiler_params=pltpu.CompilerParams(vmem_limit_bytes=KERNEL_VMEM),
        name="front",
    )(tokens, live, order, vectors, b_qkv, *pieces)


def proj_kernel(tokens_ref, values_ref, order_ref, rows_ref, *rest):
    pieces, (residual_ref, normed_ref, turned_ref, mixed_ref, w_proj, sem) = rest[:PIECES], rest[PIECES:]
    b_proj, gain, bias = (rows_ref[i : i + 1, :] for i in range(3))
    copies = copy_rows(pieces, (3 * D, D), w_proj, 0, sem)
    start_all(copies)
    mixed = dot_nn(values_ref[...], order_ref[...]).astype(BF)
    mixed_ref[...] = mixed
    wait_all(copies)
    values = tokens_ref[...].astype(F32) + dot_nn(mixed, w_proj[...]) + b_proj
    residual_ref[...] = values
    low = (normalise(values)[0] * gain + bias).astype(BF)
    low = dot_nn(low, order_ref[...])
    normed_ref[...] = low.astype(BF)
    turned_ref[...] = low.T.astype(BF)


def down_copies(pieces, owners, me_ref, weight, sems):
    copies = []
    for piece, masks in zip(pieces, owners):
        rows = piece.shape[0] // len(masks)
        for index, mask in enumerate(masks):
            to = jnp.bitwise_xor(me_ref[0], mask) * rows
            copies.append(
                pltpu.make_async_copy(
                    piece.at[index * rows : (index + 1) * rows],
                    weight.at[pl.ds(pl.multiple_of(to, rows), rows)],
                    sems.at[len(copies)],
                )
            )
    return copies


def mlp_kernel(split_rows, owners, place_ref, me_ref, *rest):
    normed_ref, turned_ref, live_ref, out_grad_ref, residual_ref, rows_ref, b_up_ref, *rest = rest
    up_pieces, rest = rest[:PIECES], rest[PIECES:]
    down_pieces, rest = rest[: len(owners)], rest[len(owners) :]
    output_ref, grad_normed_ref, kept_ref, sent_ref, grad_b_ref, *rest = rest
    if split_rows:
        kept_down_ref, sent_down_ref, *rest = rest
    else:
        grad_down_ref, *rest = rest
    branch, actives, grads, w_up, w_down, staged, sem, up_sem, down_sem = rest
    step = pl.program_id(0)
    half = D // 2

    def up_copies(index):
        return copy_rows(up_pieces, (index * TILE, TILE), w_up, index * TILE, up_sem.at[index])

    @pl.when(step == 0)
    def _():
        start_all(up_copies(0))
        start_all(down_copies(down_pieces, owners, me_ref, w_down, down_sem))
        for index in range(1, STEPS):
            start_all(up_copies(index))
        branch[...] = (out_grad_ref[...].astype(F32) * live_ref[:, :1]).astype(BF)

    wait_all(up_copies(step))
    at = pl.multiple_of(step * TILE, TILE)
    hidden = dot_nn(normed_ref[...], w_up[:, pl.ds(at, TILE)]) + b_up_ref[...]
    cdf = normal_cdf(hidden)
    active = (hidden * cdf).astype(BF)
    slope = cdf + hidden * normal_pdf(hidden)
    grad_down = dot_tn(active, branch[...]).astype(BF)

    @pl.when(step == 0)
    def _():
        wait_all(down_copies(down_pieces, owners, me_ref, w_down, down_sem))

    grad_active = dot_nt(branch[...], w_down[pl.ds(at, TILE), :])
    grad_hidden = (grad_active * slope).astype(BF)
    grad_up = dot_nn(turned_ref[...], grad_hidden).astype(BF)
    kept_ref[...] = grad_up[:half]
    sent_ref[...] = grad_up[half:]
    actives[:, pl.ds(at, TILE)] = active
    grads[:, pl.ds(at, TILE)] = grad_hidden
    grad_b_ref[...] = jnp.sum(grad_hidden.astype(F32), axis=0, keepdims=True)

    def finish_sums():
        grad_normed_ref[...] = dot_nt(grads[...], w_up[...])
        total = residual_ref[...] + rows_ref[3:4, :] + dot_nn(actives[...], w_down[...])
        output_ref[...] = (total * live_ref[:, :1]).astype(BF)

    if not split_rows:
        grad_down_ref[...] = grad_down
        pl.when(step == STEPS - 1)(finish_sums)
        return

    slot = lax.rem(step, 2)
    blocks = staged.shape[1]

    def copy(slot, block, out, to):
        return pltpu.make_async_copy(staged.at[slot, block], out.at[to], sem.at[slot, block])

    @pl.when(step >= 2)
    def _():
        for block in range(blocks):
            copy(slot, block, kept_down_ref, 0).wait()

    staged[slot] = grad_down.reshape(blocks, split_rows, D)
    places = kept_down_ref.shape[0]
    for block in range(blocks):
        to = place_ref[step * blocks + block]

        @pl.when(to < places)
        def _():
            copy(slot, block, kept_down_ref, to).start()

        @pl.when(to >= places)
        def _():
            copy(slot, block, sent_down_ref, to - places).start()

    @pl.when(step == STEPS - 1)
    def _():
        finish_sums()
        for last_slot in range(2):
            for block in range(blocks):
                copy(last_slot, block, kept_down_ref, 0).wait()


def second_norm_kernel(
    grad_normed_ref, residual_ref, mixed_ref, live_ref, out_grad_ref, order_ref, rows_ref, *rest
):
    pieces, rest = rest[:PIECES], rest[PIECES:]
    grad_residual_ref, grad_mixed_ref, *rest = rest
    kept_proj_ref, sent_proj_ref, sums_ref, w_proj, sem = rest
    half = D // 2
    copies = copy_rows(pieces, (3 * D, D), w_proj, 0, sem)
    start_all(copies)
    grad = natural_order(grad_normed_ref[...], order_ref[...])
    unit, rstd = normalise(residual_ref[...])
    grad_out = out_grad_ref[...].astype(F32) * live_ref[:, :1]
    grad_residual = grad_out + normalise_back(grad, unit, rstd, rows_ref[1:2, :])
    grad_residual_ref[...] = grad_residual
    grad_attn = grad_residual.astype(BF)
    wait_all(copies)
    grad_mixed = dot_nt(grad_attn, w_proj[...]).astype(BF)
    grad_mixed_ref[...] = dot_nt(grad_mixed, order_ref[...]).astype(BF)
    sent_proj_ref[...] = dot_tn(mixed_ref[:, half:], grad_attn).astype(BF)
    kept_proj_ref[...] = dot_tn(mixed_ref[:, :half], grad_attn).astype(BF)
    sums_ref[0:1, :] = jnp.sum(grad_attn.astype(F32), axis=0, keepdims=True)
    sums_ref[1:2, :] = jnp.sum(grad * unit, axis=0, keepdims=True)
    sums_ref[2:3, :] = jnp.sum(grad, axis=0, keepdims=True)
    sums_ref[3:4, :] = jnp.sum(grad_out.astype(BF).astype(F32), axis=0, keepdims=True)
    sums_ref[4:, :] = jnp.zeros((4, D), F32)


def natural_order(values, order):
    top = values.astype(BF).astype(F32)
    rows = values.shape[0]
    both = dot_nt(jnp.concatenate((top, values - top), axis=0).astype(BF), order)
    return both[:rows] + both[rows:]


TILE = 768
STEPS = FF // TILE


def whole(*shape):
    return pl.BlockSpec(shape, lambda step: (0,) * len(shape))


def struct(shape, dtype):
    return jax.ShapeDtypeStruct(shape, dtype)


def project(tokens, mixed, order, vectors, pieces):
    rows = tokens.shape[0]
    return pl.pallas_call(
        proj_kernel,
        in_specs=[VMEM] * 4 + [HBM] * PIECES,
        out_specs=[VMEM] * 4,
        out_shape=[
            struct((rows, D), F32),
            struct((rows, D), BF),
            struct((D, rows), BF),
            struct((rows, D), BF),
        ],
        scratch_shapes=[pltpu.VMEM((D, D), BF), pltpu.SemaphoreType.DMA((PIECES,))],
        cost_estimate=QUICK,
        compiler_params=pltpu.CompilerParams(vmem_limit_bytes=KERNEL_VMEM),
        name="project",
    )(tokens, mixed, order, vectors, *pieces)


def placed_down(pieces, me, count):
    if FF // count % 16:
        return place(pieces, ((0, 0, D, 0),), (D,), me, count), ((0,),), jnp.zeros((1,), jnp.int32)
    owners = tuple(tuple(masks) for _, masks in pieces)
    return [stack.reshape(-1, D) for stack, _ in pieces], owners, me.reshape(1)


def mlp(
    me, count, places, normed, turned, live, out_grad, residual, vectors, b_up, up_pieces, down
):
    rows = normed.shape[0]
    block_rows = FF // count
    split_rows = block_rows if block_rows % 16 == 0 else 0
    down_pieces, owners, me_down = down
    column = lambda height: pl.BlockSpec((height, TILE), lambda step: (0, step))
    if split_rows:
        half = struct((count // 2, block_rows, D), BF)
        grad_specs, grad_shapes = [HBM] * 2, [half, half]
        staged = (2, TILE // block_rows, block_rows, D)
    else:
        grad_specs = [pl.BlockSpec((TILE, D), lambda step: (step, 0))]
        grad_shapes = [struct((FF, D), BF)]
        staged = (2, 1, 16, 128)
    wide = (rows, D)
    results = pl.pallas_call(
        functools.partial(mlp_kernel, split_rows, owners),
        grid=(STEPS,),
        in_specs=[SMEM, SMEM, whole(*wide), whole(D, rows), whole(rows, 128)]
        + [whole(*wide), whole(*wide), whole(4, D), column(1)]
        + [HBM] * (len(up_pieces) + len(down_pieces)),
        out_specs=[whole(*wide), whole(*wide), column(D // 2), column(D // 2), column(1)]
        + grad_specs,
        out_shape=[
            struct(wide, BF),
            struct(wide, F32),
            struct((D // 2, FF), BF),
            struct((D // 2, FF), BF),
            struct((1, FF), F32),
        ]
        + grad_shapes,
        scratch_shapes=[
            pltpu.VMEM(wide, BF),
            pltpu.VMEM((rows, FF), BF),
            pltpu.VMEM((rows, FF), BF),
            pltpu.VMEM((D, FF), BF),
            pltpu.VMEM((FF, D), BF),
            pltpu.VMEM(staged, BF),
            pltpu.SemaphoreType.DMA(staged[:2]),
            pltpu.SemaphoreType.DMA((STEPS, PIECES)),
            pltpu.SemaphoreType.DMA((sum(map(len, owners)),)),
        ],
        cost_estimate=QUICK,
        compiler_params=pltpu.CompilerParams(vmem_limit_bytes=KERNEL_VMEM),
        name="mlp",
    )(
        places,
        me_down,
        normed,
        turned,
        live,
        out_grad,
        residual,
        vectors,
        b_up,
        *up_pieces,
        *down_pieces,
    )
    parts = results[5:] if split_rows else pick(results[5], me, count)
    return tuple(results[:5]) + (tuple(parts),)


def second_norm_back(grad_normed, residual, mixed, live, out_grad, order, vectors, pieces):
    rows = residual.shape[0]
    return pl.pallas_call(
        second_norm_kernel,
        in_specs=[VMEM] * 7 + [HBM] * PIECES,
        out_specs=[VMEM] * 5,
        out_shape=[
            struct((rows, D), F32),
            struct((rows, D), BF),
            struct((D // 2, D), BF),
            struct((D // 2, D), BF),
            struct((8, D), F32),
        ],
        scratch_shapes=[pltpu.VMEM((D, D), BF), pltpu.SemaphoreType.DMA((PIECES,))],
        cost_estimate=QUICK,
        compiler_params=pltpu.CompilerParams(vmem_limit_bytes=KERNEL_VMEM),
        name="second_norm_back",
    )(grad_normed, residual, mixed, live, out_grad, order, vectors, *pieces)


def marker_kernel(value_ref, out_ref):
    out_ref[...] = value_ref[...]


def marker(value):
    return pl.pallas_call(
        marker_kernel,
        in_specs=[VMEM],
        out_specs=VMEM,
        out_shape=struct(value.shape, value.dtype),
        cost_estimate=LONG,
        name="marker",
    )(value)


def join_kernel(sizes, *refs):
    ins, (*outs, sems) = refs[: sum(map(len, sizes))], refs[sum(map(len, sizes)) : -len(sizes)]
    spaces = refs[-len(sizes) :]
    inward, outward = [], []
    ins = list(ins)
    for out, space, parts in zip(outs, spaces, sizes):
        at = 0
        for size in parts:
            number = len(inward)
            to = pl.ds(at, size)
            inward.append(pltpu.make_async_copy(ins.pop(0), space.at[to], sems.at[0, number]))
            outward.append(pltpu.make_async_copy(space.at[to], out.at[to], sems.at[1, number]))
            inward[-1].start()
            at += size
    for first, second in zip(inward, outward):
        first.wait()
        second.start()
    wait_all(outward)


def join(groups):
    arrays = [array for group in groups for array in group]
    sizes = tuple(tuple(array.shape[0] for array in group) for group in groups)
    shapes = [(sum(parts),) + group[0].shape[1:] for parts, group in zip(sizes, groups)]
    results = pl.pallas_call(
        functools.partial(join_kernel, sizes),
        in_specs=[HBM] * len(arrays),
        out_specs=[HBM] * len(groups),
        out_shape=[struct(shape, BF) for shape in shapes],
        scratch_shapes=[pltpu.SemaphoreType.DMA((2, len(arrays)))]
        + [pltpu.VMEM(shape, BF) for shape in shapes],
        cost_estimate=QUICK,
        compiler_params=pltpu.CompilerParams(vmem_limit_bytes=KERNEL_VMEM),
        name="join",
    )(*arrays)
    return list(results)


def weight_kernel(turned_ref, grad_ref, kept_ref, sent_ref):
    total = dot_nn(turned_ref[...], grad_ref[...]).astype(BF)
    kept_ref[...] = total[: D // 2]
    sent_ref[...] = total[D // 2 :]


def weight_grad(turned, grad):
    rows, width = grad.shape
    column = lambda height: pl.BlockSpec((height, D), lambda step: (0, step))
    return pl.pallas_call(
        weight_kernel,
        grid=(width // D,),
        in_specs=[whole(D, rows), column(rows)],
        out_specs=[column(D // 2)] * 2,
        out_shape=[struct((D // 2, width), BF)] * 2,
        cost_estimate=QUICK,
        compiler_params=pltpu.CompilerParams(vmem_limit_bytes=KERNEL_VMEM),
        name="weight_grad",
    )(turned, grad)


def add_kernel(widths, outputs, *refs):
    count = sum(map(len, widths)) * 2
    ins, outs, (in_sem, out_sem, *spaces) = (
        refs[:count],
        refs[count : count + len(outputs)],
        refs[count + len(outputs) :],
    )
    firsts = np.cumsum([0] + [len(parts) for parts in widths])
    loads, stores = [], []
    for number, ranges in enumerate(outputs):
        here, below = [], 0
        for group, lo, hi in ranges:
            at = 0
            for part, width in enumerate(widths[group]):
                for side in range(2):
                    source = ins[2 * (firsts[group] + part) + side].at[lo:hi]
                    space = spaces[2 * number + side]
                    to = space.at[below : below + hi - lo, at : at + width]
                    sem = in_sem.at[number, len(here)]
                    here.append(pltpu.make_async_copy(source, to, sem))
                at += width
            below += hi - lo
        start_all(here)
        loads.append(here)
    for number in range(len(outputs)):
        wait_all(loads[number])
        left, right = spaces[2 * number], spaces[2 * number + 1]
        left[...] = (left[...].astype(F32) + right[...].astype(F32)).astype(BF)
        stores.append(pltpu.make_async_copy(left, outs[number], out_sem.at[number]))
        stores[-1].start()
    wait_all(stores)


def add_ranges(groups, outputs, cost):
    rows = groups[0][0][0].shape[1]
    flat = [side.reshape(-1, side.shape[-1]) for group in groups for pair in group for side in pair]
    widths = tuple(tuple(pair[0].shape[-1] for pair in group) for group in groups)
    plan = tuple(tuple((g, lo * rows, hi * rows) for g, lo, hi in ranges) for ranges in outputs)
    shapes = [(sum(hi - lo for _, lo, hi in r), sum(widths[r[0][0]])) for r in plan]
    most = max(sum(2 * len(widths[g]) for g, _, _ in ranges) for ranges in plan)
    results = pl.pallas_call(
        functools.partial(add_kernel, widths, plan),
        in_specs=[HBM] * len(flat),
        out_specs=[HBM] * len(plan),
        out_shape=[struct(shape, BF) for shape in shapes],
        scratch_shapes=[
            pltpu.SemaphoreType.DMA((len(plan), most)),
            pltpu.SemaphoreType.DMA((len(plan),)),
        ]
        + [pltpu.VMEM(shape, BF) for shape in shapes for _ in range(2)],
        cost_estimate=cost,
        compiler_params=pltpu.CompilerParams(vmem_limit_bytes=KERNEL_VMEM),
        name="add_ranges",
    )(*flat)
    return [r.reshape(-1, rows, r.shape[-1]) for r in results]


def first_norm_kernel(
    grad_ref,
    tokens_ref,
    live_ref,
    gain_ref,
    order_ref,
    grad_residual_ref,
    mlp_sums_ref,
    grad_b_ref,
    tables_ref,
    *rest,
):
    pieces, (tokens_grad_ref, sums_ref, total, columns, weight, sem) = rest[:PIECES], rest[PIECES:]
    step = pl.program_id(0)

    def copies(index):
        return copy_rows(pieces, (index * D, D), weight, index * D, sem.at[index])

    @pl.when(step == 0)
    def _():
        for index in range(3):
            start_all(copies(index))
        total[...] = jnp.zeros_like(total)

    wait_all(copies(step))
    grad_qkv = grad_ref[...]
    at = pl.multiple_of(step * D, 128)
    total[...] += dot_nt(grad_qkv, weight[:, pl.ds(at, D)])
    columns[pl.ds(step, 1), :] = jnp.sum(grad_qkv.astype(F32), axis=0, keepdims=True)

    @pl.when(step == 2)
    def _():
        unit, rstd = normalise(tokens_ref[...].astype(F32))
        grad = natural_order(total[...], order_ref[...]) * live_ref[:, :1]
        tokens_grad_ref[...] = (
            grad_residual_ref[...] + normalise_back(grad, unit, rstd, gain_ref[...])
        ).astype(BF)
        vectors = [
            [jnp.sum(grad * unit, axis=0, keepdims=True)],
            [jnp.sum(grad, axis=0, keepdims=True)],
            [columns[block : block + 1, :] for block in range(3)],
            [mlp_sums_ref[0:1, :]],
            [mlp_sums_ref[1:2, :]],
            [mlp_sums_ref[2:3, :]],
            [grad_b_ref[...]],
            [mlp_sums_ref[3:4, :]],
        ]
        at = 0
        for vector in vectors:
            for piece in vector:
                for lane in range(0, piece.shape[1], 128):
                    sums_ref[at : at + 1, :] = piece[:, lane : lane + 128]
                    at += 1
        sums_ref[at:TABLE_ROW, :] = jnp.zeros((TABLE_ROW - at, 128), F32)
        tables = tables_ref[...] * (1.0 / SCALE)
        low = lax.broadcasted_iota(jnp.int32, (32, 128), 1) < 64
        sums_ref[TABLE_ROW:, :] = jnp.where(
            low,
            tables[64:96] + pltpu.roll(tables[:32], 64, 1),
            pltpu.roll(tables[96:], 64, 1) + tables[32:64],
        )


TABLE_ROW = 80
SUM_ROWS = TABLE_ROW + 32


def first_norm_back(grad_qkv, pieces, tokens, live, gain, order, grad_residual, sums, b_up, tables):
    rows = tokens.shape[0]
    return pl.pallas_call(
        first_norm_kernel,
        grid=(3,),
        in_specs=[
            pl.BlockSpec((rows, D), lambda step: (0, step)),
            whole(rows, D),
            whole(rows, 128),
            whole(1, D),
            whole(D, D),
            whole(rows, D),
            whole(8, D),
            whole(1, FF),
            whole(128, 128),
        ]
        + [HBM] * PIECES,
        out_specs=[whole(rows, D), whole(SUM_ROWS, 128)],
        out_shape=[struct((rows, D), BF), struct((SUM_ROWS, 128), F32)],
        scratch_shapes=[
            pltpu.VMEM((rows, D), F32),
            pltpu.VMEM((8, D), F32),
            pltpu.VMEM((D, 3 * D), BF),
            pltpu.SemaphoreType.DMA((3, PIECES)),
        ],
        cost_estimate=QUICK,
        compiler_params=pltpu.CompilerParams(vmem_limit_bytes=KERNEL_VMEM),
        name="first_norm_back",
    )(grad_qkv, tokens, live, gain, order, grad_residual, sums, b_up, tables, *pieces)


def own_kernel(sizes, me_ref, sums_ref, *refs):
    outs, (table_h_ref, table_w_ref) = refs[:-2], refs[-2:]
    lane = lax.broadcasted_iota(jnp.int32, (1, 128), 1)
    row = 0
    for size, whole_size, out in zip(sizes, WHOLE_SIZES, outs):
        start = me_ref[0] * size
        at, shift = row + start // 128, lax.rem(start, 128)
        here = pltpu.roll(sums_ref[pl.ds(at, 1), :], lax.rem(128 - shift, 128), 1)
        there = pltpu.roll(sums_ref[pl.ds(at + 1, 1), :], lax.rem(128 - shift, 128), 1)
        out[...] = jnp.where(lane + shift < 128, here, there)[:, :size]
        row += whole_size // 128
    count = 2 * WIN - 1
    table_h_ref[...] = sums_ref[TABLE_ROW : TABLE_ROW + count, :HEAD_DIM]
    table_w_ref[...] = pltpu.roll(sums_ref[TABLE_ROW:, :], 64, 1)[:count, :HEAD_DIM]


WHOLE_SIZES = (D, D, 3 * D, D, D, D, FF, D)


def own_small(sums, me, sizes):
    table = struct((2 * WIN - 1, HEAD_DIM), F32)
    return pl.pallas_call(
        functools.partial(own_kernel, tuple(sizes)),
        in_specs=[
            pl.BlockSpec(memory_space=pltpu.SMEM),
            pl.BlockSpec(memory_space=pltpu.VMEM),
        ],
        out_specs=[pl.BlockSpec(memory_space=pltpu.VMEM)] * (len(sizes) + 2),
        out_shape=[struct((1, size), F32) for size in sizes] + [table, table],
        name="own_small",
    )(me.reshape(1), sums)


def hop(array, mask, count):
    return lax.ppermute(array, "fsdp", [(i, i ^ mask) for i in range(count)])


def hop_plan(count):
    far = count // 4
    return 2 * far, far, [1 << bit for bit in range(1, far.bit_length() - 1)]


def after(values, deps):
    if not deps:
        return list(values)
    return list(lax.optimization_barrier(tuple(values) + tuple(deps))[: len(values)])


def gather_stages(shard, count, pieces, early=False):
    farthest, far, middle = hop_plan(count)
    deps = yield
    (shard,) = after([shard], deps)
    got = hop(shard, farthest, count)
    deps = yield [shard]
    (got,) = after([got], deps)
    near = jnp.stack((shard, got))
    got = hop(near, far, count)
    deps = yield [near]
    (got,) = after([got], deps)
    stacks = [near, got]
    for masks in zip(middle, middle[::-1]):
        got = [hop(stack, mask, count) for stack, mask in zip(stacks, masks)]
        deps = yield stacks
        got = after(got, deps or stacks)
        if masks[0] != middle[-1]:
            pairs = list(zip(stacks, got))
            stacks = [jnp.concatenate(p, axis=0) for p in pairs] if early else join(pairs)
    (own,) = join([(stacks[0], got[0], stacks[1], got[1])])
    other = hop(own, 1, count)
    order = sum_order(count)
    pieces += [(own, order[: count // 2]), (other, order[count // 2 :])]
    yield [own]


def start(stages):
    next(stages)
    return stages


def finish(stages):
    for _ in stages:
        pass


def place_kernel(owners, columns, me_ref, *refs):
    stacks, outs, sem = refs[: len(owners)], refs[len(owners) : -1], refs[-1]
    copies = []
    for stack, stack_owners in zip(stacks, owners):
        for index, mask in enumerate(stack_owners):
            owner = jnp.bitwise_xor(me_ref[0], mask)
            for out, lo, hi, to in columns:
                copies.append(
                    pltpu.make_async_copy(
                        stack.at[index, :, lo:hi],
                        outs[out].at[owner, :, to : to + hi - lo],
                        sem.at[len(copies)],
                    )
                )
                copies[-1].start()
    for copy in copies:
        copy.wait()


def place(pieces, columns, widths, me, count):
    stacks = [stack for stack, _ in pieces]
    rows = stacks[0].shape[1]
    outs = pl.pallas_call(
        functools.partial(place_kernel, tuple(tuple(o) for _, o in pieces), columns),
        in_specs=[pl.BlockSpec(memory_space=pltpu.SMEM)]
        + [pl.BlockSpec(memory_space=pl.ANY)] * len(stacks),
        out_specs=[pl.BlockSpec(memory_space=pltpu.VMEM)] * len(widths),
        out_shape=[jax.ShapeDtypeStruct((count, rows, width), BF) for width in widths],
        scratch_shapes=[pltpu.SemaphoreType.DMA((count * len(columns),))],
        cost_estimate=QUICK,
        compiler_params=pltpu.CompilerParams(vmem_limit_bytes=KERNEL_VMEM),
        name="place",
    )(me.reshape(1), *stacks)
    return [out.reshape(count * rows, width) for out, width in zip(outs, widths)]


def sum_order(count):
    farthest, far, middle = hop_plan(count)
    order = []
    for masks, block in ((middle, [0, farthest]), (middle[::-1], [far, far ^ farthest])):
        for mask in masks:
            block = block + [owner ^ mask for owner in block]
        order += block
    return order + [owner ^ 1 for owner in order]


def order_matrix(me, count, rows):
    masks = np.repeat(np.array(sum_order(count), np.int32), rows)
    wanted = jnp.bitwise_xor(me, masks) * rows + np.tile(np.arange(rows, dtype=np.int32), count)
    features = lax.broadcasted_iota(jnp.int32, (count * rows, count * rows), 0)
    return (features == wanted[None, :]).astype(BF)


def pick_kernel(masks, me_ref, stack, kept, sent, sem):
    half = len(masks) // 2
    copies = []
    for index, mask in enumerate(masks):
        owner = jnp.bitwise_xor(me_ref[0], mask)
        out = kept if index < half else sent
        copies.append(
            pltpu.make_async_copy(stack.at[owner], out.at[index % half], sem.at[index])
        )
        copies[-1].start()
    for copy in copies:
        copy.wait()


def pick(array, me, count):
    stack = array.reshape(count, -1, array.shape[-1])
    half = jax.ShapeDtypeStruct((count // 2,) + stack.shape[1:], BF)
    return pl.pallas_call(
        functools.partial(pick_kernel, tuple(sum_order(count))),
        in_specs=[
            pl.BlockSpec(memory_space=pltpu.SMEM),
            pl.BlockSpec(memory_space=pl.ANY),
        ],
        out_specs=[pl.BlockSpec(memory_space=pltpu.VMEM)] * 2,
        out_shape=[half, half],
        scratch_shapes=[pltpu.SemaphoreType.DMA((count,))],
        cost_estimate=QUICK,
        compiler_params=pltpu.CompilerParams(vmem_limit_bytes=16 * 1024 * 1024),
        name="pick",
    )(me.reshape(1), stack)


def add_low(left, right):
    return (left.astype(F32) + right.astype(F32)).astype(BF)


def scatter_stages(parts, count, result, late=(), direct=False, inbox=None, costs=()):
    farthest, far, middle = hop_plan(count)
    blocks = count // 2
    half = blocks // 2
    shape = lambda side: side.reshape(blocks, -1, side.shape[-1])
    kept, sent = [shape(k) for k, _ in parts], [shape(s) for _, s in parts]
    deps = yield
    sent = after(sent, deps)
    arrived = [hop(side, 1, count) for side in sent]
    deps = yield sent
    arrived = after(arrived, deps)
    pairs = list(zip(kept, arrived)) + [(shape(k), shape(got)) for k, got in late]

    costs = list(costs)

    def added(groups, outputs):
        cost = costs.pop(0) if costs else QUICK
        rows = groups[0][0][0].shape[1]
        if all(lo * rows % 16 == 0 and hi * rows % 16 == 0 for o in outputs for _, lo, hi in o):
            return add_ranges(groups, outputs, cost)
        return [
            jnp.concatenate(
                [
                    jnp.concatenate([add_low(a[lo:hi], b[lo:hi]) for a, b in groups[g]], axis=-1)
                    for g, lo, hi in ranges
                ],
                axis=0,
            )
            for ranges in outputs
        ]

    groups, size = [pairs], half
    for masks in zip(middle[::-1], middle):
        size //= 2
        at = [(0, 0), (0, half)] if len(groups) == 1 else [(0, 0), (1, 0)]
        *sends, near, back = added(
            groups,
            [[(group, lo + size, lo + 2 * size)] for group, lo in at]
            + [[(group, lo, lo + size)] for group, lo in at],
        )
        got = [hop(send, mask, count) for send, mask in zip(sends, masks)]
        if inbox is not None:
            inbox[:] = got
        deps = yield sends
        got = after(got, deps)
        groups = [[(near, got[0])], [(back, got[1])]]
    if direct:
        near, back = (a.astype(F32) + b.astype(F32) for ((a, b),) in groups)
        sends = [block.astype(BF) for block in (near[1], back[0], back[1])]
        got = [hop(s, m, count) for s, m in zip(sends, (farthest, far, far ^ farthest))]
        deps = yield sends
        got = after(got, deps)
        total = near[0] + got[0].astype(F32) + got[1].astype(F32) + got[2].astype(F32)
        result.append(total)
        yield [total]
        return
    send, kept = added(groups, [[(1, 0, 2)], [(0, 0, 2)]])
    got = hop(send, far, count)
    deps = yield [send]
    (got,) = after([got], deps)
    send = add_low(kept[1], got[1])
    arrived = hop(send, farthest, count)
    deps = yield [send]
    (arrived,) = after([arrived], deps)
    total = kept[0].astype(F32) + got[0].astype(F32) + arrived.astype(F32)
    result.append(total)
    yield [total]


def sum_stages(array, count, result):
    bits = count.bit_length() - 1
    deps = yield
    for mask in [1 << bit for bit in [bits - 2, bits - 1, 0] + list(range(1, bits - 2))]:
        (array,) = after([array], deps)
        got = hop(array, mask, count)
        deps = yield [array]
        (got,) = after([got], deps)
        array = array + got
    result.append(array)
    yield [array]


def per_device(
    tokens,
    window_pos,
    norm1_gain,
    norm1_bias,
    qkv_weight,
    qkv_bias,
    rel_pos_h,
    rel_pos_w,
    proj_weight,
    proj_bias,
    norm2_gain,
    norm2_bias,
    lin1_weight,
    lin1_bias,
    lin2_weight,
    lin2_bias,
    out_grad,
):
    vectors = (
        norm1_gain,
        norm1_bias,
        qkv_bias,
        proj_bias,
        norm2_gain,
        norm2_bias,
        lin1_bias,
        lin2_bias,
    )
    sizes = [v.shape[0] for v in vectors]
    used = sum(sizes)
    shard_rows = qkv_weight.shape[0]
    count = lax.axis_size("fsdp")
    me = lax.axis_index("fsdp")

    packed = lax.optimization_barrier(jnp.concatenate(vectors))
    packed = jnp.pad(packed, (0, shard_rows * 128 - used)).reshape(shard_rows, 128)
    middle = len(hop_plan(count)[2])
    first_pieces, second_pieces, third_pieces = [], [], []
    first = start(
        gather_stages(
            jnp.concatenate((qkv_weight, proj_weight, packed), axis=1).astype(BF), count, first_pieces, early=True
        )
    )
    second = start(gather_stages(lin1_weight.astype(BF), count, second_pieces))
    third = start(gather_stages(lin2_weight.astype(BF), count, third_pieces))
    onehot, shift = window_constants()
    onehot = jnp.asarray(onehot, BF)
    shift = jnp.asarray(shift)
    order = order_matrix(me, count, shard_rows)
    table = table_lanes(rel_pos_h, rel_pos_w)
    live = jnp.broadcast_to(slot_mask(window_pos), (tokens.shape[0], 128))
    inverse = np.argsort(np.array(sum_order(count)))
    places = jnp.take(jnp.asarray(inverse, jnp.int32), jnp.bitwise_xor(me, np.arange(count)))
    first.send(None)
    sent = first.send(None)
    first.send(None)
    second.send(sent)
    third.send(sent)
    for _ in range(middle - 1):
        sent = first.send(None)
    sent = second.send(sent) + third.send(sent)
    sent = second.send(sent) + third.send(sent)
    first.send(sent + [order, table, live, places])

    (small,) = place(
        first_pieces, ((0, 4 * D, 4 * D + 128, 0),), (128,), me, count
    )
    small = small.reshape(count, shard_rows * 128)[:, :used].astype(F32)
    edges = np.cumsum([0] + sizes)
    gain_one, bias_one, b_qkv, b_proj, gain_two, bias_two, b_up, b_down = (
        small[:, lo:hi].reshape(-1) for lo, hi in zip(edges[:-1], edges[1:])
    )
    flat = lambda pieces: [stack.reshape(-1, stack.shape[-1]) for stack, _ in pieces]
    first_pieces = flat(first_pieces)
    (gated_tokens,) = after([tokens], sent)
    turned_one, qkv = front(
        gated_tokens, live, order, jnp.stack((gain_one, bias_one)), b_qkv.reshape(1, -1), first_pieces
    )
    sent = [turned_one]
    for _ in range(middle - 1):
        sent = second.send(sent) + third.send(sent)
    (qkv,) = after([qkv], sent)
    mixed, probs = attention(qkv, table, onehot, shift)
    sent = third.send([mixed])
    b_up = b_up.reshape(1, FF)
    (mixed,) = after([mixed], sent + [b_up])
    vectors = jnp.stack((b_proj, gain_two, bias_two, b_down))
    residual, normed_two, turned_two, ordered_mixed = project(
        tokens, mixed, order, vectors, first_pieces
    )
    second.send([residual])

    own_down, own_up, own_third, all_small = [], [], [], []
    down_weight = placed_down(third_pieces, me, count)
    output, grad_normed, kept_up, sent_up, grad_b_up, down_parts = mlp(
        me,
        count,
        places,
        normed_two,
        turned_two,
        live,
        out_grad,
        residual,
        vectors,
        b_up,
        flat(second_pieces),
        down_weight,
    )
    late, got_up, got_down = [], [], []
    up = start(scatter_stages([(kept_up, sent_up)], count, own_up, late, inbox=got_up))
    down = start(
        scatter_stages([down_parts], count, own_down, inbox=got_down, costs=(QUICK, LONG))
    )
    sent = up.send(None)
    sent = down.send(sent)
    (grad_normed,) = after([grad_normed], sent)
    grad_residual, grad_mixed, kept_proj, sent_proj, mlp_sums = second_norm_back(
        grad_normed, residual, ordered_mixed, live, out_grad, order, vectors, first_pieces
    )
    late.append((kept_proj, hop(sent_proj, 1, count)))
    sent = down.send([grad_mixed])
    sent = up.send(sent)
    (grad_mixed,) = after([grad_mixed], sent)
    grad_qkv, tables = attention_back(qkv, grad_mixed, probs, table, onehot, shift)
    kept_qkv, sent_qkv = weight_grad(turned_one, grad_qkv)
    third_sum = start(scatter_stages([(kept_qkv, sent_qkv)], count, own_third, direct=True))
    third_sum.send(None)
    sent = [kept_qkv]
    for _ in range(middle - 1):
        sent = up.send(sent)
    (grad_qkv,) = after([grad_qkv], sent)
    tokens_grad, small_sums = first_norm_back(
        grad_qkv,
        first_pieces,
        tokens,
        live,
        gain_one.reshape(1, D),
        order,
        grad_residual,
        mlp_sums,
        grad_b_up,
        tables,
    )
    small_stages = start(sum_stages(small_sums, count, all_small))
    sent = small_stages.send(None)
    for _ in range(middle - 1):
        sent = down.send([small_sums] + sent)
    sent = third_sum.send(sent + got_up)
    sent = up.send(sent)
    (gated_tables,) = after([tables], sent)
    sent = [marker(gated_tables)]
    sent = small_stages.send(sent)
    sent = down.send(sent)
    for _ in range(middle - 1):
        sent = third_sum.send(sent)
    sent = up.send(sent)
    sent = small_stages.send(sent)
    sent = third_sum.send(sent)
    sent = small_stages.send(sent)
    sent = down.send(sent)
    sent = small_stages.send(sent)
    sent = up.send(sent)
    for stages in (down, up, third_sum, small_stages):
        finish(stages)
    own_qkv, own_proj = own_third[0], own_up[0][:, FF:]
    *owned, table_h, table_w = own_small(all_small[0], me, sizes)
    owned = [vector.reshape(-1) for vector in owned]

    return (
        output,
        tokens_grad,
        owned[0],
        owned[1],
        own_qkv,
        owned[2],
        table_h,
        table_w,
        own_proj,
        owned[3],
        owned[4],
        owned[5],
        own_up[0][:, :FF],
        owned[6],
        own_down[0],
        owned[7],
    )


def solution(mesh):
    rows = P("fsdp", None)
    line = P("fsdp")
    return jax.shard_map(
        per_device,
        mesh=mesh,
        in_specs=(
            rows,
            line,
            line,
            line,
            rows,
            line,
            P(),
            P(),
            rows,
            line,
            line,
            line,
            rows,
            line,
            rows,
            line,
            rows,
        ),
        out_specs=(
            rows,
            rows,
            line,
            line,
            rows,
            line,
            P(),
            P(),
            rows,
            line,
            line,
            line,
            rows,
            line,
            rows,
            line,
        ),
        check_vma=False,
    )
```

```python
import functools

import jax
import jax.numpy as jnp
import numpy as np
from jax import lax
from jax.experimental import pallas as pl
from jax.experimental.pallas import tpu as pltpu
from jax.sharding import PartitionSpec as P

D = 768
HEADS = 12
HEAD_DIM = 64
FF = 3072
WIN = 14
NWS = 5
EDGE = 8
LENGTH = WIN * WIN
PAIRS = HEADS // 2
BLOCK = 200
SCALE = HEAD_DIM ** (-0.5)
EPS = 1e-06
ATTENTION_VMEM = 60 * 1024 * 1024
KERNEL_VMEM = 60 * 1024 * 1024
QUICK = pl.CostEstimate(flops=1, bytes_accessed=1, transcendentals=0)
LONG = pl.CostEstimate(flops=100_000_000_000, bytes_accessed=1, transcendentals=0)
LANES = 256
BF = jnp.bfloat16
F32 = jnp.float32


def window_constants():
    onehot = np.zeros((2, BLOCK, 128), np.float32)
    shift = np.zeros((2, 16, LANES), np.int32)
    for win in range(2):
        for row in range(BLOCK):
            slot = row - 4 * win
            if not 0 <= slot < LENGTH:
                onehot[win, row, 63] = onehot[win, row, 127] = -1e30
                continue
            y, x = divmod(slot, WIN)
            for base in (0, 64):
                for lane in (0, 16):
                    onehot[win, row, base + lane + WIN - 1 - y] = 1.0
                    onehot[win, row, base + 32 + lane + WIN - 1 - x] = 1.0
            shift[win, :8, row] = y
            shift[win, 8:, row] = x
    return onehot, shift


def table_lanes(rel_pos_h, rel_pos_w):
    flip = jnp.concatenate(
        (
            jnp.pad(rel_pos_h, ((0, 5), (0, 0))),
            jnp.pad(rel_pos_w, ((0, 5), (0, 0))),
        ),
        axis=0,
    ).astype(BF) * BF(1.0 / SCALE)
    nothing = jnp.zeros_like(flip)
    return jnp.concatenate(
        (jnp.concatenate((nothing, flip), axis=1), jnp.concatenate((flip, nothing), axis=1)), axis=0
    )


def dot_nn(a, b):
    return jnp.dot(a, b, preferred_element_type=F32)


def dot_nt(a, b):
    return lax.dot_general(a, b, (((1,), (1,)), ((), ())), preferred_element_type=F32)


def dot_tn(a, b):
    return lax.dot_general(a, b, (((0,), (0,)), ((), ())), preferred_element_type=F32)


def low_half():
    return lax.broadcasted_iota(jnp.int32, (BLOCK, 128), 1) < 64


def row_valid(win):
    row = lax.broadcasted_iota(jnp.int32, (BLOCK, 128), 0)
    return row < LENGTH if win == 0 else row >= BLOCK - LENGTH


def merge_windows(first, second):
    return jnp.concatenate((first[:192], first[192:] + second[:8], second[8:]), axis=0)


def pad_rows(values):
    return jnp.concatenate((values, jnp.zeros((LANES - BLOCK, 128), F32)), axis=0)


def bit_masks(shift, rows):
    shift = jnp.broadcast_to(shift[:1], (rows, LANES))
    return [(shift & (1 << bit)) != 0 for bit in range(4)]


def skew(values, masks):
    values = jnp.where(masks[3], values[8:], values[:24])
    values = jnp.where(masks[2], pltpu.roll(values, 20, 0), values)
    values = jnp.where(masks[1], pltpu.roll(values, 22, 0), values)[:16]
    return jnp.where(masks[0][:16], pltpu.roll(values, 15, 0), values)


def unskew(values, masks):
    nothing = jnp.zeros((8, LANES), F32)
    values = jnp.concatenate((values, nothing), axis=0)
    for bit in range(3):
        values = jnp.where(masks[bit], pltpu.roll(values, 1 << bit, 0), values)
    return jnp.concatenate(
        (
            jnp.where(masks[3][:8], 0.0, values[:8]),
            jnp.where(masks[3][:16], values[:16], values[8:]),
            jnp.where(masks[3][:8], values[16:], 0.0),
        ),
        axis=0,
    )


def attn_fwd_kernel(q_ref, k_ref, v_ref, table_ref, onehot_ref, shift_ref, mixed_ref, probs_ref):
    low = low_half()
    last = lax.broadcasted_iota(jnp.int32, (16, LANES), 0) == 15
    mixed = []
    for win in range(2):
        rows = pl.ds(192 * win, BLOCK)
        queries = pad_rows(q_ref[rows, :].astype(F32) * SCALE).T
        k = k_ref[rows, :].astype(F32)
        v = v_ref[rows, :].astype(F32)
        rel = dot_nn(table_ref[...], queries.astype(BF))
        onehot = onehot_ref[win].astype(F32)
        by_row = bit_masks(shift_ref[win, :8], 24)
        by_col = bit_masks(shift_ref[win, 8:], 24)
        halves = []
        for head in range(2):
            base = 64 if head == 0 else 0
            from_row = skew(rel[base : base + 32], by_row)
            from_col = skew(rel[base + 32 : base + 64], by_col)
            row_top = from_row.astype(BF).astype(F32)
            col_top = from_col.astype(BF).astype(F32)
            extra = (row_top, from_row - row_top, col_top, jnp.where(last, 1.0, from_col - col_top))
            if head == 0:
                left = jnp.concatenate((queries[:64],) + extra, axis=0).astype(BF)
                right = jnp.where(low, k, onehot).astype(BF)
            else:
                left = jnp.concatenate(extra + (queries[64:],), axis=0).astype(BF)
                right = jnp.where(low, onehot, k).astype(BF)
            scores = dot_nn(right, left)
            expon = jnp.exp(scores - jnp.max(scores, axis=0, keepdims=True))
            probs = expon * (1.0 / jnp.sum(expon, axis=0, keepdims=True))
            probs_ref[0, 2 * win + head] = probs
            halves.append(probs)
        values = jnp.concatenate((jnp.where(low, v, 0.0), jnp.where(low, 0.0, v)), axis=0)
        both = dot_tn(values.astype(BF), jnp.concatenate(halves, axis=0).astype(BF)).T[:BLOCK]
        mixed.append(jnp.where(row_valid(win), both, 0.0))
    mixed_ref[...] = merge_windows(*mixed).astype(BF)


def attn_bwd_kernel(
    q_ref,
    k_ref,
    v_ref,
    grad_ref,
    probs_ref,
    table_ref,
    onehot_ref,
    shift_ref,
    grad_qkv_ref,
    table_grad_ref,
):
    pair = pl.program_id(0)
    low = low_half()

    @pl.when(pair == 0)
    def _():
        table_grad_ref[...] = jnp.zeros_like(table_grad_ref)

    parts = ([], [], [])
    table_total = jnp.zeros((128, 128), F32)
    for win in range(2):
        rows = pl.ds(192 * win, BLOCK)
        q = pad_rows(q_ref[rows, :].astype(F32) * SCALE)
        k = k_ref[rows, :].astype(F32)
        v = v_ref[rows, :]
        grad = pad_rows(jnp.where(row_valid(win), grad_ref[rows, :].astype(F32), 0.0))
        wide_low = lax.broadcasted_iota(jnp.int32, (LANES, 128), 1) < 64

        def by_head(values):
            return jnp.concatenate(
                (jnp.where(wide_low, values, 0.0), jnp.where(wide_low, 0.0, values)), axis=0
            ).astype(BF)

        grads, queries = by_head(grad), by_head(q)
        q = q.astype(BF)
        onehot = onehot_ref[win].astype(F32)
        by_row = bit_masks(shift_ref[win, :8], 24)
        by_col = bit_masks(shift_ref[win, 8:], 24)
        probs = jnp.concatenate((probs_ref[0, 2 * win], probs_ref[0, 2 * win + 1]), axis=1)
        grad_probs = dot_nt(v, grads)
        row_dot = jnp.sum(probs * grad_probs, axis=0, keepdims=True)
        grad_scores = (probs * (grad_probs - row_dot)).astype(BF)
        parts[2].append(dot_nn(probs.astype(BF), grads))
        parts[1].append(dot_nn(grad_scores, queries))
        by_query, rel = [], []
        for head in range(2):
            right = (jnp.where(low, k, onehot) if head == 0 else jnp.where(low, onehot, k)).astype(BF)
            back = dot_tn(right, grad_scores[:, head * LANES : (head + 1) * LANES])
            own, base = (back[:64], 64) if head == 0 else (back[64:], 0)
            by_query.append(own)
            rel.append(unskew(back[base : base + 16], by_row))
            rel.append(unskew(back[base + 32 : base + 48], by_col))
        rel = jnp.concatenate((rel[2], rel[3], rel[0], rel[1]), axis=0)
        rel_top = rel.astype(BF).astype(F32)
        rel = jnp.concatenate((rel_top, rel - rel_top), axis=0).astype(BF)
        table = table_ref[...]
        from_rel = dot_tn(jnp.concatenate((table, table), axis=0), rel)
        table_parts = dot_nn(rel, q)
        table_total += table_parts[:128] + table_parts[128:]
        parts[0].append((jnp.concatenate(by_query, axis=0) + from_rel).T[:BLOCK] * SCALE)
    for block in range(3):
        at = pl.multiple_of(block * D + pair * 128, 128)
        grad_qkv_ref[:, pl.ds(at, 128)] = merge_windows(*parts[block]).astype(BF)
    table_grad_ref[...] += table_total


def attention_specs(rows):
    column = lambda block: pl.BlockSpec((rows, 128), lambda pair: (0, block * PAIRS + pair))
    whole = lambda *shape: pl.BlockSpec(shape, lambda pair: (0,) * len(shape))
    return (
        [column(0), column(1), column(2)],
        [whole(128, 128), whole(2, BLOCK, 128), whole(2, 16, LANES)],
        pl.BlockSpec((1, 4, BLOCK, LANES), lambda pair: (pair, 0, 0, 0)),
        whole,
    )


def attention(qkv, table, onehot, shift):
    rows = qkv.shape[0]
    columns, constants, probs_spec, _ = attention_specs(rows)
    return pl.pallas_call(
        attn_fwd_kernel,
        grid=(PAIRS,),
        in_specs=columns + constants,
        out_specs=[pl.BlockSpec((rows, 128), lambda pair: (0, pair)), probs_spec],
        out_shape=[
            jax.ShapeDtypeStruct((rows, D), BF),
            jax.ShapeDtypeStruct((PAIRS, 4, BLOCK, LANES), F32),
        ],
        cost_estimate=QUICK,
        compiler_params=pltpu.CompilerParams(vmem_limit_bytes=ATTENTION_VMEM),
        name="attention",
    )(qkv, qkv, qkv, table, onehot, shift)


def attention_back(qkv, grad_mixed, probs, table, onehot, shift):
    rows = qkv.shape[0]
    columns, constants, probs_spec, whole = attention_specs(rows)
    return pl.pallas_call(
        attn_bwd_kernel,
        grid=(PAIRS,),
        in_specs=columns + [pl.BlockSpec((rows, 128), lambda pair: (0, pair)), probs_spec]
        + constants,
        out_specs=[whole(rows, 3 * D), whole(128, 128)],
        out_shape=[
            jax.ShapeDtypeStruct((rows, 3 * D), BF),
            jax.ShapeDtypeStruct((128, 128), F32),
        ],
        cost_estimate=QUICK,
        compiler_params=pltpu.CompilerParams(vmem_limit_bytes=ATTENTION_VMEM),
        name="attention_back",
    )(qkv, qkv, qkv, grad_mixed, probs, table, onehot, shift)


def slot_mask(window_pos):
    row_win = window_pos // NWS
    col_win = window_pos % NWS
    rows_ok = jnp.where(row_win == NWS - 1, EDGE, WIN)
    cols_ok = jnp.where(col_win == NWS - 1, EDGE, WIN)
    positions = jnp.arange(WIN, dtype=jnp.int32)
    inside = (positions[None, :, None] < rows_ok[:, None, None]) & (
        positions[None, None, :] < cols_ok[:, None, None]
    )
    return inside.reshape(-1, 1).astype(F32)


def normalise(values):
    centred = values - jnp.mean(values, axis=-1, keepdims=True)
    rstd = lax.rsqrt(jnp.mean(centred * centred, axis=-1, keepdims=True) + EPS)
    return centred * rstd, rstd


def normalise_back(grad, hat, rstd, gain):
    grad_hat = grad * gain
    return rstd * (
        grad_hat
        - jnp.mean(grad_hat, axis=-1, keepdims=True)
        - hat * jnp.mean(grad_hat * hat, axis=-1, keepdims=True)
    )


def normal_cdf(values):
    return 0.5 * (1.0 + lax.erf(values * np.float32(np.sqrt(0.5))))


def normal_pdf(values):
    return np.float32(1.0 / np.sqrt(2.0 * np.pi)) * jnp.exp(-0.5 * values * values)


def copy_rows(pieces, columns, out, to, sems):
    rows = pieces[0].shape[0]
    lo, width = columns
    return [
        pltpu.make_async_copy(
            piece.at[:, pl.ds(lo, width)],
            out.at[index * rows : (index + 1) * rows, pl.ds(to, width)],
            sems.at[index],
        )
        for index, piece in enumerate(pieces)
    ]


def start_all(copies):
    for copy in copies:
        copy.start()


def wait_all(copies):
    for copy in copies:
        copy.wait()


def front_kernel(tokens_ref, live_ref, order_ref, rows_ref, b_qkv_ref, *rest):
    pieces, (turned_ref, qkv_ref, weight, sem) = rest[:PIECES], rest[PIECES:]
    copies = [copy_rows(pieces, (block * D, D), weight, block * D, sem.at[block]) for block in range(3)]
    for block in copies:
        start_all(block)
    unit, _ = normalise(tokens_ref[...].astype(F32))
    normed = ((unit * rows_ref[0:1, :] + rows_ref[1:2, :]) * live_ref[:, :1]).astype(BF)
    turned = dot_nn(normed, order_ref[...])
    normed = turned.astype(BF)
    turned_ref[...] = turned.T.astype(BF)
    for block in range(3):
        wait_all(copies[block])
        at = block * D
        values = dot_nn(normed, weight[:, at : at + D]) + b_qkv_ref[:, at : at + D]
        qkv_ref[:, at : at + D] = values.astype(BF)


PIECES = 2
HBM = pl.BlockSpec(memory_space=pl.ANY)
VMEM = pl.BlockSpec(memory_space=pltpu.VMEM)
SMEM = pl.BlockSpec(memory_space=pltpu.SMEM)


def front(tokens, live, order, vectors, b_qkv, pieces):
    rows = tokens.shape[0]
    return pl.pallas_call(
        front_kernel,
        in_specs=[VMEM] * 5 + [HBM] * PIECES,
        out_specs=[VMEM] * 2,
        out_shape=[struct((D, rows), BF), struct((rows, 3 * D), BF)],
        scratch_shapes=[pltpu.VMEM((D, 3 * D), BF), pltpu.SemaphoreType.DMA((3, PIECES))],
        cost_estimate=QUICK,
        compiler_params=pltpu.CompilerParams(vmem_limit_bytes=KERNEL_VMEM),
        name="front",
    )(tokens, live, order, vectors, b_qkv, *pieces)


def proj_kernel(tokens_ref, values_ref, order_ref, rows_ref, *rest):
    pieces, (residual_ref, normed_ref, turned_ref, mixed_ref, w_proj, sem) = rest[:PIECES], rest[PIECES:]
    b_proj, gain, bias = (rows_ref[i : i + 1, :] for i in range(3))
    copies = copy_rows(pieces, (3 * D, D), w_proj, 0, sem)
    start_all(copies)
    mixed = dot_nn(values_ref[...], order_ref[...]).astype(BF)
    mixed_ref[...] = mixed
    wait_all(copies)
    values = tokens_ref[...].astype(F32) + dot_nn(mixed, w_proj[...]) + b_proj
    residual_ref[...] = values
    low = (normalise(values)[0] * gain + bias).astype(BF)
    low = dot_nn(low, order_ref[...])
    normed_ref[...] = low.astype(BF)
    turned_ref[...] = low.T.astype(BF)


def down_copies(pieces, owners, me_ref, weight, sems):
    copies = []
    for piece, masks in zip(pieces, owners):
        rows = piece.shape[0] // len(masks)
        for index, mask in enumerate(masks):
            to = jnp.bitwise_xor(me_ref[0], mask) * rows
            copies.append(
                pltpu.make_async_copy(
                    piece.at[index * rows : (index + 1) * rows],
                    weight.at[pl.ds(pl.multiple_of(to, rows), rows)],
                    sems.at[len(copies)],
                )
            )
    return copies


def mlp_kernel(split_rows, owners, place_ref, me_ref, *rest):
    normed_ref, turned_ref, live_ref, out_grad_ref, residual_ref, rows_ref, b_up_ref, *rest = rest
    up_pieces, rest = rest[:PIECES], rest[PIECES:]
    down_pieces, rest = rest[: len(owners)], rest[len(owners) :]
    output_ref, grad_normed_ref, kept_ref, sent_ref, grad_b_ref, *rest = rest
    if split_rows:
        kept_down_ref, sent_down_ref, *rest = rest
    else:
        grad_down_ref, *rest = rest
    branch, actives, grads, w_up, w_down, staged, sem, up_sem, down_sem = rest
    step = pl.program_id(0)
    half = D // 2

    def up_copies(index):
        return copy_rows(up_pieces, (index * TILE, TILE), w_up, index * TILE, up_sem.at[index])

    @pl.when(step == 0)
    def _():
        start_all(up_copies(0))
        start_all(down_copies(down_pieces, owners, me_ref, w_down, down_sem))
        for index in range(1, STEPS):
            start_all(up_copies(index))
        branch[...] = (out_grad_ref[...].astype(F32) * live_ref[:, :1]).astype(BF)

    wait_all(up_copies(step))
    at = pl.multiple_of(step * TILE, TILE)
    hidden = dot_nn(normed_ref[...], w_up[:, pl.ds(at, TILE)]) + b_up_ref[...]
    cdf = normal_cdf(hidden)
    active = (hidden * cdf).astype(BF)
    slope = cdf + hidden * normal_pdf(hidden)
    grad_down = dot_tn(active, branch[...]).astype(BF)

    @pl.when(step == 0)
    def _():
        wait_all(down_copies(down_pieces, owners, me_ref, w_down, down_sem))

    grad_active = dot_nt(branch[...], w_down[pl.ds(at, TILE), :])
    grad_hidden = (grad_active * slope).astype(BF)
    grad_up = dot_nn(turned_ref[...], grad_hidden).astype(BF)
    kept_ref[...] = grad_up[:half]
    sent_ref[...] = grad_up[half:]
    actives[:, pl.ds(at, TILE)] = active
    grads[:, pl.ds(at, TILE)] = grad_hidden
    grad_b_ref[...] = jnp.sum(grad_hidden.astype(F32), axis=0, keepdims=True)

    def finish_sums():
        grad_normed_ref[...] = dot_nt(grads[...], w_up[...])
        total = residual_ref[...] + rows_ref[3:4, :] + dot_nn(actives[...], w_down[...])
        output_ref[...] = (total * live_ref[:, :1]).astype(BF)

    if not split_rows:
        grad_down_ref[...] = grad_down
        pl.when(step == STEPS - 1)(finish_sums)
        return

    slot = lax.rem(step, 2)
    blocks = staged.shape[1]

    def copy(slot, block, out, to):
        return pltpu.make_async_copy(staged.at[slot, block], out.at[to], sem.at[slot, block])

    @pl.when(step >= 2)
    def _():
        for block in range(blocks):
            copy(slot, block, kept_down_ref, 0).wait()

    staged[slot] = grad_down.reshape(blocks, split_rows, D)
    places = kept_down_ref.shape[0]
    for block in range(blocks):
        to = place_ref[step * blocks + block]

        @pl.when(to < places)
        def _():
            copy(slot, block, kept_down_ref, to).start()

        @pl.when(to >= places)
        def _():
            copy(slot, block, sent_down_ref, to - places).start()

    @pl.when(step == STEPS - 1)
    def _():
        finish_sums()
        for last_slot in range(2):
            for block in range(blocks):
                copy(last_slot, block, kept_down_ref, 0).wait()


def second_norm_kernel(
    grad_normed_ref, residual_ref, mixed_ref, live_ref, out_grad_ref, order_ref, rows_ref, *rest
):
    pieces, rest = rest[:PIECES], rest[PIECES:]
    grad_residual_ref, grad_mixed_ref, *rest = rest
    kept_proj_ref, sent_proj_ref, sums_ref, w_proj, sem, *rest = rest
    residual_here, mixed_here, out_grad_here, side_sem = rest
    half = D // 2
    sides = [
        pltpu.make_async_copy(source, here, side_sem.at[index])
        for index, (source, here) in enumerate(
            (
                (residual_ref, residual_here),
                (out_grad_ref, out_grad_here),
                (mixed_ref, mixed_here),
            )
        )
    ]
    start_all(sides)
    copies = copy_rows(pieces, (3 * D, D), w_proj, 0, sem)
    start_all(copies)
    grad = natural_order(grad_normed_ref[...], order_ref[...])
    wait_all(sides)
    residual_ref, out_grad_ref, mixed_ref = residual_here, out_grad_here, mixed_here
    unit, rstd = normalise(residual_ref[...])
    grad_out = out_grad_ref[...].astype(F32) * live_ref[:, :1]
    grad_residual = grad_out + normalise_back(grad, unit, rstd, rows_ref[1:2, :])
    grad_residual_ref[...] = grad_residual
    grad_attn = grad_residual.astype(BF)
    wait_all(copies)
    grad_mixed = dot_nt(grad_attn, w_proj[...]).astype(BF)
    grad_mixed_ref[...] = dot_nt(grad_mixed, order_ref[...]).astype(BF)
    sent_proj_ref[...] = dot_tn(mixed_ref[:, half:], grad_attn).astype(BF)
    kept_proj_ref[...] = dot_tn(mixed_ref[:, :half], grad_attn).astype(BF)
    sums_ref[0:1, :] = jnp.sum(grad_attn.astype(F32), axis=0, keepdims=True)
    sums_ref[1:2, :] = jnp.sum(grad * unit, axis=0, keepdims=True)
    sums_ref[2:3, :] = jnp.sum(grad, axis=0, keepdims=True)
    sums_ref[3:4, :] = jnp.sum(grad_out.astype(BF).astype(F32), axis=0, keepdims=True)
    sums_ref[4:, :] = jnp.zeros((4, D), F32)


def natural_order(values, order):
    top = values.astype(BF).astype(F32)
    rows = values.shape[0]
    both = dot_nt(jnp.concatenate((top, values - top), axis=0).astype(BF), order)
    return both[:rows] + both[rows:]


TILE = 768
STEPS = FF // TILE


def whole(*shape):
    return pl.BlockSpec(shape, lambda step: (0,) * len(shape))


def struct(shape, dtype):
    return jax.ShapeDtypeStruct(shape, dtype)


def project(tokens, mixed, order, vectors, pieces):
    rows = tokens.shape[0]
    return pl.pallas_call(
        proj_kernel,
        in_specs=[VMEM] * 4 + [HBM] * PIECES,
        out_specs=[VMEM] * 4,
        out_shape=[
            struct((rows, D), F32),
            struct((rows, D), BF),
            struct((D, rows), BF),
            struct((rows, D), BF),
        ],
        scratch_shapes=[pltpu.VMEM((D, D), BF), pltpu.SemaphoreType.DMA((PIECES,))],
        cost_estimate=QUICK,
        compiler_params=pltpu.CompilerParams(vmem_limit_bytes=KERNEL_VMEM),
        name="project",
    )(tokens, mixed, order, vectors, *pieces)


def placed_down(pieces, me, count):
    if FF // count % 16:
        return place(pieces, ((0, 0, D, 0),), (D,), me, count), ((0,),), jnp.zeros((1,), jnp.int32)
    owners = tuple(tuple(masks) for _, masks in pieces)
    return [stack.reshape(-1, D) for stack, _ in pieces], owners, me.reshape(1)


def mlp(
    me, count, places, normed, turned, live, out_grad, residual, vectors, b_up, up_pieces, down
):
    rows = normed.shape[0]
    block_rows = FF // count
    split_rows = block_rows if block_rows % 16 == 0 else 0
    down_pieces, owners, me_down = down
    column = lambda height: pl.BlockSpec((height, TILE), lambda step: (0, step))
    if split_rows:
        half = struct((count // 2, block_rows, D), BF)
        grad_specs, grad_shapes = [HBM] * 2, [half, half]
        staged = (2, TILE // block_rows, block_rows, D)
    else:
        grad_specs = [pl.BlockSpec((TILE, D), lambda step: (step, 0))]
        grad_shapes = [struct((FF, D), BF)]
        staged = (2, 1, 16, 128)
    wide = (rows, D)
    results = pl.pallas_call(
        functools.partial(mlp_kernel, split_rows, owners),
        grid=(STEPS,),
        in_specs=[SMEM, SMEM, whole(*wide), whole(D, rows), whole(rows, 128)]
        + [whole(*wide), whole(*wide), whole(4, D), column(1)]
        + [HBM] * (len(up_pieces) + len(down_pieces)),
        out_specs=[whole(*wide), whole(*wide), column(D // 2), column(D // 2), column(1)]
        + grad_specs,
        out_shape=[
            struct(wide, BF),
            struct(wide, F32),
            struct((D // 2, FF), BF),
            struct((D // 2, FF), BF),
            struct((1, FF), F32),
        ]
        + grad_shapes,
        scratch_shapes=[
            pltpu.VMEM(wide, BF),
            pltpu.VMEM((rows, FF), BF),
            pltpu.VMEM((rows, FF), BF),
            pltpu.VMEM((D, FF), BF),
            pltpu.VMEM((FF, D), BF),
            pltpu.VMEM(staged, BF),
            pltpu.SemaphoreType.DMA(staged[:2]),
            pltpu.SemaphoreType.DMA((STEPS, PIECES)),
            pltpu.SemaphoreType.DMA((sum(map(len, owners)),)),
        ],
        cost_estimate=QUICK,
        compiler_params=pltpu.CompilerParams(vmem_limit_bytes=KERNEL_VMEM),
        name="mlp",
    )(
        places,
        me_down,
        normed,
        turned,
        live,
        out_grad,
        residual,
        vectors,
        b_up,
        *up_pieces,
        *down_pieces,
    )
    parts = results[5:] if split_rows else pick(results[5], me, count)
    return tuple(results[:5]) + (tuple(parts),)


def second_norm_back(grad_normed, residual, mixed, live, out_grad, order, vectors, pieces):
    rows = residual.shape[0]
    return pl.pallas_call(
        second_norm_kernel,
        in_specs=[VMEM, HBM, HBM, VMEM, HBM, VMEM, VMEM] + [HBM] * PIECES,
        out_specs=[VMEM] * 5,
        out_shape=[
            struct((rows, D), F32),
            struct((rows, D), BF),
            struct((D // 2, D), BF),
            struct((D // 2, D), BF),
            struct((8, D), F32),
        ],
        scratch_shapes=[
            pltpu.VMEM((D, D), BF),
            pltpu.SemaphoreType.DMA((PIECES,)),
            pltpu.VMEM((rows, D), F32),
            pltpu.VMEM((rows, D), BF),
            pltpu.VMEM((rows, D), BF),
            pltpu.SemaphoreType.DMA((3,)),
        ],
        cost_estimate=QUICK,
        compiler_params=pltpu.CompilerParams(vmem_limit_bytes=KERNEL_VMEM),
        name="second_norm_back",
    )(grad_normed, residual, mixed, live, out_grad, order, vectors, *pieces)


def marker_kernel(value_ref, out_ref):
    out_ref[...] = value_ref[...]


def marker(value):
    return pl.pallas_call(
        marker_kernel,
        in_specs=[VMEM],
        out_specs=VMEM,
        out_shape=struct(value.shape, value.dtype),
        cost_estimate=LONG,
        name="marker",
    )(value)


def join_kernel(sizes, *refs):
    ins, (*outs, sems) = refs[: sum(map(len, sizes))], refs[sum(map(len, sizes)) : -len(sizes)]
    spaces = refs[-len(sizes) :]
    inward, outward = [], []
    ins = list(ins)
    for out, space, parts in zip(outs, spaces, sizes):
        at = 0
        for size in parts:
            number = len(inward)
            to = pl.ds(at, size)
            inward.append(pltpu.make_async_copy(ins.pop(0), space.at[to], sems.at[0, number]))
            outward.append(pltpu.make_async_copy(space.at[to], out.at[to], sems.at[1, number]))
            inward[-1].start()
            at += size
    for first, second in zip(inward, outward):
        first.wait()
        second.start()
    wait_all(outward)


def join(groups):
    arrays = [array for group in groups for array in group]
    sizes = tuple(tuple(array.shape[0] for array in group) for group in groups)
    shapes = [(sum(parts),) + group[0].shape[1:] for parts, group in zip(sizes, groups)]
    results = pl.pallas_call(
        functools.partial(join_kernel, sizes),
        in_specs=[HBM] * len(arrays),
        out_specs=[HBM] * len(groups),
        out_shape=[struct(shape, BF) for shape in shapes],
        scratch_shapes=[pltpu.SemaphoreType.DMA((2, len(arrays)))]
        + [pltpu.VMEM(shape, BF) for shape in shapes],
        cost_estimate=QUICK,
        compiler_params=pltpu.CompilerParams(vmem_limit_bytes=KERNEL_VMEM),
        name="join",
    )(*arrays)
    return list(results)


def weight_kernel(turned_ref, grad_ref, kept_ref, sent_ref):
    total = dot_nn(turned_ref[...], grad_ref[...]).astype(BF)
    kept_ref[...] = total[: D // 2]
    sent_ref[...] = total[D // 2 :]


def weight_grad(turned, grad):
    rows, width = grad.shape
    column = lambda height: pl.BlockSpec((height, D), lambda step: (0, step))
    return pl.pallas_call(
        weight_kernel,
        grid=(width // D,),
        in_specs=[whole(D, rows), column(rows)],
        out_specs=[column(D // 2)] * 2,
        out_shape=[struct((D // 2, width), BF)] * 2,
        cost_estimate=QUICK,
        compiler_params=pltpu.CompilerParams(vmem_limit_bytes=KERNEL_VMEM),
        name="weight_grad",
    )(turned, grad)


def add_kernel(widths, outputs, *refs):
    count = sum(map(len, widths)) * 2
    ins, outs, (in_sem, out_sem, *spaces) = (
        refs[:count],
        refs[count : count + len(outputs)],
        refs[count + len(outputs) :],
    )
    firsts = np.cumsum([0] + [len(parts) for parts in widths])
    loads, stores = [], []
    for number, ranges in enumerate(outputs):
        here, below = [], 0
        for group, lo, hi in ranges:
            at = 0
            for part, width in enumerate(widths[group]):
                for side in range(2):
                    source = ins[2 * (firsts[group] + part) + side].at[lo:hi]
                    space = spaces[2 * number + side]
                    to = space.at[below : below + hi - lo, at : at + width]
                    sem = in_sem.at[number, len(here)]
                    here.append(pltpu.make_async_copy(source, to, sem))
                at += width
            below += hi - lo
        start_all(here)
        loads.append(here)
    for number in range(len(outputs)):
        wait_all(loads[number])
        left, right = spaces[2 * number], spaces[2 * number + 1]
        left[...] = (left[...].astype(F32) + right[...].astype(F32)).astype(BF)
        stores.append(pltpu.make_async_copy(left, outs[number], out_sem.at[number]))
        stores[-1].start()
    wait_all(stores)


def add_ranges(groups, outputs, cost):
    rows = groups[0][0][0].shape[1]
    flat = [side.reshape(-1, side.shape[-1]) for group in groups for pair in group for side in pair]
    widths = tuple(tuple(pair[0].shape[-1] for pair in group) for group in groups)
    plan = tuple(tuple((g, lo * rows, hi * rows) for g, lo, hi in ranges) for ranges in outputs)
    shapes = [(sum(hi - lo for _, lo, hi in r), sum(widths[r[0][0]])) for r in plan]
    most = max(sum(2 * len(widths[g]) for g, _, _ in ranges) for ranges in plan)
    results = pl.pallas_call(
        functools.partial(add_kernel, widths, plan),
        in_specs=[HBM] * len(flat),
        out_specs=[HBM] * len(plan),
        out_shape=[struct(shape, BF) for shape in shapes],
        scratch_shapes=[
            pltpu.SemaphoreType.DMA((len(plan), most)),
            pltpu.SemaphoreType.DMA((len(plan),)),
        ]
        + [pltpu.VMEM(shape, BF) for shape in shapes for _ in range(2)],
        cost_estimate=cost,
        compiler_params=pltpu.CompilerParams(vmem_limit_bytes=KERNEL_VMEM),
        name="add_ranges",
    )(*flat)
    return [r.reshape(-1, rows, r.shape[-1]) for r in results]


def first_norm_kernel(
    grad_ref,
    tokens_ref,
    live_ref,
    gain_ref,
    order_ref,
    grad_residual_ref,
    mlp_sums_ref,
    grad_b_ref,
    tables_ref,
    *rest,
):
    pieces, (tokens_grad_ref, sums_ref, total, columns, weight, sem) = rest[:PIECES], rest[PIECES:]
    step = pl.program_id(0)

    def copies(index):
        return copy_rows(pieces, (index * D, D), weight, index * D, sem.at[index])

    @pl.when(step == 0)
    def _():
        for index in range(3):
            start_all(copies(index))
        total[...] = jnp.zeros_like(total)

    wait_all(copies(step))
    grad_qkv = grad_ref[...]
    at = pl.multiple_of(step * D, 128)
    total[...] += dot_nt(grad_qkv, weight[:, pl.ds(at, D)])
    columns[pl.ds(step, 1), :] = jnp.sum(grad_qkv.astype(F32), axis=0, keepdims=True)

    @pl.when(step == 2)
    def _():
        unit, rstd = normalise(tokens_ref[...].astype(F32))
        grad = natural_order(total[...], order_ref[...]) * live_ref[:, :1]
        tokens_grad_ref[...] = (
            grad_residual_ref[...] + normalise_back(grad, unit, rstd, gain_ref[...])
        ).astype(BF)
        vectors = [
            [jnp.sum(grad * unit, axis=0, keepdims=True)],
            [jnp.sum(grad, axis=0, keepdims=True)],
            [columns[block : block + 1, :] for block in range(3)],
            [mlp_sums_ref[0:1, :]],
            [mlp_sums_ref[1:2, :]],
            [mlp_sums_ref[2:3, :]],
            [grad_b_ref[...]],
            [mlp_sums_ref[3:4, :]],
        ]
        at = 0
        for vector in vectors:
            for piece in vector:
                for lane in range(0, piece.shape[1], 128):
                    sums_ref[at : at + 1, :] = piece[:, lane : lane + 128]
                    at += 1
        sums_ref[at:TABLE_ROW, :] = jnp.zeros((TABLE_ROW - at, 128), F32)
        tables = tables_ref[...] * (1.0 / SCALE)
        low = lax.broadcasted_iota(jnp.int32, (32, 128), 1) < 64
        sums_ref[TABLE_ROW:, :] = jnp.where(
            low,
            tables[64:96] + pltpu.roll(tables[:32], 64, 1),
            pltpu.roll(tables[96:], 64, 1) + tables[32:64],
        )


TABLE_ROW = 80
SUM_ROWS = TABLE_ROW + 32


def first_norm_back(grad_qkv, pieces, tokens, live, gain, order, grad_residual, sums, b_up, tables):
    rows = tokens.shape[0]
    return pl.pallas_call(
        first_norm_kernel,
        grid=(3,),
        in_specs=[
            pl.BlockSpec((rows, D), lambda step: (0, step)),
            whole(rows, D),
            whole(rows, 128),
            whole(1, D),
            whole(D, D),
            whole(rows, D),
            whole(8, D),
            whole(1, FF),
            whole(128, 128),
        ]
        + [HBM] * PIECES,
        out_specs=[whole(rows, D), whole(SUM_ROWS, 128)],
        out_shape=[struct((rows, D), BF), struct((SUM_ROWS, 128), F32)],
        scratch_shapes=[
            pltpu.VMEM((rows, D), F32),
            pltpu.VMEM((8, D), F32),
            pltpu.VMEM((D, 3 * D), BF),
            pltpu.SemaphoreType.DMA((3, PIECES)),
        ],
        cost_estimate=QUICK,
        compiler_params=pltpu.CompilerParams(vmem_limit_bytes=KERNEL_VMEM),
        name="first_norm_back",
    )(grad_qkv, tokens, live, gain, order, grad_residual, sums, b_up, tables, *pieces)


def own_kernel(sizes, me_ref, sums_ref, *refs):
    outs, (table_h_ref, table_w_ref) = refs[:-2], refs[-2:]
    lane = lax.broadcasted_iota(jnp.int32, (1, 128), 1)
    row = 0
    for size, whole_size, out in zip(sizes, WHOLE_SIZES, outs):
        start = me_ref[0] * size
        at, shift = row + start // 128, lax.rem(start, 128)
        here = pltpu.roll(sums_ref[pl.ds(at, 1), :], lax.rem(128 - shift, 128), 1)
        there = pltpu.roll(sums_ref[pl.ds(at + 1, 1), :], lax.rem(128 - shift, 128), 1)
        out[...] = jnp.where(lane + shift < 128, here, there)[:, :size]
        row += whole_size // 128
    count = 2 * WIN - 1
    table_h_ref[...] = sums_ref[TABLE_ROW : TABLE_ROW + count, :HEAD_DIM]
    table_w_ref[...] = pltpu.roll(sums_ref[TABLE_ROW:, :], 64, 1)[:count, :HEAD_DIM]


WHOLE_SIZES = (D, D, 3 * D, D, D, D, FF, D)


def own_small(sums, me, sizes):
    table = struct((2 * WIN - 1, HEAD_DIM), F32)
    return pl.pallas_call(
        functools.partial(own_kernel, tuple(sizes)),
        in_specs=[
            pl.BlockSpec(memory_space=pltpu.SMEM),
            pl.BlockSpec(memory_space=pltpu.VMEM),
        ],
        out_specs=[pl.BlockSpec(memory_space=pltpu.VMEM)] * (len(sizes) + 2),
        out_shape=[struct((1, size), F32) for size in sizes] + [table, table],
        name="own_small",
    )(me.reshape(1), sums)


def hop(array, mask, count):
    return lax.ppermute(array, "fsdp", [(i, i ^ mask) for i in range(count)])


def hop_plan(count):
    far = count // 4
    return 2 * far, far, [1 << bit for bit in range(1, far.bit_length() - 1)]


def after(values, deps):
    if not deps:
        return list(values)
    return list(lax.optimization_barrier(tuple(values) + tuple(deps))[: len(values)])


def gather_stages(shard, count, pieces, early=False):
    farthest, far, middle = hop_plan(count)
    deps = yield
    (shard,) = after([shard], deps)
    got = hop(shard, farthest, count)
    deps = yield [shard]
    (got,) = after([got], deps)
    near = jnp.stack((shard, got))
    got = hop(near, far, count)
    deps = yield [near]
    (got,) = after([got], deps)
    stacks = [near, got]
    for masks in zip(middle, middle[::-1]):
        got = [hop(stack, mask, count) for stack, mask in zip(stacks, masks)]
        deps = yield stacks
        got = after(got, deps or stacks)
        if masks[0] != middle[-1]:
            pairs = list(zip(stacks, got))
            stacks = [jnp.concatenate(p, axis=0) for p in pairs] if early else join(pairs)
    (own,) = join([(stacks[0], got[0], stacks[1], got[1])])
    other = hop(own, 1, count)
    order = sum_order(count)
    pieces += [(own, order[: count // 2]), (other, order[count // 2 :])]
    yield [own]


def start(stages):
    next(stages)
    return stages


def finish(stages):
    for _ in stages:
        pass


def place_kernel(owners, columns, me_ref, *refs):
    stacks, outs, sem = refs[: len(owners)], refs[len(owners) : -1], refs[-1]
    copies = []
    for stack, stack_owners in zip(stacks, owners):
        for index, mask in enumerate(stack_owners):
            owner = jnp.bitwise_xor(me_ref[0], mask)
            for out, lo, hi, to in columns:
                copies.append(
                    pltpu.make_async_copy(
                        stack.at[index, :, lo:hi],
                        outs[out].at[owner, :, to : to + hi - lo],
                        sem.at[len(copies)],
                    )
                )
                copies[-1].start()
    for copy in copies:
        copy.wait()


def place(pieces, columns, widths, me, count):
    stacks = [stack for stack, _ in pieces]
    rows = stacks[0].shape[1]
    outs = pl.pallas_call(
        functools.partial(place_kernel, tuple(tuple(o) for _, o in pieces), columns),
        in_specs=[pl.BlockSpec(memory_space=pltpu.SMEM)]
        + [pl.BlockSpec(memory_space=pl.ANY)] * len(stacks),
        out_specs=[pl.BlockSpec(memory_space=pltpu.VMEM)] * len(widths),
        out_shape=[jax.ShapeDtypeStruct((count, rows, width), BF) for width in widths],
        scratch_shapes=[pltpu.SemaphoreType.DMA((count * len(columns),))],
        cost_estimate=QUICK,
        compiler_params=pltpu.CompilerParams(vmem_limit_bytes=KERNEL_VMEM),
        name="place",
    )(me.reshape(1), *stacks)
    return [out.reshape(count * rows, width) for out, width in zip(outs, widths)]


def sum_order(count):
    farthest, far, middle = hop_plan(count)
    order = []
    for masks, block in ((middle, [0, farthest]), (middle[::-1], [far, far ^ farthest])):
        for mask in masks:
            block = block + [owner ^ mask for owner in block]
        order += block
    return order + [owner ^ 1 for owner in order]


def order_matrix(me, count, rows):
    masks = np.repeat(np.array(sum_order(count), np.int32), rows)
    wanted = jnp.bitwise_xor(me, masks) * rows + np.tile(np.arange(rows, dtype=np.int32), count)
    features = lax.broadcasted_iota(jnp.int32, (count * rows, count * rows), 0)
    return (features == wanted[None, :]).astype(BF)


def pick_kernel(masks, me_ref, stack, kept, sent, sem):
    half = len(masks) // 2
    copies = []
    for index, mask in enumerate(masks):
        owner = jnp.bitwise_xor(me_ref[0], mask)
        out = kept if index < half else sent
        copies.append(
            pltpu.make_async_copy(stack.at[owner], out.at[index % half], sem.at[index])
        )
        copies[-1].start()
    for copy in copies:
        copy.wait()


def pick(array, me, count):
    stack = array.reshape(count, -1, array.shape[-1])
    half = jax.ShapeDtypeStruct((count // 2,) + stack.shape[1:], BF)
    return pl.pallas_call(
        functools.partial(pick_kernel, tuple(sum_order(count))),
        in_specs=[
            pl.BlockSpec(memory_space=pltpu.SMEM),
            pl.BlockSpec(memory_space=pl.ANY),
        ],
        out_specs=[pl.BlockSpec(memory_space=pltpu.VMEM)] * 2,
        out_shape=[half, half],
        scratch_shapes=[pltpu.SemaphoreType.DMA((count,))],
        cost_estimate=QUICK,
        compiler_params=pltpu.CompilerParams(vmem_limit_bytes=16 * 1024 * 1024),
        name="pick",
    )(me.reshape(1), stack)


def add_low(left, right):
    return (left.astype(F32) + right.astype(F32)).astype(BF)


def scatter_stages(parts, count, result, late=(), direct=False, inbox=None, costs=()):
    farthest, far, middle = hop_plan(count)
    blocks = count // 2
    half = blocks // 2
    shape = lambda side: side.reshape(blocks, -1, side.shape[-1])
    kept, sent = [shape(k) for k, _ in parts], [shape(s) for _, s in parts]
    deps = yield
    sent = after(sent, deps)
    arrived = [hop(side, 1, count) for side in sent]
    deps = yield sent
    arrived = after(arrived, deps)
    pairs = list(zip(kept, arrived)) + [(shape(k), shape(got)) for k, got in late]

    costs = list(costs)

    def added(groups, outputs):
        cost = costs.pop(0) if costs else QUICK
        rows = groups[0][0][0].shape[1]
        if all(lo * rows % 16 == 0 and hi * rows % 16 == 0 for o in outputs for _, lo, hi in o):
            return add_ranges(groups, outputs, cost)
        return [
            jnp.concatenate(
                [
                    jnp.concatenate([add_low(a[lo:hi], b[lo:hi]) for a, b in groups[g]], axis=-1)
                    for g, lo, hi in ranges
                ],
                axis=0,
            )
            for ranges in outputs
        ]

    groups, size = [pairs], half
    for masks in zip(middle[::-1], middle):
        size //= 2
        at = [(0, 0), (0, half)] if len(groups) == 1 else [(0, 0), (1, 0)]
        *sends, near, back = added(
            groups,
            [[(group, lo + size, lo + 2 * size)] for group, lo in at]
            + [[(group, lo, lo + size)] for group, lo in at],
        )
        got = [hop(send, mask, count) for send, mask in zip(sends, masks)]
        if inbox is not None:
            inbox[:] = got
        deps = yield sends
        got = after(got, deps)
        groups = [[(near, got[0])], [(back, got[1])]]
    if direct:
        near, back = (a.astype(F32) + b.astype(F32) for ((a, b),) in groups)
        sends = [block.astype(BF) for block in (near[1], back[0], back[1])]
        got = [hop(s, m, count) for s, m in zip(sends, (farthest, far, far ^ farthest))]
        deps = yield sends
        got = after(got, deps)
        total = near[0] + got[0].astype(F32) + got[1].astype(F32) + got[2].astype(F32)
        result.append(total)
        yield [total]
        return
    send, kept = added(groups, [[(1, 0, 2)], [(0, 0, 2)]])
    got = hop(send, far, count)
    deps = yield [send]
    (got,) = after([got], deps)
    send = add_low(kept[1], got[1])
    arrived = hop(send, farthest, count)
    deps = yield [send]
    (arrived,) = after([arrived], deps)
    total = kept[0].astype(F32) + got[0].astype(F32) + arrived.astype(F32)
    result.append(total)
    yield [total]


def sum_stages(array, count, result):
    bits = count.bit_length() - 1
    deps = yield
    for mask in [1 << bit for bit in [bits - 2, bits - 1, 0] + list(range(1, bits - 2))]:
        (array,) = after([array], deps)
        got = hop(array, mask, count)
        deps = yield [array]
        (got,) = after([got], deps)
        array = array + got
    result.append(array)
    yield [array]


def per_device(
    tokens,
    window_pos,
    norm1_gain,
    norm1_bias,
    qkv_weight,
    qkv_bias,
    rel_pos_h,
    rel_pos_w,
    proj_weight,
    proj_bias,
    norm2_gain,
    norm2_bias,
    lin1_weight,
    lin1_bias,
    lin2_weight,
    lin2_bias,
    out_grad,
):
    vectors = (
        norm1_gain,
        norm1_bias,
        qkv_bias,
        proj_bias,
        norm2_gain,
        norm2_bias,
        lin1_bias,
        lin2_bias,
    )
    sizes = [v.shape[0] for v in vectors]
    used = sum(sizes)
    shard_rows = qkv_weight.shape[0]
    count = lax.axis_size("fsdp")
    me = lax.axis_index("fsdp")

    packed = lax.optimization_barrier(jnp.concatenate(vectors))
    packed = jnp.pad(packed, (0, shard_rows * 128 - used)).reshape(shard_rows, 128)
    middle = len(hop_plan(count)[2])
    first_pieces, second_pieces, third_pieces = [], [], []
    first = start(
        gather_stages(
            jnp.concatenate((qkv_weight, proj_weight, packed), axis=1).astype(BF), count, first_pieces, early=True
        )
    )
    second = start(gather_stages(lin1_weight.astype(BF), count, second_pieces))
    third = start(gather_stages(lin2_weight.astype(BF), count, third_pieces))
    onehot, shift = window_constants()
    onehot = jnp.asarray(onehot, BF)
    shift = jnp.asarray(shift)
    order = order_matrix(me, count, shard_rows)
    table = table_lanes(rel_pos_h, rel_pos_w)
    live = jnp.broadcast_to(slot_mask(window_pos), (tokens.shape[0], 128))
    inverse = np.argsort(np.array(sum_order(count)))
    places = jnp.take(jnp.asarray(inverse, jnp.int32), jnp.bitwise_xor(me, np.arange(count)))
    first.send(None)
    sent = first.send(None)
    first.send(None)
    second.send(sent)
    third.send(sent)
    for _ in range(middle - 1):
        sent = first.send(None)
    sent = second.send(sent) + third.send(sent)
    sent = second.send(sent) + third.send(sent)
    first.send(sent + [order, table, live, places])

    (small,) = place(
        first_pieces, ((0, 4 * D, 4 * D + 128, 0),), (128,), me, count
    )
    small = small.reshape(count, shard_rows * 128)[:, :used].astype(F32)
    edges = np.cumsum([0] + sizes)
    gain_one, bias_one, b_qkv, b_proj, gain_two, bias_two, b_up, b_down = (
        small[:, lo:hi].reshape(-1) for lo, hi in zip(edges[:-1], edges[1:])
    )
    flat = lambda pieces: [stack.reshape(-1, stack.shape[-1]) for stack, _ in pieces]
    first_pieces = flat(first_pieces)
    (gated_tokens,) = after([tokens], sent)
    turned_one, qkv = front(
        gated_tokens, live, order, jnp.stack((gain_one, bias_one)), b_qkv.reshape(1, -1), first_pieces
    )
    sent = [turned_one]
    for _ in range(middle - 1):
        sent = second.send(sent) + third.send(sent)
    (qkv,) = after([qkv], sent)
    mixed, probs = attention(qkv, table, onehot, shift)
    sent = third.send([mixed])
    b_up = b_up.reshape(1, FF)
    (mixed,) = after([mixed], sent + [b_up])
    vectors = jnp.stack((b_proj, gain_two, bias_two, b_down))
    residual, normed_two, turned_two, ordered_mixed = project(
        tokens, mixed, order, vectors, first_pieces
    )
    second.send([residual])

    own_down, own_up, own_third, all_small = [], [], [], []
    down_weight = placed_down(third_pieces, me, count)
    output, grad_normed, kept_up, sent_up, grad_b_up, down_parts = mlp(
        me,
        count,
        places,
        normed_two,
        turned_two,
        live,
        out_grad,
        residual,
        vectors,
        b_up,
        flat(second_pieces),
        down_weight,
    )
    late, got_up, got_down = [], [], []
    up = start(scatter_stages([(kept_up, sent_up)], count, own_up, late, inbox=got_up))
    down = start(
        scatter_stages([down_parts], count, own_down, inbox=got_down, costs=(QUICK, LONG))
    )
    sent = up.send(None)
    sent = down.send(sent)
    (grad_normed,) = after([grad_normed], sent)
    grad_residual, grad_mixed, kept_proj, sent_proj, mlp_sums = second_norm_back(
        grad_normed, residual, ordered_mixed, live, out_grad, order, vectors, first_pieces
    )
    late.append((kept_proj, hop(sent_proj, 1, count)))
    sent = down.send([grad_mixed])
    sent = up.send(sent)
    (grad_mixed,) = after([grad_mixed], sent)
    grad_qkv, tables = attention_back(qkv, grad_mixed, probs, table, onehot, shift)
    kept_qkv, sent_qkv = weight_grad(turned_one, grad_qkv)
    third_sum = start(scatter_stages([(kept_qkv, sent_qkv)], count, own_third, direct=True))
    third_sum.send(None)
    sent = [kept_qkv]
    for _ in range(middle - 1):
        sent = up.send(sent)
    (grad_qkv,) = after([grad_qkv], sent)
    tokens_grad, small_sums = first_norm_back(
        grad_qkv,
        first_pieces,
        tokens,
        live,
        gain_one.reshape(1, D),
        order,
        grad_residual,
        mlp_sums,
        grad_b_up,
        tables,
    )
    small_stages = start(sum_stages(small_sums, count, all_small))
    sent = small_stages.send(None)
    for _ in range(middle - 1):
        sent = down.send([small_sums] + sent)
    sent = third_sum.send(sent + got_up)
    sent = up.send(sent)
    (gated_tables,) = after([tables], sent)
    sent = [marker(gated_tables)]
    sent = small_stages.send(sent)
    sent = down.send(sent)
    for _ in range(middle - 1):
        sent = third_sum.send(sent)
    sent = up.send(sent)
    sent = small_stages.send(sent)
    sent = third_sum.send(sent)
    sent = small_stages.send(sent)
    sent = down.send(sent)
    sent = small_stages.send(sent)
    sent = up.send(sent)
    for stages in (down, up, third_sum, small_stages):
        finish(stages)
    own_qkv, own_proj = own_third[0], own_up[0][:, FF:]
    *owned, table_h, table_w = own_small(all_small[0], me, sizes)
    owned = [vector.reshape(-1) for vector in owned]

    return (
        output,
        tokens_grad,
        owned[0],
        owned[1],
        own_qkv,
        owned[2],
        table_h,
        table_w,
        own_proj,
        owned[3],
        owned[4],
        owned[5],
        own_up[0][:, :FF],
        owned[6],
        own_down[0],
        owned[7],
    )


def solution(mesh):
    rows = P("fsdp", None)
    line = P("fsdp")
    return jax.shard_map(
        per_device,
        mesh=mesh,
        in_specs=(
            rows,
            line,
            line,
            line,
            rows,
            line,
            P(),
            P(),
            rows,
            line,
            line,
            line,
            rows,
            line,
            rows,
            line,
            rows,
        ),
        out_specs=(
            rows,
            rows,
            line,
            line,
            rows,
            line,
            P(),
            P(),
            rows,
            line,
            line,
            line,
            rows,
            line,
            rows,
            line,
        ),
        check_vma=False,
    )
```
